32 devices in a mesh: rows: 8 (over z, x), seq: 4 (over y, core).
Axes of the slice: x: 2, y: 2, z: 4, core: 2. Of those that a mesh axis runs over, the one named last changes fastest.
Arguments:
- tokens: bfloat16 [96, 512, 768], P('rows', 'seq'), may hold values from -6 to 6
- seg_lengths: int32 [96, 6], P('rows'), may hold values from 1 to 256, 512 in all within a row
- w_query: bfloat16 [768, 768], replicated, may hold values from -0.25 to 0.25
- w_key: bfloat16 [768, 768], replicated, may hold values from -0.25 to 0.25
- w_value: bfloat16 [768, 768], replicated, may hold values from -0.21875 to 0.21875
- w_output: bfloat16 [768, 768], replicated, may hold values from -0.625 to 0.625
- w_inner: bfloat16 [768, 3072], replicated, may hold values from -0.21875 to 0.21875
- w_outer: bfloat16 [3072, 768], replicated, may hold values from -0.1875 to 0.1875
- gain_attn: bfloat16 [768], replicated, may hold values from 0.099609375 to 1.8984375
- gain_ffn: bfloat16 [768], replicated, may hold values from 0.099609375 to 1.8984375
- bucket_bias_table: bfloat16 [32, 12], replicated, may hold values from -4 to 4
- cotangent: bfloat16 [96, 512, 768], P('rows', 'seq'), may hold values from -6 to 6
Outputs:
- out_tokens: bfloat16 [96, 512, 768], P('rows', 'seq')
- grad_tokens: bfloat16 [96, 512, 768], P('rows', 'seq')
- grad_query: float32 [768, 768], replicated
- grad_key: float32 [768, 768], replicated
- grad_value: float32 [768, 768], replicated
- grad_output: float32 [768, 768], replicated
- grad_inner: float32 [768, 3072], replicated
- grad_outer: float32 [3072, 768], replicated
- grad_gain_attn: float32 [768], replicated
- grad_gain_ffn: float32 [768], replicated
- grad_table: float32 [32, 12], replicated
The draws below stay inside these ranges and needn't reach their ends.
Inputs may be any that keep to these rules, and one draw needn't show every extreme that they name: `seg_lengths`: each row's 6 entries sum to 512; the last is the row's padding; the largest entry of each row is 256.
All inputs are finite; a program needn't handle non-finite values.
Results may differ from the reference program's by a relative error of at most 0.015.
The reference program's roundings to bfloat16 on the way count: a program that leaves them out, or rounds other values in their place, can miss the bound.
Values may be sent and summed in bfloat16 or wider, within the bound.
A program may use at most 384 MiB of HBM per device.

```python
import math
import jax
import jax.numpy as jnp
import numpy as np
from jax import lax

D = 768
HEADS = 12
HEAD_DIM = 64
FF = 3072
BUCKETS = 32
ROW_LEN = 512
ROWS_DEV = 12
SEG_COUNT = 6
LONGEST = 256
ROWS = 96
TOKENS = 49152
N_ROWS = 8


def block_scale(key, dims, pieces, low, largest):
    factor_of, own = 1.0, jax.random.fold_in(key, 6)
    for dim, shards_of in pieces:
        heights = jnp.exp(jax.random.uniform(jax.random.fold_in(own, dim), (shards_of,), jnp.float32, low / len(pieces), largest / len(pieces)))
        factor_of = factor_of * jnp.repeat(heights, dims[dim] // shards_of).reshape([-1 if axis == dim else 1 for axis in range(len(dims))])
    return factor_of


def length_profile(count, total, reach, skew):
    loads = [(1 << 20) // math.isqrt(rank ** skew) + 1 for rank in range(2, count + 1)]
    spare, counts = total - reach - (count - 1), [1] * (count - 1)
    while spare > 0:
        candidates = [i for i in range(count - 1) if counts[i] < reach]
        whole, budget = sum([loads[i] for i in candidates]), spare
        for i in candidates:
            extra = min(reach - counts[i], max(1, budget * loads[i] // whole), spare)
            counts[i] = counts[i] + extra
            spare = spare - extra
    return np.array([reach] + counts)


def ragged_sizes(rng, number_of, total, most, skew):
    if number_of == 2:
        one = jax.random.randint(rng, (), max(1, total - most), min(most, total - 1) + 1)
        return jnp.stack([one, total - one])
    tallies = jnp.asarray(length_profile(number_of, total, most, skew), jnp.int32)
    twos = (number_of - 1) // 2
    donor, sink = tallies[1:1 + 2 * twos:2], tallies[2:2 + 2 * twos:2]
    slack = jnp.minimum(donor - 1, most - sink)
    shifted = jax.random.randint(jax.random.fold_in(rng, 1), (twos,), 0, 1 << 20) % (slack + 1)
    tallies = tallies.at[1:1 + 2 * twos:2].set(donor - shifted).at[2:2 + 2 * twos:2].set(sink + shifted)
    return tallies[jax.random.permutation(jax.random.fold_in(rng, 2), number_of)]


def scatter_about(rng, dims, width, most, shards=(), kind=jnp.bfloat16):
    drawn = jax.random.normal(rng, dims, jnp.float32) * width
    if len(shards) > 0:
        drawn = block_scale(rng, dims, shards, -0.22, 0.18) * drawn
    return jnp.clip(drawn, min=-most, max=most).astype(kind)


def setup_inputs(seed: int = 0) -> dict:
    streams_of = jax.random.split(jax.random.key(seed), 13)
    return {
        "tokens": scatter_about(streams_of[0], (ROWS, ROW_LEN, D), 1.0, 6.0, ((0, 8), (1, 4))),
        "seg_lengths": jax.vmap(lambda own: ragged_sizes(own, SEG_COUNT, ROW_LEN, LONGEST, 2))(jax.random.split(streams_of[1], ROWS)).reshape((ROWS, SEG_COUNT)).astype(jnp.int32),
        "w_query": scatter_about(streams_of[2], (D, D), (0.5 * D ** -0.5), 0.25),
        "w_key": scatter_about(streams_of[3], (D, D), (0.5 * D ** -0.5), 0.25),
        "w_value": scatter_about(streams_of[4], (D, D), D ** -0.5, 0.21875),
        "w_output": scatter_about(streams_of[5], (D, D), (D // 8) ** -0.5, 0.625),
        "w_inner": scatter_about(streams_of[6], (D, FF), D ** -0.5, 0.21875),
        "w_outer": scatter_about(streams_of[7], (FF, D), (FF // 3) ** -0.5, 0.1875),
        "gain_attn": jnp.clip(1.0 + 0.18 * jax.random.normal(streams_of[8], (D,), jnp.float32), 0.099609375, 1.8984375).astype(jnp.bfloat16),
        "gain_ffn": jnp.clip(1.0 + 0.18 * jax.random.normal(streams_of[9], (D,), jnp.float32), 0.099609375, 1.8984375).astype(jnp.bfloat16),
        "bucket_bias_table": scatter_about(streams_of[10], (BUCKETS, HEADS), 1.0, 4.0),
        "cotangent": scatter_about(streams_of[11], (ROWS, ROW_LEN, D), 1.0, 6.0, ((0, 8), (1, 4))),
    }


EPSILON = 1e-06
THRESHOLDS = (12, 16, 23, 32, 46, 64, 91)
NEGATIVE = -1e+30

@jax.custom_vjp
def low(v):
    return lax.optimization_barrier(v.astype(jnp.bfloat16)).astype(jnp.float32)

@jax.custom_vjp
def low_back(v):
    return v

def low_keep(v):
    return (low(v), None)

def low_pass(kept, grad):
    return (grad,)

def back_keep(v):
    return (v, None)

def back_low(kept, grad):
    return (low(grad),)
low.defvjp(low_keep, low_pass)
low_back.defvjp(back_keep, back_low)

def bucket_of(offsets):
    distance = jnp.abs(offsets)
    levels = 8 + sum(((distance >= threshold).astype(jnp.int32) for threshold in THRESHOLDS))
    return jnp.where(offsets > 0, BUCKETS // 2, 0) + jnp.where(distance < 8, distance, levels)

def segment_ids(seg_lengths):
    ends = jnp.cumsum(seg_lengths, axis=1).astype(jnp.int32)
    positions = jnp.arange(ROW_LEN, dtype=jnp.int32)
    return lax.optimization_barrier(jnp.sum((positions[None, :, None] >= ends[:, None, :]).astype(jnp.int32), axis=2))

def rms_norm(values_in, gain_row):
    return values_in * lax.rsqrt(lax.optimization_barrier(jnp.mean(values_in * values_in, axis=-1, keepdims=True)) + EPSILON) * gain_row

def layer_rows(tokens_wide, seg_rows, relative_position_bias, params):
    w_query, w_key, w_value, w_output, w_inner, w_outer, gain_attn, gain_ffn = params
    highest = lax.Precision.HIGHEST
    row_count = tokens_wide.shape[0]
    normed = low(rms_norm(tokens_wide, gain_attn))
    query_rows = low(low_back(jnp.einsum('rtd,de->rte', normed, w_query, precision=highest)))
    key_rows = low(low_back(jnp.einsum('rtd,de->rte', normed, w_key, precision=highest)))
    value_rows = low(low_back(jnp.einsum('rtd,de->rte', normed, w_value, precision=highest)))
    query_heads = query_rows.reshape(row_count, ROW_LEN, HEADS, HEAD_DIM)
    key_heads = key_rows.reshape(row_count, ROW_LEN, HEADS, HEAD_DIM)
    value_heads = value_rows.reshape(row_count, ROW_LEN, HEADS, HEAD_DIM)
    attention_logits = low_back(jnp.einsum('rqhd,rkhd->rhqk', query_heads, key_heads, precision=highest) + relative_position_bias[None])
    allowed = seg_rows[:, None, :, None] == seg_rows[:, None, None, :]
    attention_logits = jnp.where(allowed, attention_logits, NEGATIVE)
    exps = jnp.exp(attention_logits - lax.optimization_barrier(jnp.max(attention_logits, axis=-1, keepdims=True)))
    probs = low(exps / lax.optimization_barrier(jnp.sum(exps, axis=-1, keepdims=True)))
    mixed = jnp.einsum('rhqk,rkhd->rqhd', probs, value_heads, precision=highest).reshape(row_count, ROW_LEN, D)
    mixed = low(low_back(mixed))
    hidden = tokens_wide + low_back(jnp.einsum('rtd,de->rte', mixed, w_output, precision=highest))
    normed_two = low(rms_norm(hidden, gain_ffn))
    inner_pre = low_back(jnp.einsum('rtd,df->rtf', normed_two, w_inner, precision=highest))
    active = low(jax.nn.gelu(inner_pre, approximate=True))
    return hidden + jnp.einsum('rtf,fd->rtd', active, w_outer, precision=highest)

def reference(tokens, seg_lengths, w_query, w_key, w_value, w_output, w_inner, w_outer, gain_attn, gain_ffn, bucket_bias_table, cotangent):
    seg_all = segment_ids(seg_lengths)
    positions = jnp.arange(ROW_LEN, dtype=jnp.int32)
    offsets = positions[None, :] - positions[:, None]
    bucket_indicator = (bucket_of(offsets)[None] == jnp.arange(BUCKETS, dtype=jnp.int32)[:, None, None]).astype(jnp.float32)
    seg_blocks = seg_all.reshape(N_ROWS, ROWS_DEV, ROW_LEN)

    def forward(tokens_wide, bucket_bias_weights, wq_in, wk_in, wv_in, wo_in, wi_in, wf_in, gain_one, gain_two):
        relative_position_bias = jnp.einsum('zfu,zi->ifu', bucket_indicator, bucket_bias_weights, precision=lax.Precision.HIGHEST)
        params = (wq_in, wk_in, wv_in, wo_in, wi_in, wf_in, gain_one, gain_two)
        block_step = jax.checkpoint(lambda row_block, seg_rows: layer_rows(row_block, seg_rows, relative_position_bias, params))

        def scan_step(scan_carry, scan_item):
            return (scan_carry, block_step(scan_item[0], scan_item[1]))
        blocks_in = tokens_wide.reshape(N_ROWS, ROWS_DEV, ROW_LEN, D)
        _, layer_outs = lax.scan(scan_step, jnp.zeros((), jnp.float32), (blocks_in, seg_blocks))
        return layer_outs.reshape(ROWS, ROW_LEN, D)
    result, pullback = jax.vjp(forward, tokens.astype(jnp.float32), bucket_bias_table.astype(jnp.float32), w_query.astype(jnp.float32), w_key.astype(jnp.float32), w_value.astype(jnp.float32), w_output.astype(jnp.float32), w_inner.astype(jnp.float32), w_outer.astype(jnp.float32), gain_attn.astype(jnp.float32), gain_ffn.astype(jnp.float32))
    grads_all = pullback(cotangent.astype(jnp.float32))
    grad_scale = TOKENS ** (-0.5)
    return (result.astype(jnp.bfloat16), grads_all[0].astype(jnp.bfloat16), grads_all[2] * grad_scale, grads_all[3] * grad_scale, grads_all[4] * grad_scale, grads_all[5] * grad_scale, grads_all[6] * grad_scale, grads_all[7] * grad_scale, grads_all[8] * grad_scale, grads_all[9] * grad_scale, grads_all[1] * grad_scale)
```

```python
import math

import jax
import jax.numpy as jnp
from jax import lax
from jax.sharding import PartitionSpec as P

MICRO = 3


EPSILON = 1e-06
THRESHOLDS = (12, 16, 23, 32, 46, 64, 91)
NEGATIVE = -1e30
GELU_SCALE = math.sqrt(2.0 / math.pi)
GELU_CUBIC = 0.044715


def bucket_of(offsets, bucket_count):
    distance = jnp.abs(offsets)
    levels = 8 + sum(((distance >= threshold).astype(jnp.int32) for threshold in THRESHOLDS))
    return jnp.where(offsets > 0, bucket_count // 2, 0) + jnp.where(distance < 8, distance, levels)


def segment_ids(seg_lengths, row_len):
    order = jnp.arange(seg_lengths.shape[1])
    ends = jnp.sum(
        jnp.where(order[None, :, None] <= order[None, None, :], seg_lengths[:, :, None], 0), axis=1
    )
    positions = jnp.arange(row_len, dtype=jnp.int32)
    return jnp.sum((positions[None, :, None] >= ends[:, None, :]).astype(jnp.int32), axis=2)


def gelu_value(values_in):
    return jax.nn.gelu(values_in, approximate=True)


def gelu_slope(values_in):
    tangent = jnp.tanh(GELU_SCALE * (values_in + GELU_CUBIC * values_in * values_in * values_in))
    return 0.5 * (1.0 + tangent) + 0.5 * values_in * (1.0 - tangent * tangent) * GELU_SCALE * (
        1.0 + 3.0 * GELU_CUBIC * values_in * values_in
    )


def apply_rms_scaling(values_in, gain_row):
    inverse = lax.rsqrt(jnp.mean(values_in * values_in, axis=-1, keepdims=True) + EPSILON)
    return (values_in * inverse * gain_row, inverse)


def norm_back(values_in, inverse, gain_row, grad_normed):
    weighted = grad_normed * gain_row
    inner_mean = jnp.mean(weighted * values_in, axis=-1, keepdims=True)
    grad_values = inverse * weighted - values_in * (inverse * inverse * inverse) * inner_mean
    grad_gain = jnp.sum(grad_normed * values_in * inverse, axis=(0, 1))
    return (grad_values, grad_gain)


def split_heads(array_in, head_count):
    return array_in.reshape(
        array_in.shape[0], array_in.shape[1], head_count, array_in.shape[2] // head_count
    )


def join_heads(array_in):
    return array_in.reshape(
        array_in.shape[0], array_in.shape[1], array_in.shape[2] * array_in.shape[3]
    )


def score_block(query_rows, key_rows, relative_position_bias, allowed, head_count):
    raw_scores = jnp.einsum(
        "rqhd,rkhd->rhqk",
        split_heads(query_rows, head_count),
        split_heads(key_rows, head_count),
        preferred_element_type=jnp.float32,
    )
    return jnp.where(allowed, raw_scores + relative_position_bias[None], NEGATIVE)


def project(rows_in, weight_in):
    return jnp.einsum("rtd,de->rte", rows_in, weight_in, preferred_element_type=jnp.float32)


def project_back(rows_in, weight_in):
    return jnp.einsum("rte,de->rtd", rows_in, weight_in, preferred_element_type=jnp.float32)


def outer_sum(left_rows, right_rows):
    return jnp.einsum("rtd,rte->de", left_rows, right_rows, preferred_element_type=jnp.float32)


def per_device(
    tokens,
    seg_lengths,
    w_query,
    w_key,
    w_value,
    w_output,
    w_inner,
    w_outer,
    gain_attn,
    gain_ffn,
    bucket_bias_table,
    cotangent,
):
    rows_dev, piece_len, model_width = tokens.shape
    seq_parts = lax.axis_size("seq")
    row_len = piece_len * seq_parts
    bucket_count, head_count = bucket_bias_table.shape
    batch_rows = rows_dev // MICRO
    gain_one = gain_attn.astype(jnp.float32)
    gain_two = gain_ffn.astype(jnp.float32)
    seg_all = segment_ids(seg_lengths, row_len)
    key_place = jnp.arange(row_len, dtype=jnp.int32)
    query_place = lax.axis_index("seq") * piece_len + jnp.arange(piece_len, dtype=jnp.int32)
    offsets = key_place[None, :] - query_place[:, None]
    bucket_indicator = (
        bucket_of(offsets, bucket_count)[None]
        == jnp.arange(bucket_count, dtype=jnp.int32)[:, None, None]
    ).astype(jnp.bfloat16)
    relative_position_bias = jnp.einsum(
        "zfu,zi->ifu", bucket_indicator, bucket_bias_table, preferred_element_type=jnp.float32
    )
    sum_query = jnp.zeros(w_query.shape, jnp.float32)
    sum_key = jnp.zeros(w_key.shape, jnp.float32)
    sum_value = jnp.zeros(w_value.shape, jnp.float32)
    sum_output = jnp.zeros(w_output.shape, jnp.float32)
    sum_inner = jnp.zeros(w_inner.shape, jnp.float32)
    sum_outer = jnp.zeros(w_outer.shape, jnp.float32)
    sum_gain_one = jnp.zeros((model_width,), jnp.float32)
    sum_gain_two = jnp.zeros((model_width,), jnp.float32)
    bucket_bias_sum = jnp.zeros((head_count, query_place.shape[0], row_len), jnp.float32)
    out_list = []
    grad_in_list = []
    for micro_step in range(MICRO):
        row_start = micro_step * batch_rows
        tokens_part = tokens[row_start : row_start + batch_rows]
        grad_part = cotangent[row_start : row_start + batch_rows]
        seg_rows = seg_all[row_start : row_start + batch_rows]
        tokens_here, grad_out = (tokens_part, grad_part)
        seg_query = lax.dynamic_slice_in_dim(
            seg_rows, lax.axis_index("seq") * piece_len, piece_len, 1
        )
        allowed = seg_query[:, None, :, None] == seg_rows[:, None, None, :]
        tokens_wide = tokens_here.astype(jnp.float32)
        normed_wide, inverse_one = apply_rms_scaling(tokens_wide, gain_one)
        normed = normed_wide.astype(jnp.bfloat16)
        query_rows = project(normed, w_query).astype(jnp.bfloat16)
        key_rows = project(normed, w_key).astype(jnp.bfloat16)
        value_rows = project(normed, w_value).astype(jnp.bfloat16)
        keys_all, values_all = (
            lax.all_gather(key_rows, "seq", axis=1, tiled=True),
            lax.all_gather(value_rows, "seq", axis=1, tiled=True),
        )
        attention_logits = score_block(
            query_rows, keys_all, relative_position_bias, allowed, head_count
        )
        top_score = jnp.max(attention_logits, axis=-1, keepdims=True)
        exps = jnp.exp(attention_logits - top_score)
        exp_total = jnp.sum(exps, axis=-1, keepdims=True)
        probs_low = (exps / exp_total).astype(jnp.bfloat16)
        log_total = top_score + jnp.log(exp_total)
        mixed = join_heads(
            jnp.einsum(
                "rhqk,rkhd->rqhd",
                probs_low,
                split_heads(values_all, head_count),
                preferred_element_type=jnp.float32,
            )
        ).astype(jnp.bfloat16)
        hidden = tokens_wide + project(mixed, w_output)
        normed_two_wide, inverse_two = apply_rms_scaling(hidden, gain_two)
        normed_two = normed_two_wide.astype(jnp.bfloat16)
        inner_pre = project(normed_two, w_inner)
        active = gelu_value(inner_pre).astype(jnp.bfloat16)
        result = (hidden + project(active, w_outer)).astype(jnp.bfloat16)
        sum_outer = sum_outer + outer_sum(active, grad_out)
        grad_active = project_back(grad_out, w_outer)
        grad_pre = (grad_active * gelu_slope(inner_pre)).astype(jnp.bfloat16)
        sum_inner = sum_inner + outer_sum(normed_two, grad_pre)
        grad_hidden_part, gain_part = norm_back(
            hidden, inverse_two, gain_two, project_back(grad_pre, w_inner)
        )
        sum_gain_two = sum_gain_two + gain_part
        grad_hidden = grad_out.astype(jnp.float32) + grad_hidden_part
        grad_branch = grad_hidden.astype(jnp.bfloat16)
        sum_output = sum_output + outer_sum(mixed, grad_branch)
        grad_mixed = project_back(grad_branch, w_output).astype(jnp.bfloat16)
        keys_back, values_back = (keys_all, values_all)
        attention_logits = score_block(
            query_rows, keys_back, relative_position_bias, allowed, head_count
        )
        weights = jnp.exp(attention_logits - log_total)
        probs_back = weights.astype(jnp.bfloat16)
        grad_mixed_heads = split_heads(grad_mixed, head_count)
        grad_values_all = join_heads(
            jnp.einsum(
                "rhqk,rqhd->rkhd", probs_back, grad_mixed_heads, preferred_element_type=jnp.float32
            )
        )
        grad_probs = jnp.einsum(
            "rqhd,rkhd->rhqk",
            grad_mixed_heads,
            split_heads(values_back, head_count),
            preferred_element_type=jnp.float32,
        )
        inner_total = jnp.sum(grad_probs * weights, axis=-1, keepdims=True)
        grad_scores = (weights * (grad_probs - inner_total)).astype(jnp.bfloat16)
        bucket_bias_sum = bucket_bias_sum + jnp.sum(grad_scores.astype(jnp.float32), axis=0)
        grad_query_rows = join_heads(
            jnp.einsum(
                "rhqk,rkhd->rqhd",
                grad_scores,
                split_heads(keys_back, head_count),
                preferred_element_type=jnp.float32,
            )
        ).astype(jnp.bfloat16)
        grad_keys_all = join_heads(
            jnp.einsum(
                "rhqk,rqhd->rkhd",
                grad_scores,
                split_heads(query_rows, head_count),
                preferred_element_type=jnp.float32,
            )
        )
        grad_key_rows, grad_value_rows = (
            lax.psum_scatter(
                grad_keys_all.astype(jnp.bfloat16), "seq", scatter_dimension=1, tiled=True
            ).astype(jnp.float32),
            lax.psum_scatter(
                grad_values_all.astype(jnp.bfloat16), "seq", scatter_dimension=1, tiled=True
            ).astype(jnp.float32),
        )
        grad_key_rows = grad_key_rows.astype(jnp.bfloat16)
        grad_value_rows = grad_value_rows.astype(jnp.bfloat16)
        sum_query = sum_query + outer_sum(normed, grad_query_rows)
        sum_key = sum_key + outer_sum(normed, grad_key_rows)
        sum_value = sum_value + outer_sum(normed, grad_value_rows)
        grad_normed = (
            project_back(grad_query_rows, w_query)
            + project_back(grad_key_rows, w_key)
            + project_back(grad_value_rows, w_value)
        )
        grad_tokens_part, gain_part = norm_back(tokens_wide, inverse_one, gain_one, grad_normed)
        sum_gain_one = sum_gain_one + gain_part
        grad_input = (grad_hidden + grad_tokens_part).astype(jnp.bfloat16)
        out_list.append(result)
        grad_in_list.append(grad_input)
    sum_table = jnp.einsum(
        "eml,aml->ea",
        bucket_indicator.astype(jnp.float32),
        bucket_bias_sum,
        precision=lax.Precision.HIGHEST,
    )
    grad_list = (
        sum_query,
        sum_key,
        sum_value,
        sum_output,
        sum_inner,
        sum_outer,
        sum_gain_one,
        sum_gain_two,
        sum_table,
    )
    flat_grads = jnp.concatenate([grad_piece.reshape(-1) for grad_piece in grad_list])
    devices = lax.axis_size("rows") * lax.axis_size("seq")
    pad_count = -flat_grads.shape[0] % (devices * 128)
    flat_grads = jnp.pad(flat_grads, (0, pad_count))
    share_len = flat_grads.shape[0] // devices
    flat_grads = flat_grads.reshape(share_len, devices).T.reshape(-1, 128)
    grad_scale = float(rows_dev * lax.axis_size("rows") * row_len) ** (-0.5)
    grad_share = (
        lax.psum_scatter(flat_grads, ("rows", "seq"), scatter_dimension=0, tiled=True) * grad_scale
    )
    summed_all = lax.all_gather(
        grad_share.astype(jnp.bfloat16), ("rows", "seq"), axis=0, tiled=True
    ).astype(grad_share.dtype)
    summed_all = summed_all.reshape(devices, share_len).T.reshape(-1)
    results = []
    offset_now = 0
    for grad_piece in grad_list:
        piece_count = grad_piece.size
        results.append(summed_all[offset_now : offset_now + piece_count].reshape(grad_piece.shape))
        offset_now += piece_count
    return (
        jnp.concatenate(out_list, axis=0),
        jnp.concatenate(grad_in_list, axis=0),
        results[0],
        results[1],
        results[2],
        results[3],
        results[4],
        results[5],
        results[6],
        results[7],
        results[8],
    )


def solution(mesh):
    in_specs = (
        P("rows", "seq", None),
        P("rows", None),
        P(),
        P(),
        P(),
        P(),
        P(),
        P(),
        P(),
        P(),
        P(),
        P("rows", "seq", None),
    )
    out_specs = (
        P("rows", "seq", None),
        P("rows", "seq", None),
        P(),
        P(),
        P(),
        P(),
        P(),
        P(),
        P(),
        P(),
        P(),
    )
    return jax.shard_map(
        per_device, mesh=mesh, in_specs=in_specs, out_specs=out_specs, check_vma=False
    )
```

```python
import functools
import math

import jax
import jax.numpy as jnp
from jax import lax
from jax.experimental import pallas as pl
from jax.experimental.pallas import tpu as pltpu
from jax.sharding import PartitionSpec as P

EPSILON = 1e-06
THRESHOLDS = (12, 16, 23, 32, 46, 64, 91)
NEGATIVE = -1e30
GELU_SCALE = math.sqrt(2.0 / math.pi)
GELU_CUBIC = 0.044715
LOG2E = math.log2(math.e)
BLK = 128
QT = 256
HALF = 64
ONES_AT = 8
BF = jnp.bfloat16
F32 = jnp.float32
MESH = pl.DeviceIdType.MESH
CH = 256
LAG = 2


def bucket_of(offsets, bucket_count):
    distance = jnp.abs(offsets)
    levels = 8 + sum(((distance >= threshold).astype(jnp.int32) for threshold in THRESHOLDS))
    return jnp.where(offsets > 0, bucket_count // 2, 0) + jnp.where(distance < 8, distance, levels)


def segment_ids(seg_lengths, row_len):
    order = jnp.arange(seg_lengths.shape[1])
    ends = jnp.sum(
        jnp.where(order[None, :, None] <= order[None, None, :], seg_lengths[:, :, None], 0), axis=1
    )
    positions = jnp.arange(row_len, dtype=jnp.int32)
    return jnp.sum((positions[None, :, None] >= ends[:, None, :]).astype(jnp.int32), axis=2)


def gelu_slope(values_in):
    tangent = jnp.tanh(GELU_SCALE * (values_in + GELU_CUBIC * values_in * values_in * values_in))
    return 0.5 * (1.0 + tangent) + 0.5 * values_in * (1.0 - tangent * tangent) * GELU_SCALE * (
        1.0 + 3.0 * GELU_CUBIC * values_in * values_in
    )


def apply_rms_scaling(values_in, gain_row):
    inverse = lax.rsqrt(jnp.mean(values_in * values_in, axis=-1, keepdims=True) + EPSILON)
    return (values_in * inverse * gain_row, inverse)


def norm_back(values_in, inverse, gain_row, grad_normed):
    weighted = grad_normed * gain_row
    inner_mean = jnp.mean(weighted * values_in, axis=-1, keepdims=True)
    grad_values = inverse * weighted - values_in * (inverse * inverse * inverse) * inner_mean
    grad_gain = jnp.sum(grad_normed * values_in * inverse, axis=0)
    return (grad_values, grad_gain)


def dot(a, b, ca, cb):
    return lax.dot_general(a, b, (((ca,), (cb,)), ((), ())), preferred_element_type=F32)


def halves(value, own, other, head):
    lane = lax.broadcasted_iota(jnp.int32, value.shape, 1)
    mine = (lane < HALF) if head == 0 else (lane >= HALF)
    return jnp.where(mine, value, other)


def stack_q(q_pair, features, head):
    scaled = q_pair[head * HALF : (head + 1) * HALF].astype(F32) * LOG2E
    high = scaled.astype(BF)
    low = (scaled - high.astype(F32)).astype(BF)
    zero = jnp.zeros_like(high)
    if head == 0:
        return jnp.concatenate([high, zero, low, features], axis=0)
    return jnp.concatenate([zero, high, features, low], axis=0)


def bias_tile(bias_ref, head, key_block, query_tile, blocks):
    at = key_block - query_tile * (QT // BLK) + blocks - 1
    return jnp.concatenate([bias_ref[head, at - i] for i in range(QT // BLK)], axis=1)


def attend_kernel(q_ref, k_ref, v_ref, fq_ref, fk_ref, bias_ref, mix_ref, stat_ref):
    row_len = k_ref.shape[0]
    blocks = row_len // BLK
    keys, features_k = k_ref[...], fk_ref[0]
    v_flat = v_ref[...].T
    for head in range(2):
        q_all = stack_q(q_ref[...], fq_ref[0], head)
        k_all = jnp.concatenate([keys, halves(keys, None, features_k, head)], axis=1)
        v_head = jnp.concatenate(
            [v_flat[head * HALF : (head + 1) * HALF], jnp.ones((16, row_len), BF)], axis=0
        )
        for tile in range(row_len // QT):
            cut = slice(tile * QT, (tile + 1) * QT)
            raw = dot(k_all, q_all[:, cut], 1, 0)
            scores = jnp.concatenate(
                [
                    raw[b * BLK : (b + 1) * BLK] + bias_tile(bias_ref, head, b, tile, blocks)
                    for b in range(blocks)
                ],
                axis=0,
            )
            top = jnp.max(scores, axis=0, keepdims=True)
            probs = jnp.exp2(scores - top).astype(BF)
            summed = dot(v_head, probs, 1, 0)
            total = summed[HALF : HALF + 1]
            mix_ref[head * HALF : (head + 1) * HALF, cut] = (
                summed[:HALF] * (1.0 / total)
            ).astype(BF)
            stat_ref[0, 0, head : head + 1, cut] = top + jnp.log2(total)


def three(row):
    one = row.astype(BF)
    rest = row - one.astype(F32)
    two = rest.astype(BF)
    return one, two, (rest - two.astype(F32)).astype(BF)


def feature_rows(base, row):
    parts = three(row)
    at = lax.broadcasted_iota(jnp.int32, base.shape, 0)
    out = base.astype(F32)
    for i, part in enumerate(parts):
        out = jnp.where(at == ONES_AT + i, part.astype(F32), out)
    return out.astype(BF)


def attend_back_kernel(
    q_ref, k_ref, v_ref, do_ref, mix_ref, stat_ref, fq_ref, fk_ref, bias_ref,
    dq_ref, dk_ref, dv_ref, acc_ref, dk_sum, dv_sum,
):
    row_len = k_ref.shape[0]
    blocks = row_len // BLK
    keys, vals, features_k = k_ref[...], v_ref[...], fk_ref[0]
    k_flat = keys.T
    q_rows, do_rows = q_ref[...].T, do_ref[...].T
    zero_rows = jnp.zeros((row_len, BLK), BF)

    @pl.when(pl.program_id(1) == 0)
    def _():
        acc_ref[...] = jnp.zeros_like(acc_ref)

    for head in range(2):
        span = slice(head * HALF, (head + 1) * HALF)
        do_head = do_ref[span]
        delta = jnp.sum(do_head.astype(F32) * mix_ref[span].astype(F32), axis=0, keepdims=True)
        zeros = jnp.zeros((HALF, row_len), BF)
        q_all = stack_q(q_ref[...], feature_rows(fq_ref[0], -stat_ref[0, 0, head : head + 1]), head)
        k_all = jnp.concatenate([keys, halves(keys, None, features_k, head)], axis=1)
        v_all = halves(vals, None, features_k, head)
        back = feature_rows(zeros, -delta)
        do_all = jnp.concatenate([do_head, back] if head == 0 else [back, do_head], axis=0)
        q_own = halves(q_rows, None, zero_rows, head)
        do_own = halves(do_rows, None, zero_rows, head)
        for tile in range(row_len // QT):
            cut = slice(tile * QT, (tile + 1) * QT)
            raw = dot(k_all, q_all[:, cut], 1, 0)
            grad_probs = dot(v_all, do_all[:, cut], 1, 0)
            probs_list, grads_list = [], []
            sums = {}
            for b in range(blocks):
                part = slice(b * BLK, (b + 1) * BLK)
                probs = jnp.exp2(raw[part] + bias_tile(bias_ref, head, b, tile, blocks))
                grads = probs * grad_probs[part]
                probs_list.append(probs.astype(BF))
                grads_list.append(grads.astype(BF))
                for i in range(QT // BLK):
                    at = b - tile * (QT // BLK) - i + blocks - 1
                    piece = grads[:, i * BLK : (i + 1) * BLK]
                    sums[at] = sums[at] + piece if at in sums else piece
            for at, piece in sums.items():
                acc_ref[head, at] += piece
            probs_low = jnp.concatenate(probs_list, axis=0)
            grads_low = jnp.concatenate(grads_list, axis=0)
            dv_new = dot(probs_low, do_own[cut], 1, 0)
            dk_new = dot(grads_low, q_own[cut], 1, 0)
            if head == 0 and tile == 0:
                dv_sum[...] = dv_new
                dk_sum[...] = dk_new
            else:
                dv_sum[...] += dv_new
                dk_sum[...] += dk_new
            dq_ref[span, cut] = dot(k_flat[span], grads_low, 1, 0).astype(BF)
    dk_ref[...] = dk_sum[...].astype(BF)
    dv_ref[...] = dv_sum[...].astype(BF)


def specs(row_len):
    flat = pl.BlockSpec((BLK, row_len), lambda g, r: (g, r))
    rows = pl.BlockSpec((row_len, BLK), lambda g, r: (r, g))
    stat = pl.BlockSpec((1, 1, 2, row_len), lambda g, r: (r, g, 0, 0))
    fq = pl.BlockSpec((1, HALF, row_len), lambda g, r: (r, 0, 0))
    fk = pl.BlockSpec((1, row_len, BLK), lambda g, r: (r, 0, 0))
    blocks = 2 * (row_len // BLK) - 1
    bias = pl.BlockSpec((2, blocks, BLK, BLK), lambda g, r: (g, 0, 0, 0))
    return flat, rows, stat, fq, fk, bias


def attend(q_flat, k_rows, v_rows, fq, fk, bias, row_len):
    width, count = q_flat.shape
    flat, rows, stat, fqs, fks, biass = specs(row_len)
    pairs, row_count = width // BLK, count // row_len
    return pl.pallas_call(
        attend_kernel,
        grid=(pairs, row_count),
        in_specs=[flat, rows, rows, fqs, fks, biass],
        out_specs=[flat, stat],
        out_shape=[
            jax.ShapeDtypeStruct((width, count), BF),
            jax.ShapeDtypeStruct((row_count, pairs, 2, row_len), F32),
        ],
        compiler_params=pltpu.CompilerParams(vmem_limit_bytes=48 << 20),
        cost_estimate=pl.CostEstimate(
            flops=4 * 4 * width * count * row_len,
            bytes_accessed=8 * width * count,
            transcendentals=0,
        ),
    )(q_flat, k_rows, v_rows, fq, fk, bias)


def attend_back(q_flat, k_rows, v_rows, do_flat, mix_flat, stat_in, fq, fk, bias, row_len):
    width, count = q_flat.shape
    flat, rows, stat, fqs, fks, biass = specs(row_len)
    pairs, row_count = width // BLK, count // row_len
    return pl.pallas_call(
        attend_back_kernel,
        grid=(pairs, row_count),
        in_specs=[flat, rows, rows, flat, flat, stat, fqs, fks, biass],
        out_specs=[flat, rows, rows, biass],
        out_shape=[
            jax.ShapeDtypeStruct((width, count), BF),
            jax.ShapeDtypeStruct((count, width), BF),
            jax.ShapeDtypeStruct((count, width), BF),
            jax.ShapeDtypeStruct(bias.shape, F32),
        ],
        scratch_shapes=[pltpu.VMEM((row_len, BLK), F32)] * 2,
        compiler_params=pltpu.CompilerParams(vmem_limit_bytes=48 << 20),
        cost_estimate=pl.CostEstimate(
            flops=10 * 4 * width * count * row_len,
            bytes_accessed=16 * width * count,
            transcendentals=0,
        ),
    )(q_flat, k_rows, v_rows, do_flat, mix_flat, stat_in, fq, fk, bias)


class Place:
    def __init__(self):
        self.r, self.s = lax.axis_index("rows"), lax.axis_index("seq")
        self.x, self.z = lax.rem(self.r, 2), self.r // 2
        self.core, self.y = lax.rem(self.s, 2), self.s // 2

    def at(self, x=None, y=None, core=None, z=None):
        x = self.x if x is None else x
        y = self.y if y is None else y
        core = self.core if core is None else core
        z = self.z if z is None else z
        return (z * 2 + x, y * 2 + core)


def reduce_kernel(chunks, depth, scale, in_ref, out_ref, got, own, got_one, got_two, got_z, share,
                  load_sem, keep_sem, send, recv, send_z, recv_z):
    me = Place()
    w = in_ref.shape[1] // 2
    half, quarter, piece = CH // 2, CH // 4, CH // (4 * depth)
    barrier = pltpu.get_barrier_semaphore()
    others = [me.at(core=1 - me.core), me.at(x=1 - me.x), me.at(y=1 - me.y)]
    others += [me.at(z=lax.rem(me.z + k, depth)) for k in range(1, depth)]
    for place in others:
        pl.semaphore_signal(barrier, inc=1, device_id=place, device_id_type=MESH)
    pl.semaphore_wait(barrier, len(others))

    def copy(src, dst, stage, c, place):
        return pltpu.make_async_remote_copy(
            src_ref=src, dst_ref=dst, send_sem=send.at[stage, c], recv_sem=recv.at[stage, c],
            device_id=place, device_id_type=MESH)

    def lanes(core):
        return pl.ds(pl.multiple_of(core * w, 128), w)

    def rows(base, size):
        return pl.ds(pl.multiple_of(base, 16), size)

    def order(c):
        odd = lax.rem(c, 2)
        one = jnp.where(odd == 0, me.x, me.y)
        two = jnp.where(odd == 0, me.y, me.x)
        x_first = (me.r + (1 - odd) * (1 - 2 * me.x), me.s + odd * (2 - 4 * me.y))
        y_first = (me.r + odd * (1 - 2 * me.x), me.s + (1 - odd) * (2 - 4 * me.y))
        return one, two, x_first, y_first

    def load(c):
        return pltpu.make_async_copy(in_ref.at[rows(c * CH, CH), lanes(me.core)], own.at[c], load_sem.at[c])

    def step_core(c):
        return copy(in_ref.at[rows(c * CH, CH), lanes(1 - me.core)], got.at[c], 0, c, me.at(core=1 - me.core))

    def step_one(c):
        one, _, place, _ = order(c)
        return copy(own.at[c, rows((1 - one) * half, half)], got_one.at[c], 1, c, place)

    def step_two(c):
        one, two, _, place = order(c)
        return copy(own.at[c, rows(one * half + (1 - two) * quarter, quarter)], got_two.at[c], 2, c, place)

    def base(c):
        one, two, _, _ = order(c)
        return one * half + two * quarter

    def step_z(c, k):
        to = lax.rem(me.z + k, depth)
        return pltpu.make_async_remote_copy(
            src_ref=own.at[c, rows(base(c) + to * piece, piece)], dst_ref=got_z.at[c, depth - 1 - k],
            send_sem=send_z.at[0, c, k - 1], recv_sem=recv_z.at[0, c, depth - 1 - k],
            device_id=me.at(z=to), device_id_type=MESH)

    def keep(c):
        return pltpu.make_async_copy(
            share.at[c], out_ref.at[rows(c * CH + base(c) + me.z * piece, piece), lanes(me.core)], keep_sem.at[c])

    def give_z(c, k):
        to = lax.rem(me.z + k, depth)
        return pltpu.make_async_remote_copy(
            src_ref=share.at[c],
            dst_ref=out_ref.at[rows(c * CH + base(c) + me.z * piece, piece), lanes(me.core)],
            send_sem=send_z.at[1, c, k - 1], recv_sem=recv_z.at[1, c, depth - 1 - k],
            device_id=me.at(z=to), device_id_type=MESH)

    def give_two(c):
        one, two, _, place = order(c)
        part = out_ref.at[rows(c * CH + one * half + two * quarter, quarter), lanes(me.core)]
        return copy(part, part, 3, c, place)

    def give_one(c):
        one, _, place, _ = order(c)
        part = out_ref.at[rows(c * CH + one * half, half), lanes(me.core)]
        return copy(part, part, 4, c, place)

    def give_core(c):
        part = out_ref.at[rows(c * CH, CH), lanes(me.core)]
        return copy(part, part, 5, c, me.at(core=1 - me.core))

    def add(c, start, size, from_ref):
        part = rows(start, size)
        own[c, part] = (own[c, part].astype(F32) + from_ref[c].astype(F32)).astype(BF)

    def run(stage, c):
        if stage == 0:
            step_core(c).start()
        if stage == 1:
            step_core(c).wait_recv()
            load(c).wait()
            add(c, 0, CH, got)
            step_one(c).start()
        if stage == 2:
            step_one(c).wait_recv()
            one, _, _, _ = order(c)
            add(c, one * half, half, got_one)
            step_two(c).start()
        if stage == 3:
            step_two(c).wait_recv()
            add(c, base(c), quarter, got_two)
            for k in range(1, depth):
                step_z(c, k).start()
        if stage == 4:
            for k in range(1, depth):
                step_z(c, k).wait_recv()
            total = own[c, rows(base(c) + me.z * piece, piece)].astype(F32)
            for k in range(depth - 1):
                total = total + got_z[c, k].astype(F32)
            share[c] = (total * scale).astype(BF)
            keep(c).start()
            for k in range(1, depth):
                give_z(c, k).start()
        if stage == 5:
            keep(c).wait()
            for k in range(1, depth):
                give_z(c, k).wait_recv()
            give_two(c).start()
        if stage == 6:
            give_two(c).wait_recv()
            give_one(c).start()
        if stage == 7:
            give_one(c).wait_recv()
            give_core(c).start()
        if stage == 8:
            give_core(c).wait_recv()
            for d in (step_core(c), step_one(c), step_two(c), give_two(c), give_one(c), give_core(c)):
                d.wait_send()
            for k in range(1, depth):
                step_z(c, k).wait_send()
                give_z(c, k).wait_send()

    def first(c, _):
        load(c).start()
        return 0

    lax.fori_loop(0, chunks, first, 0)

    def tick(t, _):
        for stage in range(8, -1, -1):
            p = t - stage * LAG

            @pl.when((p >= 0) & (p < chunks // 2))
            def _():
                run(stage, 2 * p)
                run(stage, 2 * p + 1)
        return 0

    lax.fori_loop(0, chunks // 2 + 8 * LAG, tick, 0)


def reduce_ring(flat, scale, depth):
    chunks, w = flat.shape[0] // CH, flat.shape[1] // 2
    piece = CH // (4 * depth)
    dma = pltpu.SemaphoreType.DMA
    return pl.pallas_call(
        functools.partial(reduce_kernel, chunks, depth, scale),
        out_shape=jax.ShapeDtypeStruct(flat.shape, BF),
        in_specs=[pl.BlockSpec(memory_space=pl.ANY)],
        out_specs=pl.BlockSpec(memory_space=pl.ANY),
        scratch_shapes=[
            pltpu.VMEM((chunks, CH, w), BF),
            pltpu.VMEM((chunks, CH, w), BF),
            pltpu.VMEM((chunks, CH // 2, w), BF),
            pltpu.VMEM((chunks, CH // 4, w), BF),
            pltpu.VMEM((chunks, depth - 1, piece, w), BF),
            pltpu.VMEM((chunks, piece, w), BF),
            dma((chunks,)), dma((chunks,)),
            dma((6, chunks)), dma((6, chunks)),
            dma((2, chunks, depth - 1)), dma((2, chunks, depth - 1)),
        ],
        compiler_params=pltpu.CompilerParams(
            collective_id=0, has_side_effects=True, vmem_limit_bytes=56 << 20),
    )(flat)


def reduce_plain(flat, scale):
    share = lax.psum_scatter(flat, ("rows", "seq"), scatter_dimension=0, tiled=True)
    share = (share.astype(F32) * scale).astype(BF)
    return lax.all_gather(share, ("rows", "seq"), axis=0, tiled=True)


def reduce_all(flat, scale):
    depth = lax.axis_size("rows") // 2
    if lax.axis_size("seq") == 4 and CH % (4 * depth * 16) == 0:
        return reduce_ring(flat, scale, depth)
    return reduce_plain(flat, scale)


def per_device(
    tokens, seg_lengths, w_query, w_key, w_value, w_output, w_inner, w_outer,
    gain_attn, gain_ffn, bucket_bias_table, cotangent,
):
    rows_dev, piece_len, width = tokens.shape
    seq_parts = lax.axis_size("seq")
    row_len = piece_len * seq_parts
    bucket_count, head_count = bucket_bias_table.shape
    mine = rows_dev // seq_parts
    count = mine * row_len
    seg_count = seg_lengths.shape[1]
    gain_one = gain_attn.astype(F32)
    gain_two = gain_ffn.astype(F32)

    def to_rows(array_in):
        out = lax.all_to_all(array_in, "seq", split_axis=0, concat_axis=1, tiled=True)
        return out.reshape(count, width)

    def from_rows(array_in):
        return lax.all_to_all(
            array_in.reshape(mine, row_len, width), "seq", split_axis=1, concat_axis=0, tiled=True
        )

    lengths = lax.dynamic_slice_in_dim(seg_lengths, lax.axis_index("seq") * mine, mine, 0)
    seg = segment_ids(lengths, row_len)
    slots = jnp.arange(HALF, dtype=jnp.int32)
    fq = (seg[:, None, :] == slots[None, :, None]).astype(BF)
    fk_half = jnp.where(
        slots < seg_count,
        jnp.where(seg[:, :, None] != slots, NEGATIVE, 0.0),
        jnp.where((slots >= ONES_AT) & (slots < ONES_AT + 3), 1.0, 0.0),
    ).astype(BF)
    fk = jnp.concatenate([fk_half, fk_half], axis=2)
    blocks = row_len // BLK
    offsets = (
        (jnp.arange(2 * blocks - 1, dtype=jnp.int32) - (blocks - 1))[:, None, None] * BLK
        + jnp.arange(BLK, dtype=jnp.int32)[None, :, None]
        - jnp.arange(BLK, dtype=jnp.int32)[None, None, :]
    )
    buckets = bucket_of(offsets, bucket_count)
    indicator = (
        buckets[None] == jnp.arange(bucket_count, dtype=jnp.int32)[:, None, None, None]
    ).astype(BF)
    bias = (
        jnp.einsum("zbfu,zi->ibfu", indicator, bucket_bias_table, preferred_element_type=F32)
        * LOG2E
    )

    tok = to_rows(tokens)
    grad_out = to_rows(cotangent)
    wide = tok.astype(F32)
    normed_wide, inverse_one = apply_rms_scaling(wide, gain_one)
    normed = normed_wide.astype(BF)
    q_flat = dot(w_query, normed, 0, 1).astype(BF)
    k_rows = dot(normed, w_key, 1, 0).astype(BF)
    v_rows = dot(normed, w_value, 1, 0).astype(BF)
    mix_flat, stat = attend(q_flat, k_rows, v_rows, fq, fk, bias, row_len)
    hidden = wide + dot(mix_flat, w_output, 0, 0)
    normed_two_wide, inverse_two = apply_rms_scaling(hidden, gain_two)
    normed_two = normed_two_wide.astype(BF)
    inner_pre = dot(normed_two, w_inner, 1, 0)
    active = jax.nn.gelu(inner_pre, approximate=True).astype(BF)
    result = (hidden + dot(active, w_outer, 1, 0)).astype(BF)
    grad_pre = (dot(grad_out, w_outer, 1, 1) * gelu_slope(inner_pre)).astype(BF)
    sum_outer = dot(active, grad_out, 0, 0)
    sum_inner = dot(grad_pre, normed_two, 0, 0)
    grad_hidden_part, sum_gain_two = norm_back(
        hidden, inverse_two, gain_two, dot(grad_pre, w_inner, 1, 1)
    )
    grad_hidden = grad_out.astype(F32) + grad_hidden_part
    grad_branch = grad_hidden.astype(BF)
    sum_output = dot(mix_flat, grad_branch, 1, 0)
    do_flat = dot(w_output, grad_branch, 1, 1).astype(BF)
    dq_flat, dk_rows, dv_rows, table_blocks = attend_back(
        q_flat, k_rows, v_rows, do_flat, mix_flat, stat, fq, fk, bias, row_len
    )
    sum_query = dot(normed, dq_flat, 0, 1)
    sum_key = dot(normed, dk_rows, 0, 0)
    sum_value = dot(normed, dv_rows, 0, 0)
    grad_normed = (
        dot(dq_flat, w_query, 0, 1) + dot(dk_rows, w_key, 1, 1) + dot(dv_rows, w_value, 1, 1)
    )
    grad_tokens_part, sum_gain_one = norm_back(wide, inverse_one, gain_one, grad_normed)
    grad_input = (grad_hidden + grad_tokens_part).astype(BF)
    sum_table = jnp.einsum(
        "zbfu,ibfu->zi", indicator.astype(F32), table_blocks, precision=lax.Precision.HIGHEST
    )

    scale = float(rows_dev * lax.axis_size("rows") * row_len) ** (-0.5)
    small = jnp.concatenate([sum_gain_one, sum_gain_two, sum_table.reshape(-1)])
    small = jnp.pad(small, (0, -small.size % (2 * CH * width))).reshape(-1, width)
    parts = (sum_outer, sum_inner, sum_output, sum_query, sum_key, sum_value, small)
    total = reduce_all(jnp.concatenate([g.astype(BF) for g in parts]), scale).astype(F32)
    out, at = [], 0
    for g in parts:
        out.append(total[at : at + g.shape[0]])
        at += g.shape[0]
    rest = out[6].reshape(-1)
    return (
        from_rows(result),
        from_rows(grad_input),
        out[3],
        out[4],
        out[5],
        out[2],
        out[1].T,
        out[0],
        rest[:width],
        rest[width : 2 * width],
        rest[2 * width : 2 * width + sum_table.size].reshape(sum_table.shape),
    )


def solution(mesh):
    tok = P("rows", "seq", None)
    in_specs = (tok, P("rows", None)) + (P(),) * 9 + (tok,)
    out_specs = (tok, tok) + (P(),) * 9
    return jax.shard_map(
        per_device, mesh=mesh, in_specs=in_specs, out_specs=out_specs, check_vma=False
    )
```

```python
import functools
import math

import jax
import jax.numpy as jnp
from jax import lax
from jax.experimental import pallas as pl
from jax.experimental.pallas import tpu as pltpu
from jax.sharding import PartitionSpec as P

EPSILON = 1e-06
THRESHOLDS = (12, 16, 23, 32, 46, 64, 91)
NEGATIVE = -1e30
BUCKETS = 32
GELU_SCALE = math.sqrt(2.0 / math.pi)
GELU_CUBIC = 0.044715
LOG2E = math.log2(math.e)
BLK = 128
QT = 256
HALF = 64
ONES_AT = 8
BF = jnp.bfloat16
F32 = jnp.float32
TOK = 512
TILE_TOK = 256
MESH = pl.DeviceIdType.MESH
CH_ROWS, CH_COLS = 768, 256
SUM_STEPS = ((1,), (2,), (3,), (4,))
GIVE_STEPS = ((5,), (6,), (7,), (8,), (9,))
GIVE_LAG = 3
EARLY = 6
SWAPS = 12
SEQ = 4
SEND_SLOTS = 8
BOTH_STEPS = ((1,), (2,), (3,), (4, 5), (6,), (7,), (8,), (9,))
REST_LAG = 2


def bucket_of(offsets, bucket_count):
    distance = jnp.abs(offsets)
    levels = 8 + sum(((distance >= threshold).astype(jnp.int32) for threshold in THRESHOLDS))
    return jnp.where(offsets > 0, bucket_count // 2, 0) + jnp.where(distance < 8, distance, levels)


def segment_ids(seg_lengths, row_len):
    order = jnp.arange(seg_lengths.shape[1])
    ends = jnp.sum(
        jnp.where(order[None, :, None] <= order[None, None, :], seg_lengths[:, :, None], 0), axis=1
    )
    positions = jnp.arange(row_len, dtype=jnp.int32)
    return jnp.sum((positions[None, :, None] >= ends[:, None, :]).astype(jnp.int32), axis=2)


def gelu_both(x):
    square = x * x
    tangent = jnp.tanh(x * (GELU_SCALE + GELU_SCALE * GELU_CUBIC * square))
    upper = 0.5 * tangent + 0.5
    slope = upper + (0.5 * x) * (1.0 - tangent * tangent) * (
        GELU_SCALE + 3.0 * GELU_SCALE * GELU_CUBIC * square
    )
    return x * upper, slope


def apply_rms_scaling(values_in, gain_row):
    inverse = lax.rsqrt(jnp.mean(values_in * values_in, axis=-1, keepdims=True) + EPSILON)
    return (values_in * inverse * gain_row, inverse)


def norm_back(values_in, inverse, gain_row, grad_normed):
    weighted = grad_normed * gain_row
    inner_mean = jnp.mean(weighted * values_in, axis=-1, keepdims=True)
    grad_values = inverse * weighted - values_in * (inverse * inverse * inverse) * inner_mean
    grad_gain = jnp.sum(grad_normed * values_in * inverse, axis=0)
    return (grad_values, grad_gain)


def dot(a, b, ca, cb):
    return lax.dot_general(a, b, (((ca,), (cb,)), ((), ())), preferred_element_type=F32)


def halves(value, own, other, head):
    lane = lax.broadcasted_iota(jnp.int32, value.shape, 1)
    mine = (lane < HALF) if head == 0 else (lane >= HALF)
    return jnp.where(mine, value, other)


def stack_q(q_pair, features, head):
    scaled = q_pair[head * HALF : (head + 1) * HALF].astype(F32) * LOG2E
    high = scaled.astype(BF)
    low = (scaled - high.astype(F32)).astype(BF)
    zero = jnp.zeros_like(high)
    if head == 0:
        return jnp.concatenate([high, zero, low, features], axis=0)
    return jnp.concatenate([zero, high, features, low], axis=0)


def bias_tile(bias_ref, head, key_block, query_tile, blocks):
    at = key_block - query_tile * (QT // BLK) + blocks - 1
    return jnp.concatenate([bias_ref[head, at - i] for i in range(QT // BLK)], axis=1)


def attend_kernel(q_ref, k_ref, v_ref, fq_ref, fk_ref, bias_ref, *refs):
    if len(refs) > 2:
        away, mix_ref, stat_ref, near, *sems = refs
        swap = Exchange(away, near, *sems, True)
        now = pl.program_id(0) * pl.num_programs(1) + pl.program_id(1)

        @pl.when(now == 0)
        def _():
            swap.meet()
            swap.start(0)

        @pl.when(now == pl.num_programs(0) * pl.num_programs(1) - 1)
        def _():
            swap.wait(0)
    else:
        mix_ref, stat_ref = refs
    row_len = k_ref.shape[0]
    blocks = row_len // BLK
    keys, features_k = k_ref[...], fk_ref[0]
    v_flat = v_ref[...].T
    for head in range(2):
        q_all = stack_q(q_ref[...], fq_ref[0], head)
        k_all = jnp.concatenate([keys, halves(keys, None, features_k, head)], axis=1)
        v_head = jnp.concatenate(
            [v_flat[head * HALF : (head + 1) * HALF], jnp.ones((16, row_len), BF)], axis=0
        )
        for tile in range(row_len // QT):
            cut = slice(tile * QT, (tile + 1) * QT)
            raw = dot(k_all, q_all[:, cut], 1, 0)
            scores = jnp.concatenate(
                [
                    raw[b * BLK : (b + 1) * BLK] + bias_tile(bias_ref, head, b, tile, blocks)
                    for b in range(blocks)
                ],
                axis=0,
            )
            top = jnp.max(scores, axis=0, keepdims=True)
            probs = jnp.exp2(scores - top).astype(BF)
            summed = dot(v_head, probs, 1, 0)
            total = summed[HALF : HALF + 1]
            mix_ref[head * HALF : (head + 1) * HALF, cut] = (
                summed[:HALF] * (1.0 / total)
            ).astype(BF)
            stat_ref[0, 0, head : head + 1, cut] = top + jnp.log2(total)


def three(row):
    one = row.astype(BF)
    rest = row - one.astype(F32)
    two = rest.astype(BF)
    return one, two, (rest - two.astype(F32)).astype(BF)


def feature_rows(base, row):
    parts = three(row)
    at = lax.broadcasted_iota(jnp.int32, base.shape, 0)
    out = base.astype(F32)
    for i, part in enumerate(parts):
        out = jnp.where(at == ONES_AT + i, part.astype(F32), out)
    return out.astype(BF)


def bucket_sums(acc_ref, head, blocks):
    row = lax.broadcasted_iota(jnp.int32, (BLK, BLK), 0)
    lane = lax.broadcasted_iota(jnp.int32, (BLK, BLK), 1)
    far = 2 * [jnp.zeros((1, BLK), F32)]
    sums = BUCKETS * [jnp.zeros((1, BLK), F32)]
    for at in range(2 * blocks - 1):
        value = acc_ref[head, at]
        low, high = (at - blocks + 1) * BLK - BLK + 1, (at - blocks + 1) * BLK + BLK - 1
        if low >= THRESHOLDS[-1] or high <= -THRESHOLDS[-1]:
            side = 1 if low > 0 else 0
            far[side] = far[side] + jnp.sum(value, axis=0, keepdims=True)
            continue
        bucket = bucket_of((at - blocks + 1) * BLK + row - lane, BUCKETS)
        for b in range(BUCKETS):
            if (b < BUCKETS // 2 and low > 0) or (b >= BUCKETS // 2 and high <= 0):
                continue
            picked = jnp.sum(jnp.where(bucket == b, value, 0.0), axis=0, keepdims=True)
            sums[b] = sums[b] + picked
    sums[BUCKETS // 2 - 1] = sums[BUCKETS // 2 - 1] + far[0]
    sums[BUCKETS - 1] = sums[BUCKETS - 1] + far[1]
    return jnp.concatenate(sums, axis=0)


def attend_back_kernel(
    depth, q_ref, k_ref, v_ref, do_ref, mix_ref, stat_ref, fq_ref, fk_ref, bias_ref, *refs
):
    if depth:
        share, done, dq_ref, dk_ref, dv_ref, table_ref, gi_ref, go_ref, out_ref = refs[:9]
        acc_ref, dk_sum, dv_sum, *sems = refs[9:15]
        swap = Exchange(done, out_ref, *sems, False, SWAPS)
        giving = Summing(
            depth, share, give_refs=refs[15:], targets=(gi_ref, go_ref), turned=True,
            given=(share.shape[0] // 2 - gi_ref.shape[1] // CH_COLS, share.shape[0] // 2),
        )
        now = pl.program_id(0) * pl.num_programs(1) + pl.program_id(1)

        @pl.when(now == 0)
        def _():
            giving.meet()

        @pl.when(now < SWAPS)
        def _():
            swap.start(now)

        giving.tick(now + giving.given[0] + GIVE_LAG, GIVE_STEPS, GIVE_LAG)
    else:
        dq_ref, dk_ref, dv_ref, table_ref, acc_ref, dk_sum, dv_sum = refs
    row_len = k_ref.shape[0]
    blocks = row_len // BLK
    keys, vals, features_k = k_ref[...], v_ref[...], fk_ref[0]
    k_flat = keys.T
    q_rows, do_rows = q_ref[...].T, do_ref[...].T
    zero_rows = jnp.zeros((row_len, BLK), BF)

    @pl.when(pl.program_id(1) == 0)
    def _():
        acc_ref[...] = jnp.zeros_like(acc_ref)

    for head in range(2):
        span = slice(head * HALF, (head + 1) * HALF)
        do_head = do_ref[span]
        delta = jnp.sum(do_head.astype(F32) * mix_ref[span].astype(F32), axis=0, keepdims=True)
        zeros = jnp.zeros((HALF, row_len), BF)
        q_all = stack_q(q_ref[...], feature_rows(fq_ref[0], -stat_ref[0, 0, head : head + 1]), head)
        k_all = jnp.concatenate([keys, halves(keys, None, features_k, head)], axis=1)
        v_all = halves(vals, None, features_k, head)
        back = feature_rows(zeros, -delta)
        do_all = jnp.concatenate([do_head, back] if head == 0 else [back, do_head], axis=0)
        q_own = halves(q_rows, None, zero_rows, head)
        do_own = halves(do_rows, None, zero_rows, head)
        for tile in range(row_len // QT):
            cut = slice(tile * QT, (tile + 1) * QT)
            raw = dot(k_all, q_all[:, cut], 1, 0)
            grad_probs = dot(v_all, do_all[:, cut], 1, 0)
            probs_list, grads_list = [], []
            sums = {}
            for b in range(blocks):
                part = slice(b * BLK, (b + 1) * BLK)
                probs = jnp.exp2(raw[part] + bias_tile(bias_ref, head, b, tile, blocks))
                grads = probs * grad_probs[part]
                probs_list.append(probs.astype(BF))
                grads_list.append(grads.astype(BF))
                for i in range(QT // BLK):
                    at = b - tile * (QT // BLK) - i + blocks - 1
                    piece = grads[:, i * BLK : (i + 1) * BLK]
                    sums[at] = sums[at] + piece if at in sums else piece
            for at, piece in sums.items():
                acc_ref[head, at] += piece
            probs_low = jnp.concatenate(probs_list, axis=0)
            grads_low = jnp.concatenate(grads_list, axis=0)
            dv_new = dot(probs_low, do_own[cut], 1, 0)
            dk_new = dot(grads_low, q_own[cut], 1, 0)
            if head == 0 and tile == 0:
                dv_sum[...] = dv_new
                dk_sum[...] = dk_new
            else:
                dv_sum[...] += dv_new
                dk_sum[...] += dk_new
            dq_ref[span, cut] = dot(k_flat[span], grads_low, 1, 0).astype(BF)
    dk_ref[...] = dk_sum[...].astype(BF)
    dv_ref[...] = dv_sum[...].astype(BF)

    @pl.when(pl.program_id(1) == pl.num_programs(1) - 1)
    def _():
        for head in range(2):
            table_ref[head] = bucket_sums(acc_ref, head, blocks)

    if depth:
        steps = pl.num_programs(0) * pl.num_programs(1)

        @pl.when(now == steps - 1)
        def _():
            giving.drain(steps + giving.given[0] + GIVE_LAG, GIVE_STEPS, GIVE_LAG)
            giving.finish()
            swap.finish()


def specs(row_len):
    flat = pl.BlockSpec((BLK, row_len), lambda g, r: (g, r))
    rows = pl.BlockSpec((row_len, BLK), lambda g, r: (r, g))
    stat = pl.BlockSpec((1, 1, 2, row_len), lambda g, r: (r, g, 0, 0))
    fq = pl.BlockSpec((1, HALF, row_len), lambda g, r: (r, 0, 0))
    fk = pl.BlockSpec((1, row_len, BLK), lambda g, r: (r, 0, 0))
    blocks = 2 * (row_len // BLK) - 1
    bias = pl.BlockSpec((2, blocks, BLK, BLK), lambda g, r: (g, 0, 0, 0))
    return flat, rows, stat, fq, fk, bias


def attend(q_flat, k_rows, v_rows, fq, fk, bias, row_len, away=None):
    width, count = q_flat.shape
    flat, rows, stat, fqs, fks, biass = specs(row_len)
    pairs, row_count = width // BLK, count // row_len
    anywhere = pl.BlockSpec(memory_space=pl.ANY)
    extra, near, scratch, params = (), [], [], {}
    if away is not None:
        extra, near = (away,), [jax.ShapeDtypeStruct((row_count, row_len, width), BF)]
        scratch, params = Exchange.scratch(), dict(collective_id=5, has_side_effects=True)
    return pl.pallas_call(
        attend_kernel,
        grid=(pairs, row_count),
        in_specs=[flat, rows, rows, fqs, fks, biass] + [anywhere] * len(extra),
        out_specs=[flat, stat] + [anywhere] * len(near),
        out_shape=[
            jax.ShapeDtypeStruct((width, count), BF),
            jax.ShapeDtypeStruct((row_count, pairs, 2, row_len), F32),
        ] + near,
        scratch_shapes=scratch,
        compiler_params=pltpu.CompilerParams(vmem_limit_bytes=48 << 20, **params),
        cost_estimate=pl.CostEstimate(
            flops=4 * 4 * width * count * row_len,
            bytes_accessed=8 * width * count,
            transcendentals=0,
        ),
    )(q_flat, k_rows, v_rows, fq, fk, bias, *extra)


def attend_back(q_flat, k_rows, v_rows, do_flat, mix_flat, stat_in, fq, fk, bias, row_len, gives):
    width, count = q_flat.shape
    flat, rows, stat, fqs, fks, biass = specs(row_len)
    pairs, row_count = width // BLK, count // row_len
    anywhere = pl.BlockSpec(memory_space=pl.ANY)
    depth, extra, extra_in, extra_out, scratch, params = 0, (), [], [], [], {}
    if gives is not None:
        share, depth, early, done = gives
        shapes = [(width, share.shape[0] // 2 * CH_COLS - early), (share.shape[0] // 2 * CH_COLS - early, width)]
        done = done.reshape(row_count, row_len, width)
        extra, extra_in = (share, done), [pl.BlockSpec(share.shape, lambda g, r: (0, 0, 0)), anywhere]
        extra_out = [jax.ShapeDtypeStruct(shape, BF) for shape in shapes]
        extra_out += [jax.ShapeDtypeStruct((row_count * SEQ, row_len // SEQ, width), BF)]
        scratch = Exchange.scratch(SWAPS) + Summing.give_scratch(share.shape[0], depth, True)
        params = dict(collective_id=3, has_side_effects=True)
    return pl.pallas_call(
        functools.partial(attend_back_kernel, depth),
        grid=(pairs, row_count),
        in_specs=[flat, rows, rows, flat, flat, stat, fqs, fks, biass] + extra_in,
        out_specs=[flat, rows, rows, pl.BlockSpec((2, BUCKETS, BLK), lambda g, r: (g, 0, 0))]
        + [anywhere] * len(extra_out),
        out_shape=[
            jax.ShapeDtypeStruct((width, count), BF),
            jax.ShapeDtypeStruct((count, width), BF),
            jax.ShapeDtypeStruct((count, width), BF),
            jax.ShapeDtypeStruct((2 * pairs, BUCKETS, BLK), F32),
        ] + extra_out,
        scratch_shapes=[pltpu.VMEM((2,) + bias.shape[1:], F32)]
        + [pltpu.VMEM((row_len, BLK), F32)] * 2
        + scratch,
        compiler_params=pltpu.CompilerParams(vmem_limit_bytes=48 << 20, **params),
        cost_estimate=pl.CostEstimate(
            flops=10 * 4 * width * count * row_len,
            bytes_accessed=16 * width * count,
            transcendentals=0,
        ),
    )(q_flat, k_rows, v_rows, do_flat, mix_flat, stat_in, fq, fk, bias, *extra)


class Place:
    def __init__(self):
        self.r, self.s = lax.axis_index("rows"), lax.axis_index("seq")
        self.x, self.z = lax.rem(self.r, 2), self.r // 2
        self.core, self.y = lax.rem(self.s, 2), self.s // 2

    def at(self, x=None, y=None, core=None, z=None):
        x = self.x if x is None else x
        y = self.y if y is None else y
        core = self.core if core is None else core
        z = self.z if z is None else z
        return (z * 2 + x, y * 2 + core)


def spans(base, size, step=16):
    return pl.ds(pl.multiple_of(base, step), size)


class Exchange:
    def __init__(self, src, dst, send, recv, keep, to_rows, parts=1):
        self.src, self.dst, self.send, self.recv, self.keep, self.to_rows = src, dst, send, recv, keep, to_rows
        pieces, rows = (src, dst) if to_rows else (dst, src)
        self.mine, self.piece, self.parts = rows.shape[0], pieces.shape[1], parts
        self.r, self.s = lax.axis_index("rows"), lax.axis_index("seq")

    @staticmethod
    def scratch(parts=1):
        dma = pltpu.SemaphoreType.DMA
        return [dma((parts, SEQ - 1)), dma((parts, SEQ - 1)), dma((parts,))]

    def meet(self):
        barrier = pltpu.get_barrier_semaphore()
        for k in range(1, SEQ):
            place = (self.r, lax.rem(self.s + k, SEQ))
            pl.semaphore_signal(barrier, inc=1, device_id=place, device_id_type=MESH)
        pl.semaphore_wait(barrier, SEQ - 1)

    def ends(self, part, peer):
        if self.parts <= self.mine:
            size, long = self.mine // self.parts, self.piece
            row, at = part * size, 0
        else:
            cuts = self.parts // self.mine
            size, long = 1, self.piece // cuts
            row, at = part // cuts, lax.rem(part, cuts) * long
        if self.to_rows:
            return (self.src.at[pl.ds(peer * self.mine + row, size), spans(at, long)],
                    self.dst.at[pl.ds(row, size), spans(self.s * self.piece + at, long)])
        return (self.src.at[pl.ds(row, size), spans(peer * self.piece + at, long)],
                self.dst.at[pl.ds(self.s * self.mine + row, size), spans(at, long)])

    def copies(self, part):
        out = []
        for k in range(1, SEQ):
            peer = lax.rem(self.s + k, SEQ)
            src, dst = self.ends(part, peer)
            out.append(pltpu.make_async_remote_copy(
                src_ref=src, dst_ref=dst, send_sem=self.send.at[part, k - 1],
                recv_sem=self.recv.at[part, SEQ - 1 - k], device_id=(self.r, peer), device_id_type=MESH))
        src, dst = self.ends(part, self.s)
        return out, pltpu.make_async_copy(src, dst, self.keep.at[part])

    def start(self, part):
        away, here = self.copies(part)
        for d in away:
            d.start()
        here.start()

    def wait(self, part):
        away, here = self.copies(part)
        for d in away:
            d.wait()
        here.wait()

    def finish(self):
        def one(part, _):
            self.wait(part)
            return 0

        lax.fori_loop(0, self.parts, one, 0)


class Summing:
    def __init__(self, depth, share, sum_refs=None, give_refs=None, scale=1.0, targets=None, turned=False, mixed=True, given=None):
        if sum_refs is not None:
            (self.snd, self.got, self.own, self.got_one, self.got_two, self.got_z,
             self.send_sum, self.recv_sum, self.send_sum_z, self.recv_sum_z) = sum_refs
        if give_refs is not None:
            (self.gath, self.flip, self.sems,
             self.send_give, self.recv_give, self.send_give_z, self.recv_give_z) = give_refs
        self.summed = (0, share.shape[0] // 2)
        self.given = self.summed if given is None else given
        self.share, self.chunks, self.targets, self.turned = share, share.shape[0], targets, turned
        self.depth, self.scale, self.mixed = depth, scale, mixed
        self.me = Place()
        self.w = CH_COLS // 2
        self.half, self.quarter = CH_ROWS // 2, CH_ROWS // 4
        self.piece = CH_ROWS // (4 * depth)

    @staticmethod
    def sum_scratch(chunks, depth):
        w, piece = CH_COLS // 2, CH_ROWS // (4 * depth)
        dma = pltpu.SemaphoreType.DMA
        return [
            pltpu.VMEM((SEND_SLOTS, CH_ROWS, w), BF),
            pltpu.VMEM((chunks, CH_ROWS, w), BF),
            pltpu.VMEM((chunks, CH_ROWS, w), BF),
            pltpu.VMEM((chunks, CH_ROWS // 2, w), BF),
            pltpu.VMEM((chunks, CH_ROWS // 4, w), BF),
            pltpu.VMEM((chunks, depth - 1, piece, w), BF),
            dma((3, chunks)), dma((3, chunks)),
            dma((chunks, depth - 1)), dma((chunks, depth - 1)),
        ]

    @staticmethod
    def give_scratch(chunks, depth, turned):
        dma = pltpu.SemaphoreType.DMA
        return [
            pltpu.VMEM((chunks, 2, CH_ROWS, CH_COLS // 2), BF),
            pltpu.VMEM((2, CH_COLS, CH_ROWS) if turned else (1, 16, 128), BF),
            dma((2, chunks)),
            dma((3, chunks)), dma((3, chunks)),
            dma((chunks, depth - 1)), dma((chunks, depth - 1)),
        ]

    @staticmethod
    def share_shape(chunks, depth):
        return (chunks, CH_ROWS // (4 * depth), CH_COLS // 2)

    def meet(self):
        me = self.me
        barrier = pltpu.get_barrier_semaphore()
        others = [me.at(x=1 - me.x)] + [(me.r, lax.rem(me.s + k, SEQ)) for k in range(1, SEQ)]
        others += [me.at(z=lax.rem(me.z + k, self.depth)) for k in range(1, self.depth)]
        for place in others:
            pl.semaphore_signal(barrier, inc=1, device_id=place, device_id_type=MESH)
        pl.semaphore_wait(barrier, len(others))

    def copy(self, src, dst, stage, c, place):
        if stage < 3:
            send, recv = self.send_sum.at[stage, c], self.recv_sum.at[stage, c]
        else:
            send, recv = self.send_give.at[stage - 3, c], self.recv_give.at[stage - 3, c]
        return pltpu.make_async_remote_copy(
            src_ref=src, dst_ref=dst, send_sem=send, recv_sem=recv, device_id=place, device_id_type=MESH)

    def part(self, c, start, size):
        return self.gath.at[c, self.me.core, spans(start, size)]

    def order(self, c):
        me, odd = self.me, lax.rem(c, 2) if self.mixed else 0
        one = me.x + odd * (me.y - me.x)
        two = me.y + odd * (me.x - me.y)
        x_there, y_there = 1 - 2 * me.x, 2 - 4 * me.y
        first = (me.r + (1 - odd) * x_there, me.s + odd * y_there)
        second = (me.r + odd * x_there, me.s + (1 - odd) * y_there)
        return one, two, first, second

    def put(self, c, value):
        left, right = value[:, : self.w].astype(BF), value[:, self.w :].astype(BF)
        first = self.me.core == 0
        self.own[c] = jnp.where(first, left, right)
        self.snd[lax.rem(c, SEND_SLOTS)] = jnp.where(first, right, left)
        self.step_core(c).start()

    def step_core(self, c):
        return self.copy(self.snd.at[lax.rem(c, SEND_SLOTS)], self.got.at[c], 0, c, self.me.at(core=1 - self.me.core))

    def step_one(self, c):
        one, _, place, _ = self.order(c)
        return self.copy(self.own.at[c, spans((1 - one) * self.half, self.half)], self.got_one.at[c], 1, c, place)

    def step_two(self, c):
        one, two, _, place = self.order(c)
        part = spans(one * self.half + (1 - two) * self.quarter, self.quarter)
        return self.copy(self.own.at[c, part], self.got_two.at[c], 2, c, place)

    def base(self, c):
        one, two, _, _ = self.order(c)
        return one * self.half + two * self.quarter

    def step_z(self, c, k):
        to = lax.rem(self.me.z + k, self.depth)
        return pltpu.make_async_remote_copy(
            src_ref=self.own.at[c, spans(self.base(c) + to * self.piece, self.piece)],
            dst_ref=self.got_z.at[c, self.depth - 1 - k],
            send_sem=self.send_sum_z.at[c, k - 1], recv_sem=self.recv_sum_z.at[c, self.depth - 1 - k],
            device_id=self.me.at(z=to), device_id_type=MESH)

    def mine(self, c):
        return self.part(c, self.base(c) + self.me.z * self.piece, self.piece)

    def give_z(self, c, k):
        return pltpu.make_async_remote_copy(
            src_ref=self.mine(c), dst_ref=self.mine(c),
            send_sem=self.send_give_z.at[c, k - 1], recv_sem=self.recv_give_z.at[c, self.depth - 1 - k],
            device_id=self.me.at(z=lax.rem(self.me.z + k, self.depth)), device_id_type=MESH)

    def give_two(self, c):
        part = self.part(c, self.base(c), self.quarter)
        return self.copy(part, part, 3, c, self.order(c)[3])

    def give_one(self, c):
        one, _, place, _ = self.order(c)
        part = self.part(c, one * self.half, self.half)
        return self.copy(part, part, 4, c, place)

    def give_core(self, c):
        part = self.part(c, 0, CH_ROWS)
        return self.copy(part, part, 5, c, self.me.at(core=1 - self.me.core))

    def leave(self, c, kind):
        if len(self.targets) == 1:
            array, at = self.targets[0], c * CH_COLS
        else:
            array, at = self.targets[kind], (c // 2 - self.given[0]) * CH_COLS
        if self.turned and kind == 1:
            flip = self.flip.at[lax.rem(c // 2, 2)]
            return [pltpu.make_async_copy(flip, array.at[spans(at, CH_COLS, CH_COLS)], self.sems.at[0, c])]
        return [
            pltpu.make_async_copy(
                self.gath.at[c, i], array.at[:, spans(at + i * self.w, self.w, 128)], self.sems.at[i, c])
            for i in range(2)
        ]

    def add(self, c, start, size, from_ref):
        part = spans(start, size)
        self.own[c, part] = (self.own[c, part].astype(F32) + from_ref[c].astype(F32)).astype(BF)

    def run(self, stage, c, kind):
        depth = self.depth
        if stage == 1:
            self.step_core(c).wait()
            self.add(c, 0, CH_ROWS, self.got)
            self.step_one(c).start()
        if stage == 2:
            self.step_one(c).wait_recv()
            self.add(c, self.order(c)[0] * self.half, self.half, self.got_one)
            self.step_two(c).start()
        if stage == 3:
            self.step_two(c).wait_recv()
            self.add(c, self.base(c), self.quarter, self.got_two)
            for k in range(1, depth):
                self.step_z(c, k).start()
        if stage == 4:
            for k in range(1, depth):
                self.step_z(c, k).wait_recv()
            total = self.own[c, spans(self.base(c) + self.me.z * self.piece, self.piece)].astype(F32)
            for k in range(depth - 1):
                total = total + self.got_z[c, k].astype(F32)
            self.share[c] = (total * self.scale).astype(BF)
            for d in (self.step_one(c), self.step_two(c)):
                d.wait_send()
            for k in range(1, depth):
                self.step_z(c, k).wait_send()
        if stage == 5:
            self.gath[c, self.me.core, spans(self.base(c) + self.me.z * self.piece, self.piece)] = self.share[c]
            for k in range(1, depth):
                self.give_z(c, k).start()
        if stage == 6:
            for k in range(1, depth):
                self.give_z(c, k).wait_recv()
            self.give_two(c).start()
        if stage == 7:
            self.give_two(c).wait_recv()
            self.give_one(c).start()
        if stage == 8:
            self.give_one(c).wait_recv()
            self.give_core(c).start()
        if stage == 9:
            self.give_core(c).wait_recv()
            if self.turned and kind == 1:

                @pl.when(c // 2 >= self.given[0] + 2)
                def _():
                    for d in self.leave(c - 4, kind):
                        d.wait()

                slot = lax.rem(c // 2, 2)
                for i in range(2):
                    self.flip[slot, i * self.w : (i + 1) * self.w] = self.gath[c, i].T
            for d in self.leave(c, kind):
                d.start()
            for d in (self.give_two, self.give_one, self.give_core):
                d(c).wait_send()
            for k in range(1, depth):
                self.give_z(c, k).wait_send()

    def tick(self, t, steps, lag):
        for at in range(len(steps), 0, -1):
            p = t - at * lag
            for stage in steps[at - 1]:
                low, high = self.summed if stage < 5 else self.given

                @pl.when((p >= low) & (p < high))
                def _():
                    for kind in range(2):
                        self.run(stage, 2 * p + kind, kind)

    def drain(self, start, steps, lag):
        def one(t, _):
            self.tick(t, steps, lag)
            return 0

        last = 0
        for at in range(len(steps), 0, -1):
            for stage in steps[at - 1]:
                last = max(last, (self.summed if stage < 5 else self.given)[1] + at * lag)
        lax.fori_loop(start, last, one, 0)

    def finish(self):
        def one(c, kind):
            for d in self.leave(c, kind):
                d.wait()

        def pair(p, _):
            one(2 * p, 0)
            if not self.turned:
                one(2 * p + 1, 1)
            return 0

        low, high = self.given
        lax.fori_loop(low, high, pair, 0)
        if self.turned:
            for p in range(max(low, high - 2), high):
                one(2 * p + 1, 1)


def before_kernel(fused, tok, gain, wq, wk, wv, normed_ref, flat_ref, q_ref, k_ref, v_ref, *refs):
    if fused:
        tok_ref, rows, *sems = refs
        swap = Exchange(tok, rows, *sems, True, rows.shape[0])
        m = pl.program_id(0)

        @pl.when(m == 0)
        def _():
            swap.meet()
            for part in range(rows.shape[0]):
                swap.start(part)

        swap.wait(m)
        own = rows[m]
        tok_ref[...] = own
        wide = own.astype(F32)
    else:
        wide = tok[...].astype(F32)
    normed = apply_rms_scaling(wide, gain[...])[0].astype(BF)
    normed_ref[...] = normed
    flat_ref[...] = normed.T
    q_ref[...] = dot(normed, wq[...], 1, 0).astype(BF).T
    k_ref[...] = dot(normed, wk[...], 1, 0).astype(BF)
    v_ref[...] = dot(normed, wv[...], 1, 0).astype(BF)


def tall(width):
    return pl.BlockSpec((TOK, width), lambda m: (m, 0))


def broad(width):
    return pl.BlockSpec((width, TOK), lambda m: (0, m))


def whole(array):
    return pl.BlockSpec(array.shape, lambda m: (0,) * array.ndim)


def plain_call(kernel, count, ins, in_specs, outs, out_specs, flops, scratch=(), collective_id=None):
    params = {} if collective_id is None else dict(collective_id=collective_id, has_side_effects=True)
    return pl.pallas_call(
        kernel,
        grid=(count // TOK,),
        in_specs=in_specs,
        out_specs=out_specs,
        out_shape=[jax.ShapeDtypeStruct(shape, kind) for shape, kind in outs],
        scratch_shapes=list(scratch),
        compiler_params=pltpu.CompilerParams(vmem_limit_bytes=48 << 20, **params),
        cost_estimate=pl.CostEstimate(flops=flops, bytes_accessed=16 << 20, transcendentals=0),
    )(*ins)


def before(tok, gain, wq, wk, wv, mine, fused):
    width = tok.shape[-1]
    count = tok.size // width
    t, f = tall(width), broad(width)
    spec, more, scratch = t, [], []
    if fused:
        spec = pl.BlockSpec(memory_space=pl.ANY)
        more = [((count, width), BF)]
        scratch = [pltpu.VMEM((mine, count // mine, width), BF)] + Exchange.scratch(mine)
    return plain_call(
        functools.partial(before_kernel, fused), count, (tok, gain, wq, wk, wv),
        [spec] + [whole(a) for a in (gain, wq, wk, wv)],
        [((count, width), BF), ((width, count), BF), ((width, count), BF)] + [((count, width), BF)] * 2 + more,
        [t, f, f, t, t] + [t] * len(more), 6 * count * width * width, scratch, 4 if fused else None,
    )


def between_kernel(tok, mix, wo, gain, dy, hidden_ref, nt_ref, nt_flat_ref, dy_flat_ref):
    hidden = tok[...].astype(F32) + dot(mix[...].T, wo[...], 1, 0)
    hidden_ref[...] = hidden
    normed = apply_rms_scaling(hidden, gain[...])[0].astype(BF)
    nt_ref[...] = normed
    nt_flat_ref[...] = normed.T
    dy_flat_ref[...] = dy[...].T


def between(tok, mix_flat, wo, gain, dy):
    count, width = tok.shape
    t, f = tall(width), broad(width)
    return plain_call(
        between_kernel, count, (tok, mix_flat, wo, gain, dy), [t, f, whole(wo), whole(gain), t],
        [((count, width), F32), ((count, width), BF), ((width, count), BF), ((width, count), BF)],
        [t, t, f, f], 2 * count * width * width,
    )


def after_kernel(tok, gain, gh, dq, dk, dv, wq, wk, wv, grad_ref, gain_ref):
    wide = tok[...].astype(F32)
    _, inverse = apply_rms_scaling(wide, gain[...])
    grad_normed = (
        dot(dq[...].T, wq[...], 1, 1) + dot(dk[...], wk[...], 1, 1) + dot(dv[...], wv[...], 1, 1)
    )
    part, grad_gain = norm_back(wide, inverse, gain[...], grad_normed)
    grad_ref[...] = (gh[...] + part).astype(BF)

    @pl.when(pl.program_id(0) == 0)
    def _():
        gain_ref[...] = jnp.zeros_like(gain_ref)

    gain_ref[...] += grad_gain[None]


def after(tok, gain, gh, dq, dk, dv, wq, wk, wv):
    count, width = tok.shape
    t, f = tall(width), broad(width)
    return plain_call(
        after_kernel, count, (tok, gain, gh, dq, dk, dv, wq, wk, wv),
        [t, whole(gain), t, f, t, t, whole(wq), whole(wk), whole(wv)],
        [((count, width), BF), ((1, width), F32)], [t, whole(gain)], 6 * count * width * width,
    )


def ffn_kernel(depth, scale, nt, nt_flat, dy, dy_flat, gain, wi_hbm, wo_hbm, hidden_hbm,
               res_hbm, gh_hbm, gb_hbm, gain_ref, share, gi_ref, go_ref,
               out_acc, gnt_acc, wi_buf, wo_buf, act, gp, hid, res_buf, gb_buf, w_sem, h_sem, *refs):
    count, width = nt.shape
    tile = 2 * CH_COLS
    tiles = wi_hbm.shape[1] // tile
    parts = count // TOK
    given = gi_ref.shape[1] // CH_COLS
    summing = Summing(
        depth, share, refs[:10], refs[10:], scale, targets=(gi_ref, go_ref), turned=True, given=(0, given)
    )

    def weights(j):
        cut, slot = spans(j * tile, tile, tile), lax.rem(j, 2)
        return (
            pltpu.make_async_copy(wi_hbm.at[:, cut], wi_buf.at[slot], w_sem.at[0, slot]),
            pltpu.make_async_copy(wo_hbm.at[cut], wo_buf.at[slot], w_sem.at[1, slot]),
        )

    def hidden(m):
        return pltpu.make_async_copy(hidden_hbm.at[pl.ds(m * TOK, TOK)], hid, h_sem.at[0])

    for w in weights(0):
        w.start()
    hidden(0).start()
    out_acc[...] = jnp.zeros_like(out_acc)
    gnt_acc[...] = jnp.zeros_like(gnt_acc)
    summing.meet()

    def step(j, _):
        for w in weights(j):
            w.wait()

        @pl.when(j + 1 < tiles)
        def _():
            for w in weights(j + 1):
                w.start()

        slot = lax.rem(j, 2)
        wi, wo = wi_buf.at[slot], wo_buf.at[slot]
        for m in range(count // TILE_TOK):
            part = slice(m * TILE_TOK, (m + 1) * TILE_TOK)
            pre = dot(nt[part], wi[...], 1, 0)
            grad_active = dot(dy[part], wo[...], 1, 1)
            value, slope = gelu_both(pre)
            act[part] = value.astype(BF)
            gp[part] = (grad_active * slope).astype(BF)
        for h in range(2):
            cut = slice(h * CH_COLS, (h + 1) * CH_COLS)
            summing.put(4 * j + 2 * h, dot(nt_flat[...], gp[:, cut], 1, 0))
            summing.put(4 * j + 2 * h + 1, dot(dy_flat[...], act[:, cut], 1, 0))
            if h == 0:
                summing.tick(2 * j, BOTH_STEPS, 1)
        for m in range(count // TILE_TOK):
            part = slice(m * TILE_TOK, (m + 1) * TILE_TOK)
            out_acc[part] += dot(act[part], wo[...], 1, 0)
            gnt_acc[part] += dot(gp[part], wi[...], 1, 1)
        summing.tick(2 * j + 1, BOTH_STEPS, 1)
        return 0

    lax.fori_loop(0, tiles, step, 0)

    def outputs(m):
        rows = pl.ds(m * TOK, TOK)
        return (
            pltpu.make_async_copy(res_buf.at[m % 2], res_hbm.at[rows], h_sem.at[1 + m % 2]),
            pltpu.make_async_copy(gb_buf.at[m % 2], gb_hbm.at[rows], h_sem.at[3 + m % 2]),
            pltpu.make_async_copy(gnt_acc.at[rows], gh_hbm.at[rows], h_sem.at[5 + m % 2]),
        )

    total_gain = jnp.zeros((1, width), F32)
    gain_row = gain[...]
    for m in range(parts):
        summing.tick(2 * tiles + m, BOTH_STEPS, 1)
        rows = slice(m * TOK, (m + 1) * TOK)
        hidden(m).wait()
        if m >= 2:
            for d in outputs(m - 2):
                d.wait()
        value = hid[...]
        res_buf[m % 2] = (value + out_acc[rows]).astype(BF)
        _, inverse = apply_rms_scaling(value, gain_row)
        part, grad_gain = norm_back(value, inverse, gain_row, gnt_acc[rows])
        total_gain = total_gain + grad_gain[None]
        grad_hidden = dy[rows].astype(F32) + part
        gnt_acc[rows] = grad_hidden
        gb_buf[m % 2] = grad_hidden.astype(BF)
        if m + 1 < parts:
            hidden(m + 1).start()
        for d in outputs(m):
            d.start()
    gain_ref[...] = total_gain
    summing.drain(2 * tiles + parts, BOTH_STEPS, 1)
    summing.finish()
    for m in range(max(0, parts - 2), parts):
        for d in outputs(m):
            d.wait()


def ffn_summed(nt, nt_flat, dy, dy_flat, gain, w_inner, w_outer, hidden, scale, depth):
    count, width = nt.shape
    ff = w_inner.shape[1]
    chunks = 2 * ff // CH_COLS
    tile = 2 * CH_COLS
    vm = pl.BlockSpec(memory_space=pltpu.VMEM)
    anywhere = pl.BlockSpec(memory_space=pl.ANY)
    return pl.pallas_call(
        functools.partial(ffn_kernel, depth, scale),
        in_specs=[vm] * 5 + [anywhere] * 3,
        out_specs=[anywhere] * 3 + [vm] * 2 + [anywhere] * 2,
        out_shape=[
            jax.ShapeDtypeStruct((count, width), BF),
            jax.ShapeDtypeStruct((count, width), F32),
            jax.ShapeDtypeStruct((count, width), BF),
            jax.ShapeDtypeStruct((1, width), F32),
            jax.ShapeDtypeStruct(Summing.share_shape(chunks, depth), BF),
            jax.ShapeDtypeStruct((width, EARLY * CH_COLS), BF),
            jax.ShapeDtypeStruct((EARLY * CH_COLS, width), BF),
        ],
        scratch_shapes=[
            pltpu.VMEM((count, width), F32),
            pltpu.VMEM((count, width), F32),
            pltpu.VMEM((2, width, tile), BF),
            pltpu.VMEM((2, tile, width), BF),
            pltpu.VMEM((count, tile), BF),
            pltpu.VMEM((count, tile), BF),
            pltpu.VMEM((TOK, width), F32),
            pltpu.VMEM((2, TOK, width), BF),
            pltpu.VMEM((2, TOK, width), BF),
            pltpu.SemaphoreType.DMA((2, 2)),
            pltpu.SemaphoreType.DMA((7,)),
        ] + Summing.sum_scratch(chunks, depth) + Summing.give_scratch(2 * EARLY, depth, True),
        compiler_params=pltpu.CompilerParams(
            collective_id=1, has_side_effects=True, vmem_limit_bytes=62 << 20),
        cost_estimate=pl.CostEstimate(
            flops=12 * count * width * ff, bytes_accessed=40 << 20, transcendentals=0),
    )(nt, nt_flat, dy, dy_flat, gain, w_inner, w_outer, hidden)


def rest_kernel(depth, scale, normed_flat, dq, dk, dv, mix, gb, small, done, out, out_ref, share, *refs):
    width = normed_flat.shape[0]
    each = width // CH_COLS
    chunks = share.shape[0]
    swap = Exchange(done, out_ref, *refs[:3], False, SWAPS)
    summing = Summing(depth, share, refs[3:13], refs[13:], scale, targets=(out,), mixed=False)
    summing.meet()

    def terms(which, cut):
        if which == 0:
            return dot(mix[...], gb[:, cut], 1, 0)
        if which == 1:
            return dot(normed_flat[...], dq[cut], 1, 1)
        return dot(normed_flat[...], (dk if which == 2 else dv)[:, cut], 1, 0)

    def step(p, _):
        for kind in range(2):
            c = 2 * p + kind
            for which in range(4):

                @pl.when(c // each == which)
                def _():
                    cut = spans((c - which * each) * CH_COLS, CH_COLS, CH_COLS)
                    summing.put(c, terms(which, cut))

            @pl.when(c >= 4 * each)
            def _():
                summing.put(c, small[:, spans((c - 4 * each) * CH_COLS, CH_COLS, CH_COLS)])

        for i in range(2):

            @pl.when(2 * p + i < SWAPS)
            def _():
                swap.start(2 * p + i)

        summing.tick(p, BOTH_STEPS, REST_LAG)
        return 0

    lax.fori_loop(0, chunks // 2, step, 0)
    summing.drain(chunks // 2, BOTH_STEPS, REST_LAG)
    summing.finish()
    swap.finish()


def rest_summed(normed_flat, dq, dk, dv, mix, gb, small, done, scale, depth):
    width, count = normed_flat.shape
    chunks = (4 * width + small.shape[1]) // CH_COLS
    vm = pl.BlockSpec(memory_space=pltpu.VMEM)
    anywhere = pl.BlockSpec(memory_space=pl.ANY)
    mine, row_len, _ = done.shape
    return pl.pallas_call(
        functools.partial(rest_kernel, depth, scale),
        in_specs=[vm] * 7 + [anywhere],
        out_specs=[anywhere] * 2,
        out_shape=[
            jax.ShapeDtypeStruct((CH_ROWS, chunks * CH_COLS), BF),
            jax.ShapeDtypeStruct((mine * SEQ, row_len // SEQ, width), BF),
        ],
        scratch_shapes=[pltpu.VMEM(Summing.share_shape(chunks, depth), BF)]
        + Exchange.scratch(SWAPS)
        + Summing.sum_scratch(chunks, depth)
        + Summing.give_scratch(chunks, depth, False),
        compiler_params=pltpu.CompilerParams(
            collective_id=2, has_side_effects=True, vmem_limit_bytes=60 << 20),
    )(normed_flat, dq, dk, dv, mix, gb, small, done)


def reduce_plain(flat, scale):
    share = lax.psum_scatter(flat, ("rows", "seq"), scatter_dimension=0, tiled=True)
    share = (share.astype(F32) * scale).astype(BF)
    return lax.all_gather(share, ("rows", "seq"), axis=0, tiled=True)


def prepare(seg_lengths, bucket_bias_table, mine, row_len):
    bucket_count = bucket_bias_table.shape[0]
    seg_count = seg_lengths.shape[1]
    lengths = lax.dynamic_slice_in_dim(seg_lengths, lax.axis_index("seq") * mine, mine, 0)
    seg = segment_ids(lengths, row_len)
    slots = jnp.arange(HALF, dtype=jnp.int32)
    fq = (seg[:, None, :] == slots[None, :, None]).astype(BF)
    fk_half = jnp.where(
        slots < seg_count,
        jnp.where(seg[:, :, None] != slots, NEGATIVE, 0.0),
        jnp.where((slots >= ONES_AT) & (slots < ONES_AT + 3), 1.0, 0.0),
    ).astype(BF)
    fk = jnp.concatenate([fk_half, fk_half], axis=2)
    blocks = row_len // BLK
    offsets = (
        (jnp.arange(2 * blocks - 1, dtype=jnp.int32) - (blocks - 1))[:, None, None] * BLK
        + jnp.arange(BLK, dtype=jnp.int32)[None, :, None]
        - jnp.arange(BLK, dtype=jnp.int32)[None, None, :]
    )
    buckets = bucket_of(offsets, bucket_count)
    indicator = (
        buckets[None] == jnp.arange(bucket_count, dtype=jnp.int32)[:, None, None, None]
    ).astype(BF)
    bias = (
        jnp.einsum("zbfu,zi->ibfu", indicator, bucket_bias_table, preferred_element_type=F32)
        * LOG2E
    )
    return fq, fk, bias


def per_device(
    tokens, seg_lengths, w_query, w_key, w_value, w_output, w_inner, w_outer,
    gain_attn, gain_ffn, bucket_bias_table, cotangent,
):
    rows_dev, piece_len, width = tokens.shape
    seq_parts = lax.axis_size("seq")
    row_len = piece_len * seq_parts
    mine = rows_dev // seq_parts
    count = mine * row_len
    gain_one = gain_attn.astype(F32)[None]
    gain_two = gain_ffn.astype(F32)[None]
    depth = lax.axis_size("rows") // 2
    scale = float(rows_dev * lax.axis_size("rows") * row_len) ** (-0.5)
    fused = seq_parts == 4 and CH_ROWS % (4 * depth * 16) == 0 and width == CH_ROWS

    def to_rows(array_in):
        out = lax.all_to_all(array_in, "seq", split_axis=0, concat_axis=1, tiled=True)
        return lax.optimization_barrier(out.reshape(count, width))

    def from_rows(array_in):
        return lax.all_to_all(
            array_in.reshape(mine, row_len, width), "seq", split_axis=1, concat_axis=0, tiled=True
        )

    fq, fk, bias = prepare(seg_lengths, bucket_bias_table, mine, row_len)
    tok = tokens if fused else to_rows(tokens)
    normed, normed_flat, q_flat, k_rows, v_rows, *rows = before(
        tok, gain_one, w_query, w_key, w_value, mine, fused
    )
    if fused:
        tok = rows[0]
    mix_flat, stat, *near = attend(
        q_flat, k_rows, v_rows, fq, fk, bias, row_len, cotangent if fused else None
    )
    dy = near[0].reshape(count, width) if fused else to_rows(cotangent)
    hidden, nt, nt_flat, dy_flat = between(tok, mix_flat, w_output, gain_two, dy)
    if fused:
        result, grad_hidden, branch, sum_two, share, *early = ffn_summed(
            nt, nt_flat, dy, dy_flat, gain_two, w_inner, w_outer, hidden, scale, depth
        )
        gives = (share, depth, early[0].shape[1], result)
    else:
        value, slope = gelu_both(dot(nt, w_inner, 1, 0))
        active = value.astype(BF)
        grad_pre = (dot(dy, w_outer, 1, 1) * slope).astype(BF)
        result = (hidden + dot(active, w_outer, 1, 0)).astype(BF)
        sum_outer, sum_inner = dot(active, dy, 0, 0), dot(grad_pre, nt, 0, 0)
        _, inverse = apply_rms_scaling(hidden, gain_two)
        part, sum_two = norm_back(hidden, inverse, gain_two, dot(grad_pre, w_inner, 1, 1))
        grad_hidden = dy.astype(F32) + part
        branch = grad_hidden.astype(BF)
        gives = None
    do_flat = dot(w_output, branch, 1, 1).astype(BF)
    dq_flat, dk_rows, dv_rows, table, *given = attend_back(
        q_flat, k_rows, v_rows, do_flat, mix_flat, stat, fq, fk, bias, row_len, gives
    )
    grad_input, sum_one = after(
        tok, gain_one, grad_hidden, dq_flat, dk_rows, dv_rows, w_query, w_key, w_value
    )
    sum_table = jnp.sum(table, axis=2).T
    small = jnp.concatenate([sum_one.reshape(-1), sum_two.reshape(-1), sum_table.reshape(-1)])
    if fused:
        small = jnp.pad(small, (0, -small.size % (CH_ROWS * BLK))).reshape(CH_ROWS, BLK)
        small = jnp.pad(small.astype(BF), ((0, 0), (0, 2 * CH_COLS - BLK)))
        total, grad_back = rest_summed(
            normed_flat, dq_flat, dk_rows, dv_rows, mix_flat, branch, small,
            grad_input.reshape(mine, row_len, width), scale, depth,
        )
        out_back = given[2]
        grad_inner = jnp.concatenate([early[0], given[0]], axis=1).astype(F32)
        grad_outer = jnp.concatenate([early[1], given[1]], axis=0).astype(F32)
        squares = [total[:, i * width : (i + 1) * width].astype(F32) for i in range(4)]
        rest = total[:, 4 * width : 4 * width + BLK].astype(F32).reshape(-1)
    else:
        devices = lax.axis_size("rows") * seq_parts
        small = jnp.pad(small, (0, -small.size % (16 * devices * width))).reshape(-1, width)
        parts = (
            dot(mix_flat, branch, 1, 0), dot(normed, dq_flat, 0, 1), dot(normed, dk_rows, 0, 0),
            dot(normed, dv_rows, 0, 0), small, sum_outer, sum_inner,
        )
        total = reduce_plain(jnp.concatenate([g.astype(BF) for g in parts]), scale).astype(F32)
        outs, at = [], 0
        for g in parts:
            outs.append(total[at : at + g.shape[0]])
            at += g.shape[0]
        squares, grad_outer, grad_inner = outs[:4], outs[5], outs[6].T
        rest = outs[4].reshape(-1)
        out_back, grad_back = from_rows(result), from_rows(grad_input)
    return (
        out_back,
        grad_back,
        squares[1],
        squares[2],
        squares[3],
        squares[0],
        grad_inner,
        grad_outer,
        rest[:width],
        rest[width : 2 * width],
        rest[2 * width : 2 * width + sum_table.size].reshape(sum_table.shape),
    )


def solution(mesh):
    tok = P("rows", "seq", None)
    in_specs = (tok, P("rows", None)) + (P(),) * 9 + (tok,)
    out_specs = (tok, tok) + (P(),) * 9
    return jax.shard_map(
        per_device, mesh=mesh, in_specs=in_specs, out_specs=out_specs, check_vma=False
    )
```

```python
import functools
import math

import jax
import jax.numpy as jnp
from jax import lax
from jax.experimental import pallas as pl
from jax.experimental.pallas import tpu as pltpu
from jax.sharding import PartitionSpec as P

EPSILON = 1e-06
THRESHOLDS = (12, 16, 23, 32, 46, 64, 91)
NEGATIVE = -1e30
BUCKETS = 32
GELU_SCALE = math.sqrt(2.0 / math.pi)
GELU_CUBIC = 0.044715
LOG2E = math.log2(math.e)
BLK = 128
QT = 256
HALF = 64
ONES_AT = 8
BF = jnp.bfloat16
F32 = jnp.float32
TOK = 512
TILE_TOK = 256
MESH = pl.DeviceIdType.MESH
CH_ROWS, CH_COLS = 768, 256
SUM_STEPS = ((1,), (2,), (3,), (4,))
GIVE_STEPS = ((5,), (6,), (7,), (8,), (9,))
GIVE_LAG = 3
EARLY = 6
SWAPS = 12
SEQ = 4
SEND_SLOTS = 8
BOTH_STEPS = ((1,), (2,), (3,), (4, 5), (6,), (7,), (8,), (9,))
REST_LAG = 2


def bucket_of(offsets, bucket_count):
    distance = jnp.abs(offsets)
    levels = 8 + sum(((distance >= threshold).astype(jnp.int32) for threshold in THRESHOLDS))
    return jnp.where(offsets > 0, bucket_count // 2, 0) + jnp.where(distance < 8, distance, levels)


def segment_ids(seg_lengths, row_len):
    order = jnp.arange(seg_lengths.shape[1])
    ends = jnp.sum(
        jnp.where(order[None, :, None] <= order[None, None, :], seg_lengths[:, :, None], 0), axis=1
    )
    positions = jnp.arange(row_len, dtype=jnp.int32)
    return jnp.sum((positions[None, :, None] >= ends[:, None, :]).astype(jnp.int32), axis=2)


def gelu_both(x):
    square = x * x
    tangent = jnp.tanh(x * (GELU_SCALE + GELU_SCALE * GELU_CUBIC * square))
    upper = 0.5 * tangent + 0.5
    slope = upper + (0.5 * x) * (1.0 - tangent * tangent) * (
        GELU_SCALE + 3.0 * GELU_SCALE * GELU_CUBIC * square
    )
    return x * upper, slope


def apply_rms_scaling(values_in, gain_row):
    inverse = lax.rsqrt(jnp.mean(values_in * values_in, axis=-1, keepdims=True) + EPSILON)
    return (values_in * inverse * gain_row, inverse)


def norm_back(values_in, inverse, gain_row, grad_normed):
    weighted = grad_normed * gain_row
    inner_mean = jnp.mean(weighted * values_in, axis=-1, keepdims=True)
    grad_values = inverse * weighted - values_in * (inverse * inverse * inverse) * inner_mean
    grad_gain = jnp.sum(grad_normed * values_in * inverse, axis=0)
    return (grad_values, grad_gain)


def dot(a, b, ca, cb):
    return lax.dot_general(a, b, (((ca,), (cb,)), ((), ())), preferred_element_type=F32)


def halves(value, own, other, head):
    lane = lax.broadcasted_iota(jnp.int32, value.shape, 1)
    mine = (lane < HALF) if head == 0 else (lane >= HALF)
    return jnp.where(mine, value, other)


def stack_q(q_pair, features, head):
    scaled = q_pair[head * HALF : (head + 1) * HALF].astype(F32) * LOG2E
    high = scaled.astype(BF)
    low = (scaled - high.astype(F32)).astype(BF)
    zero = jnp.zeros_like(high)
    if head == 0:
        return jnp.concatenate([high, zero, low, features], axis=0)
    return jnp.concatenate([zero, high, features, low], axis=0)


def bias_tile(bias_ref, head, key_block, query_block, number, blocks):
    at = key_block - query_block + blocks - 1
    return jnp.concatenate([bias_ref[head, at - i] for i in range(number)], axis=1)


def attend_kernel(q_ref, k_ref, v_ref, fq_ref, fk_ref, bias_ref, *refs):
    if len(refs) > 2:
        away, mix_ref, stat_ref, near, *sems = refs
        swap = Exchange(away, near, *sems, True)
        now = pl.program_id(0) * pl.num_programs(1) + pl.program_id(1)

        @pl.when(now == 0)
        def _():
            swap.meet()
            swap.start(0)

        @pl.when(now == pl.num_programs(0) * pl.num_programs(1) - 1)
        def _():
            swap.wait(0)
    else:
        mix_ref, stat_ref = refs
    row_len = k_ref.shape[0]
    blocks = row_len // BLK
    keys, vals, features_q, features_k = k_ref[...], v_ref[...], fq_ref[0], fk_ref[0]
    q_pair = q_ref[...].T
    lane = lax.broadcasted_iota(jnp.int32, (row_len, BLK), 1)
    ones = jnp.ones_like(vals)
    queries = [stack_q(q_pair, features_q, h) for h in range(2)]
    keys_all = [jnp.concatenate([keys, halves(keys, None, features_k, h)], axis=1) for h in range(2)]
    values = [halves(vals, None, ones, h) for h in range(2)]
    mixed, stats = [], []
    for h in range(2):
        raw = dot(keys_all[h], queries[h], 1, 0)
        scores = [
            raw[b * BLK : (b + 1) * BLK] + bias_tile(bias_ref, h, b, 0, blocks, blocks)
            for b in range(blocks)
        ]
        top = functools.reduce(jnp.maximum, scores)
        top = jnp.max(top, axis=0, keepdims=True)
        probs = jnp.concatenate([jnp.exp2(s - top).astype(BF) for s in scores], axis=0)
        summed = dot(probs, values[h], 0, 0)
        at = HALF if h == 0 else 0
        total = summed[:, at : at + 1]
        mixed.append(summed * (1.0 / total))
        stats.append(top)
        stats.append(total)
    mix_ref[...] = jnp.where(lane < HALF, mixed[0], mixed[1]).astype(BF)
    totals = jnp.where(lane == 0, stats[1], stats[3]).T
    for h in range(2):
        stat_ref[0, 0, h : h + 1] = stats[2 * h] + jnp.log2(totals[h : h + 1])


def three(row):
    one = row.astype(BF)
    rest = row - one.astype(F32)
    two = rest.astype(BF)
    return one, two, (rest - two.astype(F32)).astype(BF)


def feature_rows(base, row):
    parts = three(row)
    at = lax.broadcasted_iota(jnp.int32, base.shape, 0)
    out = base.astype(F32)
    for i, part in enumerate(parts):
        out = jnp.where(at == ONES_AT + i, part.astype(F32), out)
    return out.astype(BF)


def block_buckets(at, blocks):
    ahead = (at - blocks + 1) * BLK
    low, high = ahead - BLK + 1, ahead + BLK - 1
    if low >= THRESHOLDS[-1] or high <= -THRESHOLDS[-1]:
        return BUCKETS - 1 if low > 0 else BUCKETS // 2 - 1, None, ()
    row = lax.broadcasted_iota(jnp.int32, (BLK, BLK), 0)
    lane = lax.broadcasted_iota(jnp.int32, (BLK, BLK), 1)
    first = BUCKETS // 2 if low > 0 else 0
    last = BUCKETS // 2 if high <= 0 else BUCKETS
    return None, bucket_of(ahead + row - lane, BUCKETS), range(first, last)


def bias_blocks(table_ref, bias_ref):
    heads, number = bias_ref.shape[:2]
    for at in range(number):
        one, bucket, some = block_buckets(at, (number + 1) // 2)

        def head_blocks(h, _):
            if one is not None:
                bias_ref[h, at] = jnp.full((BLK, BLK), table_ref[one, h] * LOG2E, F32)
                return 0
            value = jnp.zeros((BLK, BLK), F32)
            for b in some:
                value = jnp.where(bucket == b, table_ref[b, h] * LOG2E, value)
            bias_ref[h, at] = value
            return 0

        lax.fori_loop(0, heads, head_blocks, 0)


def bucket_sums(acc_ref, head, blocks):
    sums = BUCKETS * [jnp.zeros((1, BLK), F32)]
    for at in range(2 * blocks - 1):
        value = acc_ref[head, at]
        one, bucket, some = block_buckets(at, blocks)
        if one is not None:
            sums[one] = sums[one] + jnp.sum(value, axis=0, keepdims=True)
        for b in some:
            picked = jnp.sum(jnp.where(bucket == b, value, 0.0), axis=0, keepdims=True)
            sums[b] = sums[b] + picked
    return jnp.concatenate(sums, axis=0)


def attend_back_kernel(
    depth, q_ref, k_ref, v_ref, wp_ref, gb_ref, mix_ref, stat_ref, fq_ref, fk_ref, bias_ref, *refs
):
    if depth:
        share, done, dq_ref, dk_ref, dv_ref, table_ref, gi_ref, go_ref, out_ref = refs[:9]
        acc_ref, dk_sum, dv_sum, *sems = refs[9:15]
        swap = Exchange(done, out_ref, *sems, False, SWAPS)
        giving = Summing(
            depth, share, give_refs=refs[15:], targets=(gi_ref, go_ref), turned=True,
            given=(share.shape[0] // 2 - gi_ref.shape[1] // CH_COLS, share.shape[0] // 2),
        )
        now = pl.program_id(0) * pl.num_programs(1) + pl.program_id(1)

        @pl.when(now == 0)
        def _():
            giving.meet()

        @pl.when(now < SWAPS)
        def _():
            swap.start(now)

        giving.tick(now + giving.given[0] + GIVE_LAG, GIVE_STEPS, GIVE_LAG)
    else:
        dq_ref, dk_ref, dv_ref, table_ref, acc_ref, dk_sum, dv_sum = refs
    row_len = k_ref.shape[0]
    blocks = row_len // BLK
    keys, vals, features_k = k_ref[...], v_ref[...], fk_ref[0]
    k_flat = keys.T
    do_pair = dot(wp_ref[...], gb_ref[...], 1, 1).astype(BF)
    q_rows, do_rows = q_ref[...], do_pair.T
    q_pair, mix_pair = q_rows.T, mix_ref[...].T
    zero_rows = jnp.zeros((row_len, BLK), BF)

    @pl.when(pl.program_id(1) == 0)
    def _():
        acc_ref[...] = jnp.zeros_like(acc_ref)

    for head in range(2):
        span = slice(head * HALF, (head + 1) * HALF)
        do_head = do_pair[span]
        delta = jnp.sum(do_head.astype(F32) * mix_pair[span].astype(F32), axis=0, keepdims=True)
        zeros = jnp.zeros((HALF, row_len), BF)
        q_all = stack_q(q_pair, feature_rows(fq_ref[0], -stat_ref[0, 0, head : head + 1]), head)
        k_all = jnp.concatenate([keys, halves(keys, None, features_k, head)], axis=1)
        v_all = halves(vals, None, features_k, head)
        back = feature_rows(zeros, -delta)
        do_all = jnp.concatenate([do_head, back] if head == 0 else [back, do_head], axis=0)
        q_own = halves(q_rows, None, zero_rows, head)
        do_own = halves(do_rows, None, zero_rows, head)
        for tile in range(row_len // QT):
            cut = slice(tile * QT, (tile + 1) * QT)
            raw = dot(k_all, q_all[:, cut], 1, 0)
            grad_probs = dot(v_all, do_all[:, cut], 1, 0)
            probs_list, grads_list = [], []
            sums = {}
            for b in range(blocks):
                part = slice(b * BLK, (b + 1) * BLK)
                probs = jnp.exp2(raw[part] + bias_tile(bias_ref, head, b, tile * (QT // BLK), QT // BLK, blocks))
                grads = probs * grad_probs[part]
                probs_list.append(probs.astype(BF))
                grads_list.append(grads.astype(BF))
                for i in range(QT // BLK):
                    at = b - tile * (QT // BLK) - i + blocks - 1
                    piece = grads[:, i * BLK : (i + 1) * BLK]
                    sums[at] = sums[at] + piece if at in sums else piece
            for at, piece in sums.items():
                acc_ref[head, at] += piece
            probs_low = jnp.concatenate(probs_list, axis=0)
            grads_low = jnp.concatenate(grads_list, axis=0)
            dv_new = dot(probs_low, do_own[cut], 1, 0)
            dk_new = dot(grads_low, q_own[cut], 1, 0)
            if head == 0 and tile == 0:
                dv_sum[...] = dv_new
                dk_sum[...] = dk_new
            else:
                dv_sum[...] += dv_new
                dk_sum[...] += dk_new
            dq_ref[span, cut] = dot(k_flat[span], grads_low, 1, 0).astype(BF)
    dk_ref[...] = dk_sum[...].astype(BF)
    dv_ref[...] = dv_sum[...].astype(BF)

    @pl.when(pl.program_id(1) == pl.num_programs(1) - 1)
    def _():
        for head in range(2):
            table_ref[head] = bucket_sums(acc_ref, head, blocks)

    if depth:
        steps = pl.num_programs(0) * pl.num_programs(1)

        @pl.when(now == steps - 1)
        def _():
            giving.drain(steps + giving.given[0] + GIVE_LAG, GIVE_STEPS, GIVE_LAG)
            giving.finish()
            swap.finish()


def specs(row_len):
    flat = pl.BlockSpec((BLK, row_len), lambda g, r: (g, r))
    rows = pl.BlockSpec((row_len, BLK), lambda g, r: (r, g))
    stat = pl.BlockSpec((1, 1, 2, row_len), lambda g, r: (r, g, 0, 0))
    fq = pl.BlockSpec((1, HALF, row_len), lambda g, r: (r, 0, 0))
    fk = pl.BlockSpec((1, row_len, BLK), lambda g, r: (r, 0, 0))
    blocks = 2 * (row_len // BLK) - 1
    bias = pl.BlockSpec((2, blocks, BLK, BLK), lambda g, r: (g, 0, 0, 0))
    return flat, rows, stat, fq, fk, bias


def attend(q_rows, k_rows, v_rows, fq, fk, bias, row_len, away=None):
    count, width = q_rows.shape
    flat, rows, stat, fqs, fks, biass = specs(row_len)
    pairs, row_count = width // BLK, count // row_len
    anywhere = pl.BlockSpec(memory_space=pl.ANY)
    extra, near, scratch, params = (), [], [], {}
    if away is not None:
        extra, near = (away,), [jax.ShapeDtypeStruct((row_count, row_len, width), BF)]
        scratch, params = Exchange.scratch(), dict(collective_id=5, has_side_effects=True)
    return pl.pallas_call(
        attend_kernel,
        grid=(pairs, row_count),
        in_specs=[rows, rows, rows, fqs, fks, biass] + [anywhere] * len(extra),
        out_specs=[rows, stat] + [anywhere] * len(near),
        out_shape=[
            jax.ShapeDtypeStruct((count, width), BF),
            jax.ShapeDtypeStruct((row_count, pairs, 2, row_len), F32),
        ] + near,
        scratch_shapes=scratch,
        compiler_params=pltpu.CompilerParams(vmem_limit_bytes=48 << 20, **params),
        cost_estimate=pl.CostEstimate(
            flops=4 * 4 * width * count * row_len,
            bytes_accessed=8 * width * count,
            transcendentals=0,
        ),
    )(q_rows, k_rows, v_rows, fq, fk, bias, *extra)


def attend_back(q_rows, k_rows, v_rows, wp, gb, mix, stat_in, fq, fk, bias, row_len, gives):
    count, width = q_rows.shape
    flat, rows, stat, fqs, fks, biass = specs(row_len)
    pairs, row_count = width // BLK, count // row_len
    anywhere = pl.BlockSpec(memory_space=pl.ANY)
    depth, extra, extra_in, extra_out, scratch, params = 0, (), [], [], [], {}
    if gives is not None:
        share, depth, early, done = gives
        shapes = [(width, share.shape[0] // 2 * CH_COLS - early), (share.shape[0] // 2 * CH_COLS - early, width)]
        done = done.reshape(row_count, row_len, width)
        extra, extra_in = (share, done), [pl.BlockSpec(share.shape, lambda g, r: (0, 0, 0)), anywhere]
        extra_out = [jax.ShapeDtypeStruct(shape, BF) for shape in shapes]
        extra_out += [jax.ShapeDtypeStruct((row_count * SEQ, row_len // SEQ, width), BF)]
        scratch = Exchange.scratch(SWAPS) + Summing.give_scratch(share.shape[0], depth, True)
        params = dict(collective_id=3, has_side_effects=True)
    return pl.pallas_call(
        functools.partial(attend_back_kernel, depth),
        grid=(pairs, row_count),
        in_specs=[
            rows, rows, rows, pl.BlockSpec((BLK, width), lambda g, r: (g, 0)),
            pl.BlockSpec((row_len, width), lambda g, r: (r, 0)), rows, stat, fqs, fks, biass,
        ] + extra_in,
        out_specs=[flat, rows, rows, pl.BlockSpec((2, BUCKETS, BLK), lambda g, r: (g, 0, 0))]
        + [anywhere] * len(extra_out),
        out_shape=[
            jax.ShapeDtypeStruct((width, count), BF),
            jax.ShapeDtypeStruct((count, width), BF),
            jax.ShapeDtypeStruct((count, width), BF),
            jax.ShapeDtypeStruct((2 * pairs, BUCKETS, BLK), F32),
        ] + extra_out,
        scratch_shapes=[pltpu.VMEM((2,) + bias.shape[1:], F32)]
        + [pltpu.VMEM((row_len, BLK), F32)] * 2
        + scratch,
        compiler_params=pltpu.CompilerParams(vmem_limit_bytes=48 << 20, **params),
        cost_estimate=pl.CostEstimate(
            flops=10 * 4 * width * count * row_len,
            bytes_accessed=16 * width * count,
            transcendentals=0,
        ),
    )(q_rows, k_rows, v_rows, wp, gb, mix, stat_in, fq, fk, bias, *extra)


class Place:
    def __init__(self):
        self.r, self.s = lax.axis_index("rows"), lax.axis_index("seq")
        self.x, self.z = lax.rem(self.r, 2), self.r // 2
        self.core, self.y = lax.rem(self.s, 2), self.s // 2

    def at(self, x=None, y=None, core=None, z=None):
        x = self.x if x is None else x
        y = self.y if y is None else y
        core = self.core if core is None else core
        z = self.z if z is None else z
        return (z * 2 + x, y * 2 + core)


def spans(base, size, step=16):
    return pl.ds(pl.multiple_of(base, step), size)


class Exchange:
    def __init__(self, src, dst, send, recv, keep, to_rows, parts=1):
        self.src, self.dst, self.send, self.recv, self.keep, self.to_rows = src, dst, send, recv, keep, to_rows
        pieces, rows = (src, dst) if to_rows else (dst, src)
        self.mine, self.piece, self.parts = rows.shape[0], pieces.shape[1], parts
        self.r, self.s = lax.axis_index("rows"), lax.axis_index("seq")

    @staticmethod
    def scratch(parts=1):
        dma = pltpu.SemaphoreType.DMA
        return [dma((parts, SEQ - 1)), dma((parts, SEQ - 1)), dma((parts,))]

    def meet(self):
        barrier = pltpu.get_barrier_semaphore()
        for k in range(1, SEQ):
            place = (self.r, lax.rem(self.s + k, SEQ))
            pl.semaphore_signal(barrier, inc=1, device_id=place, device_id_type=MESH)
        pl.semaphore_wait(barrier, SEQ - 1)

    def ends(self, part, peer):
        if self.parts <= self.mine:
            size, long = self.mine // self.parts, self.piece
            row, at = part * size, 0
        else:
            cuts = self.parts // self.mine
            size, long = 1, self.piece // cuts
            row, at = part // cuts, lax.rem(part, cuts) * long
        if self.to_rows:
            return (self.src.at[pl.ds(peer * self.mine + row, size), spans(at, long)],
                    self.dst.at[pl.ds(row, size), spans(self.s * self.piece + at, long)])
        return (self.src.at[pl.ds(row, size), spans(peer * self.piece + at, long)],
                self.dst.at[pl.ds(self.s * self.mine + row, size), spans(at, long)])

    def copies(self, part):
        out = []
        for k in range(1, SEQ):
            peer = lax.rem(self.s + k, SEQ)
            src, dst = self.ends(part, peer)
            out.append(pltpu.make_async_remote_copy(
                src_ref=src, dst_ref=dst, send_sem=self.send.at[part, k - 1],
                recv_sem=self.recv.at[part, SEQ - 1 - k], device_id=(self.r, peer), device_id_type=MESH))
        src, dst = self.ends(part, self.s)
        return out, pltpu.make_async_copy(src, dst, self.keep.at[part])

    def start(self, part):
        away, here = self.copies(part)
        for d in away:
            d.start()
        here.start()

    def wait(self, part):
        away, here = self.copies(part)
        for d in away:
            d.wait()
        here.wait()

    def finish(self):
        def one(part, _):
            self.wait(part)
            return 0

        lax.fori_loop(0, self.parts, one, 0)


class Summing:
    def __init__(self, depth, share, sum_refs=None, give_refs=None, scale=1.0, targets=None, turned=False, mixed=True, given=None):
        if sum_refs is not None:
            (self.snd, self.got, self.own, self.got_one, self.got_two, self.got_z,
             self.send_sum, self.recv_sum, self.send_sum_z, self.recv_sum_z) = sum_refs
        if give_refs is not None:
            (self.gath, self.flip, self.sems,
             self.send_give, self.recv_give, self.send_give_z, self.recv_give_z) = give_refs
        self.summed = (0, share.shape[0] // 2)
        self.given = self.summed if given is None else given
        self.share, self.chunks, self.targets, self.turned = share, share.shape[0], targets, turned
        self.depth, self.scale, self.mixed = depth, scale, mixed
        self.me = Place()
        self.w = CH_COLS // 2
        self.half, self.quarter = CH_ROWS // 2, CH_ROWS // 4
        self.piece = CH_ROWS // (4 * depth)

    @staticmethod
    def sum_scratch(chunks, depth):
        w, piece = CH_COLS // 2, CH_ROWS // (4 * depth)
        dma = pltpu.SemaphoreType.DMA
        return [
            pltpu.VMEM((SEND_SLOTS, CH_ROWS, w), BF),
            pltpu.VMEM((chunks, CH_ROWS, w), BF),
            pltpu.VMEM((chunks, CH_ROWS, w), BF),
            pltpu.VMEM((chunks, CH_ROWS // 2, w), BF),
            pltpu.VMEM((chunks, CH_ROWS // 4, w), BF),
            pltpu.VMEM((chunks, depth - 1, piece, w), BF),
            dma((3, chunks)), dma((3, chunks)),
            dma((chunks, depth - 1)), dma((chunks, depth - 1)),
        ]

    @staticmethod
    def give_scratch(chunks, depth, turned):
        dma = pltpu.SemaphoreType.DMA
        return [
            pltpu.VMEM((chunks, 2, CH_ROWS, CH_COLS // 2), BF),
            pltpu.VMEM((2, CH_COLS, CH_ROWS) if turned else (1, 16, 128), BF),
            dma((2, chunks)),
            dma((3, chunks)), dma((3, chunks)),
            dma((chunks, depth - 1)), dma((chunks, depth - 1)),
        ]

    @staticmethod
    def share_shape(chunks, depth):
        return (chunks, CH_ROWS // (4 * depth), CH_COLS // 2)

    def meet(self):
        me = self.me
        barrier = pltpu.get_barrier_semaphore()
        others = [me.at(x=1 - me.x)] + [(me.r, lax.rem(me.s + k, SEQ)) for k in range(1, SEQ)]
        others += [me.at(z=lax.rem(me.z + k, self.depth)) for k in range(1, self.depth)]
        for place in others:
            pl.semaphore_signal(barrier, inc=1, device_id=place, device_id_type=MESH)
        pl.semaphore_wait(barrier, len(others))

    def copy(self, src, dst, stage, c, place):
        if stage < 3:
            send, recv = self.send_sum.at[stage, c], self.recv_sum.at[stage, c]
        else:
            send, recv = self.send_give.at[stage - 3, c], self.recv_give.at[stage - 3, c]
        return pltpu.make_async_remote_copy(
            src_ref=src, dst_ref=dst, send_sem=send, recv_sem=recv, device_id=place, device_id_type=MESH)

    def part(self, c, start, size):
        return self.gath.at[c, self.me.core, spans(start, size)]

    def order(self, c):
        me, odd = self.me, lax.rem(c, 2) if self.mixed else 0
        one = me.x + odd * (me.y - me.x)
        two = me.y + odd * (me.x - me.y)
        x_there, y_there = 1 - 2 * me.x, 2 - 4 * me.y
        first = (me.r + (1 - odd) * x_there, me.s + odd * y_there)
        second = (me.r + odd * x_there, me.s + (1 - odd) * y_there)
        return one, two, first, second

    def put(self, c, value):
        left, right = value[:, : self.w].astype(BF), value[:, self.w :].astype(BF)
        first = self.me.core == 0
        self.own[c] = jnp.where(first, left, right)
        self.snd[lax.rem(c, SEND_SLOTS)] = jnp.where(first, right, left)
        self.step_core(c).start()

    def step_core(self, c):
        return self.copy(self.snd.at[lax.rem(c, SEND_SLOTS)], self.got.at[c], 0, c, self.me.at(core=1 - self.me.core))

    def step_one(self, c):
        one, _, place, _ = self.order(c)
        return self.copy(self.own.at[c, spans((1 - one) * self.half, self.half)], self.got_one.at[c], 1, c, place)

    def step_two(self, c):
        one, two, _, place = self.order(c)
        part = spans(one * self.half + (1 - two) * self.quarter, self.quarter)
        return self.copy(self.own.at[c, part], self.got_two.at[c], 2, c, place)

    def base(self, c):
        one, two, _, _ = self.order(c)
        return one * self.half + two * self.quarter

    def step_z(self, c, k):
        to = lax.rem(self.me.z + k, self.depth)
        return pltpu.make_async_remote_copy(
            src_ref=self.own.at[c, spans(self.base(c) + to * self.piece, self.piece)],
            dst_ref=self.got_z.at[c, self.depth - 1 - k],
            send_sem=self.send_sum_z.at[c, k - 1], recv_sem=self.recv_sum_z.at[c, self.depth - 1 - k],
            device_id=self.me.at(z=to), device_id_type=MESH)

    def mine(self, c):
        return self.part(c, self.base(c) + self.me.z * self.piece, self.piece)

    def give_z(self, c, k):
        return pltpu.make_async_remote_copy(
            src_ref=self.mine(c), dst_ref=self.mine(c),
            send_sem=self.send_give_z.at[c, k - 1], recv_sem=self.recv_give_z.at[c, self.depth - 1 - k],
            device_id=self.me.at(z=lax.rem(self.me.z + k, self.depth)), device_id_type=MESH)

    def give_two(self, c):
        part = self.part(c, self.base(c), self.quarter)
        return self.copy(part, part, 3, c, self.order(c)[3])

    def give_one(self, c):
        one, _, place, _ = self.order(c)
        part = self.part(c, one * self.half, self.half)
        return self.copy(part, part, 4, c, place)

    def give_core(self, c):
        part = self.part(c, 0, CH_ROWS)
        return self.copy(part, part, 5, c, self.me.at(core=1 - self.me.core))

    def leave(self, c, kind):
        if len(self.targets) == 1:
            array, at = self.targets[0], c * CH_COLS
        else:
            array, at = self.targets[kind], (c // 2 - self.given[0]) * CH_COLS
        if self.turned and kind == 1:
            flip = self.flip.at[lax.rem(c // 2, 2)]
            return [pltpu.make_async_copy(flip, array.at[spans(at, CH_COLS, CH_COLS)], self.sems.at[0, c])]
        return [
            pltpu.make_async_copy(
                self.gath.at[c, i], array.at[:, spans(at + i * self.w, self.w, 128)], self.sems.at[i, c])
            for i in range(2)
        ]

    def add(self, c, start, size, from_ref):
        part = spans(start, size)
        self.own[c, part] = (self.own[c, part].astype(F32) + from_ref[c].astype(F32)).astype(BF)

    def run(self, stage, c, kind):
        depth = self.depth
        if stage == 1:
            self.step_core(c).wait()
            self.add(c, 0, CH_ROWS, self.got)
            self.step_one(c).start()
        if stage == 2:
            self.step_one(c).wait_recv()
            self.add(c, self.order(c)[0] * self.half, self.half, self.got_one)
            self.step_two(c).start()
        if stage == 3:
            self.step_two(c).wait_recv()
            self.add(c, self.base(c), self.quarter, self.got_two)
            for k in range(1, depth):
                self.step_z(c, k).start()
        if stage == 4:
            for k in range(1, depth):
                self.step_z(c, k).wait_recv()
            total = self.own[c, spans(self.base(c) + self.me.z * self.piece, self.piece)].astype(F32)
            for k in range(depth - 1):
                total = total + self.got_z[c, k].astype(F32)
            self.share[c] = (total * self.scale).astype(BF)
            for d in (self.step_one(c), self.step_two(c)):
                d.wait_send()
            for k in range(1, depth):
                self.step_z(c, k).wait_send()
        if stage == 5:
            self.gath[c, self.me.core, spans(self.base(c) + self.me.z * self.piece, self.piece)] = self.share[c]
            for k in range(1, depth):
                self.give_z(c, k).start()
        if stage == 6:
            for k in range(1, depth):
                self.give_z(c, k).wait_recv()
            self.give_two(c).start()
        if stage == 7:
            self.give_two(c).wait_recv()
            self.give_one(c).start()
        if stage == 8:
            self.give_one(c).wait_recv()
            self.give_core(c).start()
        if stage == 9:
            self.give_core(c).wait_recv()
            if self.turned and kind == 1:

                @pl.when(c // 2 >= self.given[0] + 2)
                def _():
                    for d in self.leave(c - 4, kind):
                        d.wait()

                slot = lax.rem(c // 2, 2)
                for i in range(2):
                    self.flip[slot, i * self.w : (i + 1) * self.w] = self.gath[c, i].T
            for d in self.leave(c, kind):
                d.start()
            for d in (self.give_two, self.give_one, self.give_core):
                d(c).wait_send()
            for k in range(1, depth):
                self.give_z(c, k).wait_send()

    def tick(self, t, steps, lag):
        for at in range(len(steps), 0, -1):
            p = t - at * lag
            for stage in steps[at - 1]:
                low, high = self.summed if stage < 5 else self.given

                @pl.when((p >= low) & (p < high))
                def _():
                    for kind in range(2):
                        self.run(stage, 2 * p + kind, kind)

    def drain(self, start, steps, lag):
        def one(t, _):
            self.tick(t, steps, lag)
            return 0

        last = 0
        for at in range(len(steps), 0, -1):
            for stage in steps[at - 1]:
                last = max(last, (self.summed if stage < 5 else self.given)[1] + at * lag)
        lax.fori_loop(start, last, one, 0)

    def finish(self):
        def one(c, kind):
            for d in self.leave(c, kind):
                d.wait()

        def pair(p, _):
            one(2 * p, 0)
            if not self.turned:
                one(2 * p + 1, 1)
            return 0

        low, high = self.given
        lax.fori_loop(low, high, pair, 0)
        if self.turned:
            for p in range(max(low, high - 2), high):
                one(2 * p + 1, 1)


def before_kernel(
    fused, tok, gain, wq, wk, wv, table, normed_ref, flat_ref, q_ref, k_ref, v_ref, bias_ref, *refs
):
    if fused:
        tok_ref, rows, *sems = refs
        swap = Exchange(tok, rows, *sems, True, rows.shape[0])
        m = pl.program_id(0)

        @pl.when(m == 0)
        def _():
            swap.meet()
            for part in range(rows.shape[0]):
                swap.start(part)

    @pl.when(pl.program_id(0) == 0)
    def _():
        bias_blocks(table, bias_ref)

    if fused:
        swap.wait(m)
        own = rows[m]
        tok_ref[...] = own
        wide = own.astype(F32)
    else:
        wide = tok[...].astype(F32)
    normed = apply_rms_scaling(wide, gain[...])[0].astype(BF)
    normed_ref[...] = normed
    flat_ref[...] = normed.T
    q_ref[...] = dot(normed, wq[...], 1, 0).astype(BF)
    k_ref[...] = dot(normed, wk[...], 1, 0).astype(BF)
    v_ref[...] = dot(normed, wv[...], 1, 0).astype(BF)


def tall(width):
    return pl.BlockSpec((TOK, width), lambda m: (m, 0))


def broad(width):
    return pl.BlockSpec((width, TOK), lambda m: (0, m))


def whole(array):
    return pl.BlockSpec(array.shape, lambda m: (0,) * array.ndim)


def plain_call(kernel, count, ins, in_specs, outs, out_specs, flops, scratch=(), collective_id=None):
    params = {} if collective_id is None else dict(collective_id=collective_id, has_side_effects=True)
    return pl.pallas_call(
        kernel,
        grid=(count // TOK,),
        in_specs=in_specs,
        out_specs=out_specs,
        out_shape=[jax.ShapeDtypeStruct(shape, kind) for shape, kind in outs],
        scratch_shapes=list(scratch),
        compiler_params=pltpu.CompilerParams(vmem_limit_bytes=48 << 20, **params),
        cost_estimate=pl.CostEstimate(flops=flops, bytes_accessed=16 << 20, transcendentals=0),
    )(*ins)


def before(tok, gain, wq, wk, wv, table, mine, fused):
    width = tok.shape[-1]
    count = tok.size // width
    t, f = tall(width), broad(width)
    spec, more, scratch = t, [], []
    bias = (table.shape[1], 2 * (count // mine // BLK) - 1, BLK, BLK)
    if fused:
        spec = pl.BlockSpec(memory_space=pl.ANY)
        more = [((count, width), BF)]
        scratch = [pltpu.VMEM((mine, count // mine, width), BF)] + Exchange.scratch(mine)
    return plain_call(
        functools.partial(before_kernel, fused), count, (tok, gain, wq, wk, wv, table),
        [spec] + [whole(a) for a in (gain, wq, wk, wv)] + [pl.BlockSpec(memory_space=pltpu.SMEM)],
        [((count, width), BF), ((width, count), BF)] + [((count, width), BF)] * 3
        + [(bias, F32)] + more,
        [t, f, t, t, t] + [pl.BlockSpec(bias, lambda m: (0, 0, 0, 0))] + [t] * len(more), 6 * count * width * width, scratch, 4 if fused else None,
    )


def between_kernel(tok, mix, wo, gain, dy, hidden_ref, nt_ref, nt_flat_ref, dy_flat_ref, mix_flat_ref):
    hidden = tok[...].astype(F32) + dot(mix[...], wo[...], 1, 0)
    hidden_ref[...] = hidden
    normed = apply_rms_scaling(hidden, gain[...])[0].astype(BF)
    nt_ref[...] = normed
    nt_flat_ref[...] = normed.T
    dy_flat_ref[...] = dy[...].T
    mix_flat_ref[...] = mix[...].T


def between(tok, mix, wo, gain, dy):
    count, width = tok.shape
    t, f = tall(width), broad(width)
    return plain_call(
        between_kernel, count, (tok, mix, wo, gain, dy), [t, t, whole(wo), whole(gain), t],
        [((count, width), F32), ((count, width), BF)] + [((width, count), BF)] * 3,
        [t, t, f, f, f], 2 * count * width * width,
    )


def after_kernel(tok, gain, gh, dq, dk, dv, wq, wk, wv, grad_ref, gain_ref):
    wide = tok[...].astype(F32)
    _, inverse = apply_rms_scaling(wide, gain[...])
    grad_normed = (
        dot(dq[...].T, wq[...], 1, 1) + dot(dk[...], wk[...], 1, 1) + dot(dv[...], wv[...], 1, 1)
    )
    part, grad_gain = norm_back(wide, inverse, gain[...], grad_normed)
    grad_ref[...] = (gh[...] + part).astype(BF)

    @pl.when(pl.program_id(0) == 0)
    def _():
        gain_ref[...] = jnp.zeros_like(gain_ref)

    gain_ref[...] += grad_gain[None]


def after(tok, gain, gh, dq, dk, dv, wq, wk, wv):
    count, width = tok.shape
    t, f = tall(width), broad(width)
    return plain_call(
        after_kernel, count, (tok, gain, gh, dq, dk, dv, wq, wk, wv),
        [t, whole(gain), t, f, t, t, whole(wq), whole(wk), whole(wv)],
        [((count, width), BF), ((1, width), F32)], [t, whole(gain)], 6 * count * width * width,
    )


def ffn_kernel(depth, scale, nt, nt_flat, dy, dy_flat, gain, wi_hbm, wo_hbm, hidden_hbm,
               res_hbm, gh_hbm, gb_hbm, gain_ref, share, gi_ref, go_ref,
               out_acc, gnt_acc, wi_buf, wo_buf, act, gp, hid, res_buf, gb_buf, w_sem, h_sem, *refs):
    count, width = nt.shape
    tile = 2 * CH_COLS
    tiles = wi_hbm.shape[1] // tile
    parts = count // TOK
    given = gi_ref.shape[1] // CH_COLS
    summing = Summing(
        depth, share, refs[:10], refs[10:], scale, targets=(gi_ref, go_ref), turned=True, given=(0, given)
    )

    def weights(j):
        cut, slot = spans(j * tile, tile, tile), lax.rem(j, 2)
        return (
            pltpu.make_async_copy(wi_hbm.at[:, cut], wi_buf.at[slot], w_sem.at[0, slot]),
            pltpu.make_async_copy(wo_hbm.at[cut], wo_buf.at[slot], w_sem.at[1, slot]),
        )

    def hidden(m):
        return pltpu.make_async_copy(hidden_hbm.at[pl.ds(m * TOK, TOK)], hid, h_sem.at[0])

    for w in weights(0):
        w.start()
    hidden(0).start()
    out_acc[...] = jnp.zeros_like(out_acc)
    gnt_acc[...] = jnp.zeros_like(gnt_acc)
    summing.meet()

    def step(j, _):
        for w in weights(j):
            w.wait()

        @pl.when(j + 1 < tiles)
        def _():
            for w in weights(j + 1):
                w.start()

        slot = lax.rem(j, 2)
        wi, wo = wi_buf.at[slot], wo_buf.at[slot]
        for m in range(count // TILE_TOK):
            part = slice(m * TILE_TOK, (m + 1) * TILE_TOK)
            pre = dot(nt[part], wi[...], 1, 0)
            grad_active = dot(dy[part], wo[...], 1, 1)
            value, slope = gelu_both(pre)
            act[part] = value.astype(BF)
            gp[part] = (grad_active * slope).astype(BF)
        for h in range(2):
            cut = slice(h * CH_COLS, (h + 1) * CH_COLS)
            summing.put(4 * j + 2 * h, dot(nt_flat[...], gp[:, cut], 1, 0))
            summing.put(4 * j + 2 * h + 1, dot(dy_flat[...], act[:, cut], 1, 0))
            if h == 0:
                summing.tick(2 * j, BOTH_STEPS, 1)
        for m in range(count // TILE_TOK):
            part = slice(m * TILE_TOK, (m + 1) * TILE_TOK)
            out_acc[part] += dot(act[part], wo[...], 1, 0)
            gnt_acc[part] += dot(gp[part], wi[...], 1, 1)
        summing.tick(2 * j + 1, BOTH_STEPS, 1)
        return 0

    lax.fori_loop(0, tiles, step, 0)

    def outputs(m):
        rows = pl.ds(m * TOK, TOK)
        return (
            pltpu.make_async_copy(res_buf.at[m % 2], res_hbm.at[rows], h_sem.at[1 + m % 2]),
            pltpu.make_async_copy(gb_buf.at[m % 2], gb_hbm.at[rows], h_sem.at[3 + m % 2]),
            pltpu.make_async_copy(gnt_acc.at[rows], gh_hbm.at[rows], h_sem.at[5 + m % 2]),
        )

    total_gain = jnp.zeros((1, width), F32)
    gain_row = gain[...]
    for m in range(parts):
        summing.tick(2 * tiles + m, BOTH_STEPS, 1)
        rows = slice(m * TOK, (m + 1) * TOK)
        hidden(m).wait()
        if m >= 2:
            for d in outputs(m - 2):
                d.wait()
        value = hid[...]
        res_buf[m % 2] = (value + out_acc[rows]).astype(BF)
        _, inverse = apply_rms_scaling(value, gain_row)
        part, grad_gain = norm_back(value, inverse, gain_row, gnt_acc[rows])
        total_gain = total_gain + grad_gain[None]
        grad_hidden = dy[rows].astype(F32) + part
        gnt_acc[rows] = grad_hidden
        gb_buf[m % 2] = grad_hidden.astype(BF)
        if m + 1 < parts:
            hidden(m + 1).start()
        for d in outputs(m):
            d.start()
    gain_ref[...] = total_gain
    summing.drain(2 * tiles + parts, BOTH_STEPS, 1)
    summing.finish()
    for m in range(max(0, parts - 2), parts):
        for d in outputs(m):
            d.wait()


def ffn_summed(nt, nt_flat, dy, dy_flat, gain, w_inner, w_outer, hidden, scale, depth):
    count, width = nt.shape
    ff = w_inner.shape[1]
    chunks = 2 * ff // CH_COLS
    tile = 2 * CH_COLS
    vm = pl.BlockSpec(memory_space=pltpu.VMEM)
    anywhere = pl.BlockSpec(memory_space=pl.ANY)
    return pl.pallas_call(
        functools.partial(ffn_kernel, depth, scale),
        in_specs=[vm] * 5 + [anywhere] * 3,
        out_specs=[anywhere] * 3 + [vm] * 2 + [anywhere] * 2,
        out_shape=[
            jax.ShapeDtypeStruct((count, width), BF),
            jax.ShapeDtypeStruct((count, width), F32),
            jax.ShapeDtypeStruct((count, width), BF),
            jax.ShapeDtypeStruct((1, width), F32),
            jax.ShapeDtypeStruct(Summing.share_shape(chunks, depth), BF),
            jax.ShapeDtypeStruct((width, EARLY * CH_COLS), BF),
            jax.ShapeDtypeStruct((EARLY * CH_COLS, width), BF),
        ],
        scratch_shapes=[
            pltpu.VMEM((count, width), F32),
            pltpu.VMEM((count, width), F32),
            pltpu.VMEM((2, width, tile), BF),
            pltpu.VMEM((2, tile, width), BF),
            pltpu.VMEM((count, tile), BF),
            pltpu.VMEM((count, tile), BF),
            pltpu.VMEM((TOK, width), F32),
            pltpu.VMEM((2, TOK, width), BF),
            pltpu.VMEM((2, TOK, width), BF),
            pltpu.SemaphoreType.DMA((2, 2)),
            pltpu.SemaphoreType.DMA((7,)),
        ] + Summing.sum_scratch(chunks, depth) + Summing.give_scratch(2 * EARLY, depth, True),
        compiler_params=pltpu.CompilerParams(
            collective_id=1, has_side_effects=True, vmem_limit_bytes=62 << 20),
        cost_estimate=pl.CostEstimate(
            flops=12 * count * width * ff, bytes_accessed=40 << 20, transcendentals=0),
    )(nt, nt_flat, dy, dy_flat, gain, w_inner, w_outer, hidden)


def rest_kernel(depth, scale, *refs):
    sources, (small, done, out, out_ref) = refs[:6], refs[6:10]
    mix, gb, normed_flat, dq, dk, dv = held = refs[10:16]
    load_sem, share, *refs = refs[16:]
    width = normed_flat.shape[0]
    each = width // CH_COLS
    chunks = share.shape[0]
    loads = [pltpu.make_async_copy(a, b, load_sem.at[i]) for i, (a, b) in enumerate(zip(sources, held))]
    needs = (loads[:2], loads[2:4], loads[4:5], loads[5:])
    for d in loads:
        d.start()
    swap = Exchange(done, out_ref, *refs[:3], False, SWAPS)
    summing = Summing(depth, share, refs[3:13], refs[13:], scale, targets=(out,), mixed=False)
    summing.meet()

    def terms(which, cut):
        if which == 0:
            return dot(mix[...], gb[:, cut], 1, 0)
        if which == 1:
            return dot(normed_flat[...], dq[cut], 1, 1)
        return dot(normed_flat[...], (dk if which == 2 else dv)[:, cut], 1, 0)

    def step(p, _):
        for kind in range(2):
            c = 2 * p + kind
            for which in range(4):

                @pl.when(c // each == which)
                def _():
                    @pl.when(c == which * each)
                    def _():
                        for d in needs[which]:
                            d.wait()

                    cut = spans((c - which * each) * CH_COLS, CH_COLS, CH_COLS)
                    summing.put(c, terms(which, cut))

            @pl.when(c >= 4 * each)
            def _():
                summing.put(c, small[:, spans((c - 4 * each) * CH_COLS, CH_COLS, CH_COLS)])

        for i in range(2):

            @pl.when(2 * p + i < SWAPS)
            def _():
                swap.start(2 * p + i)

        summing.tick(p, BOTH_STEPS, REST_LAG)
        return 0

    lax.fori_loop(0, chunks // 2, step, 0)
    summing.drain(chunks // 2, BOTH_STEPS, REST_LAG)
    summing.finish()
    swap.finish()


def rest_summed(normed_flat, dq, dk, dv, mix, gb, small, done, scale, depth):
    width, count = normed_flat.shape
    chunks = (4 * width + small.shape[1]) // CH_COLS
    vm = pl.BlockSpec(memory_space=pltpu.VMEM)
    anywhere = pl.BlockSpec(memory_space=pl.ANY)
    mine, row_len, _ = done.shape
    sources = (mix, gb, normed_flat, dq, dk, dv)
    return pl.pallas_call(
        functools.partial(rest_kernel, depth, scale),
        in_specs=[anywhere] * 6 + [vm, anywhere],
        out_specs=[anywhere] * 2,
        out_shape=[
            jax.ShapeDtypeStruct((CH_ROWS, chunks * CH_COLS), BF),
            jax.ShapeDtypeStruct((mine * SEQ, row_len // SEQ, width), BF),
        ],
        scratch_shapes=[pltpu.VMEM(a.shape, BF) for a in sources]
        + [pltpu.SemaphoreType.DMA((6,)), pltpu.VMEM(Summing.share_shape(chunks, depth), BF)]
        + Exchange.scratch(SWAPS)
        + Summing.sum_scratch(chunks, depth)
        + Summing.give_scratch(chunks, depth, False),
        compiler_params=pltpu.CompilerParams(
            collective_id=2, has_side_effects=True, vmem_limit_bytes=60 << 20),
    )(*sources, small, done)


def reduce_plain(flat, scale):
    share = lax.psum_scatter(flat, ("rows", "seq"), scatter_dimension=0, tiled=True)
    share = (share.astype(F32) * scale).astype(BF)
    return lax.all_gather(share, ("rows", "seq"), axis=0, tiled=True)


def prepare(seg_lengths, mine, row_len):
    seg_count = seg_lengths.shape[1]
    lengths = lax.dynamic_slice_in_dim(seg_lengths, lax.axis_index("seq") * mine, mine, 0)
    seg = segment_ids(lengths, row_len)
    slots = jnp.arange(HALF, dtype=jnp.int32)
    fq = (seg[:, None, :] == slots[None, :, None]).astype(BF)
    fk_half = jnp.where(
        slots < seg_count,
        jnp.where(seg[:, :, None] != slots, NEGATIVE, 0.0),
        jnp.where((slots >= ONES_AT) & (slots < ONES_AT + 3), 1.0, 0.0),
    ).astype(BF)
    fk = jnp.concatenate([fk_half, fk_half], axis=2)
    return fq, fk


def per_device(
    tokens, seg_lengths, w_query, w_key, w_value, w_output, w_inner, w_outer,
    gain_attn, gain_ffn, bucket_bias_table, cotangent,
):
    rows_dev, piece_len, width = tokens.shape
    seq_parts = lax.axis_size("seq")
    row_len = piece_len * seq_parts
    mine = rows_dev // seq_parts
    count = mine * row_len
    gain_one = gain_attn.astype(F32)[None]
    gain_two = gain_ffn.astype(F32)[None]
    depth = lax.axis_size("rows") // 2
    scale = float(rows_dev * lax.axis_size("rows") * row_len) ** (-0.5)
    fused = seq_parts == 4 and CH_ROWS % (4 * depth * 16) == 0 and width == CH_ROWS

    def to_rows(array_in):
        out = lax.all_to_all(array_in, "seq", split_axis=0, concat_axis=1, tiled=True)
        return lax.optimization_barrier(out.reshape(count, width))

    def from_rows(array_in):
        return lax.all_to_all(
            array_in.reshape(mine, row_len, width), "seq", split_axis=1, concat_axis=0, tiled=True
        )

    fq, fk = prepare(seg_lengths, mine, row_len)
    tok = tokens if fused else to_rows(tokens)
    normed, normed_flat, q_rows, k_rows, v_rows, bias, *rows = before(
        tok, gain_one, w_query, w_key, w_value, bucket_bias_table.astype(F32), mine, fused
    )
    if fused:
        tok = rows[0]
    mix, stat, *near = attend(
        q_rows, k_rows, v_rows, fq, fk, bias, row_len, cotangent if fused else None
    )
    dy = near[0].reshape(count, width) if fused else to_rows(cotangent)
    hidden, nt, nt_flat, dy_flat, mix_flat = between(tok, mix, w_output, gain_two, dy)
    if fused:
        result, grad_hidden, branch, sum_two, share, *early = ffn_summed(
            nt, nt_flat, dy, dy_flat, gain_two, w_inner, w_outer, hidden, scale, depth
        )
        gives = (share, depth, early[0].shape[1], result)
    else:
        value, slope = gelu_both(dot(nt, w_inner, 1, 0))
        active = value.astype(BF)
        grad_pre = (dot(dy, w_outer, 1, 1) * slope).astype(BF)
        result = (hidden + dot(active, w_outer, 1, 0)).astype(BF)
        sum_outer, sum_inner = dot(active, dy, 0, 0), dot(grad_pre, nt, 0, 0)
        _, inverse = apply_rms_scaling(hidden, gain_two)
        part, sum_two = norm_back(hidden, inverse, gain_two, dot(grad_pre, w_inner, 1, 1))
        grad_hidden = dy.astype(F32) + part
        branch = grad_hidden.astype(BF)
        gives = None
    dq_flat, dk_rows, dv_rows, table, *given = attend_back(
        q_rows, k_rows, v_rows, w_output, branch, mix, stat, fq, fk, bias, row_len, gives
    )
    grad_input, sum_one = after(
        tok, gain_one, grad_hidden, dq_flat, dk_rows, dv_rows, w_query, w_key, w_value
    )
    sum_table = jnp.sum(table, axis=2).T
    small = jnp.concatenate([sum_one.reshape(-1), sum_two.reshape(-1), sum_table.reshape(-1)])
    if fused:
        small = jnp.pad(small, (0, -small.size % (CH_ROWS * BLK))).reshape(CH_ROWS, BLK)
        small = jnp.pad(small.astype(BF), ((0, 0), (0, 2 * CH_COLS - BLK)))
        total, grad_back = rest_summed(
            normed_flat, dq_flat, dk_rows, dv_rows, mix_flat, branch, small,
            grad_input.reshape(mine, row_len, width), scale, depth,
        )
        out_back = given[2]
        grad_inner = jnp.concatenate([early[0], given[0]], axis=1).astype(F32)
        grad_outer = jnp.concatenate([early[1], given[1]], axis=0).astype(F32)
        squares = [total[:, i * width : (i + 1) * width].astype(F32) for i in range(4)]
        rest = total[:, 4 * width : 4 * width + BLK].astype(F32).reshape(-1)
    else:
        devices = lax.axis_size("rows") * seq_parts
        small = jnp.pad(small, (0, -small.size % (16 * devices * width))).reshape(-1, width)
        parts = (
            dot(mix_flat, branch, 1, 0), dot(normed, dq_flat, 0, 1), dot(normed, dk_rows, 0, 0),
            dot(normed, dv_rows, 0, 0), small, sum_outer, sum_inner,
        )
        total = reduce_plain(jnp.concatenate([g.astype(BF) for g in parts]), scale).astype(F32)
        outs, at = [], 0
        for g in parts:
            outs.append(total[at : at + g.shape[0]])
            at += g.shape[0]
        squares, grad_outer, grad_inner = outs[:4], outs[5], outs[6].T
        rest = outs[4].reshape(-1)
        out_back, grad_back = from_rows(result), from_rows(grad_input)
    return (
        out_back,
        grad_back,
        squares[1],
        squares[2],
        squares[3],
        squares[0],
        grad_inner,
        grad_outer,
        rest[:width],
        rest[width : 2 * width],
        rest[2 * width : 2 * width + sum_table.size].reshape(sum_table.shape),
    )


def solution(mesh):
    tok = P("rows", "seq", None)
    in_specs = (tok, P("rows", None)) + (P(),) * 9 + (tok,)
    out_specs = (tok, tok) + (P(),) * 9
    return jax.shard_map(
        per_device, mesh=mesh, in_specs=in_specs, out_specs=out_specs, check_vma=False
    )
```

```python
import functools
import math

import jax
import jax.numpy as jnp
from jax import lax
from jax.experimental import pallas as pl
from jax.experimental.pallas import tpu as pltpu
from jax.sharding import PartitionSpec as P

EPSILON = 1e-06
THRESHOLDS = (12, 16, 23, 32, 46, 64, 91)
NEGATIVE = -1e30
BUCKETS = 32
GELU_SCALE = math.sqrt(2.0 / math.pi)
GELU_CUBIC = 0.044715
LOG2E = math.log2(math.e)
BLK = 128
QT = 256
HALF = 64
ONES_AT = 8
BF = jnp.bfloat16
F32 = jnp.float32
TOK = 512
TILE_TOK = 256
MESH = pl.DeviceIdType.MESH
CH_ROWS, CH_COLS = 768, 256
SUM_STEPS = ((1,), (2,), (3,), (4,))
GIVE_STEPS = ((5,), (6,), (7,), (8,), (9,))
GIVE_LAG = 3
EARLY = 6
SWAPS = 12
SEQ = 4
SEND_SLOTS = 8
BOTH_STEPS = ((1,), (2,), (3,), (4, 5), (6,), (7,), (8,), (9,))
REST_LAG = 2


def bucket_of(offsets, bucket_count):
    distance = jnp.abs(offsets)
    levels = 8 + sum(((distance >= threshold).astype(jnp.int32) for threshold in THRESHOLDS))
    return jnp.where(offsets > 0, bucket_count // 2, 0) + jnp.where(distance < 8, distance, levels)


def segment_ids(seg_lengths, row_len):
    order = jnp.arange(seg_lengths.shape[1])
    ends = jnp.sum(
        jnp.where(order[None, :, None] <= order[None, None, :], seg_lengths[:, :, None], 0), axis=1
    )
    positions = jnp.arange(row_len, dtype=jnp.int32)
    return jnp.sum((positions[None, :, None] >= ends[:, None, :]).astype(jnp.int32), axis=2)


def gelu_both(x):
    square = x * x
    tangent = jnp.tanh(x * (GELU_SCALE + GELU_SCALE * GELU_CUBIC * square))
    upper = 0.5 * tangent + 0.5
    slope = upper + (0.5 * x) * (1.0 - tangent * tangent) * (
        GELU_SCALE + 3.0 * GELU_SCALE * GELU_CUBIC * square
    )
    return x * upper, slope


def apply_rms_scaling(values_in, gain_row):
    inverse = lax.rsqrt(jnp.mean(values_in * values_in, axis=-1, keepdims=True) + EPSILON)
    return (values_in * inverse * gain_row, inverse)


def norm_back(values_in, inverse, gain_row, grad_normed):
    weighted = grad_normed * gain_row
    inner_mean = jnp.mean(weighted * values_in, axis=-1, keepdims=True)
    grad_values = inverse * weighted - values_in * (inverse * inverse * inverse) * inner_mean
    grad_gain = jnp.sum(grad_normed * values_in * inverse, axis=0)
    return (grad_values, grad_gain)


def dot(a, b, ca, cb):
    return lax.dot_general(a, b, (((ca,), (cb,)), ((), ())), preferred_element_type=F32)


def halves(value, own, other, head):
    lane = lax.broadcasted_iota(jnp.int32, value.shape, 1)
    mine = (lane < HALF) if head == 0 else (lane >= HALF)
    return jnp.where(mine, value, other)


def stack_q(q_pair, features, head):
    scaled = q_pair[head * HALF : (head + 1) * HALF].astype(F32) * LOG2E
    high = scaled.astype(BF)
    low = (scaled - high.astype(F32)).astype(BF)
    zero = jnp.zeros_like(high)
    if head == 0:
        return jnp.concatenate([high, zero, low, features], axis=0)
    return jnp.concatenate([zero, high, features, low], axis=0)


def bias_tile(bias_ref, head, key_block, query_block, number, blocks):
    at = key_block - query_block + blocks - 1
    return jnp.concatenate([bias_ref[head, at - i] for i in range(number)], axis=1)


def attend_kernel(q_ref, k_ref, v_ref, fq_ref, fk_ref, bias_ref, *refs):
    if len(refs) > 2:
        away, mix_ref, stat_ref, near, *sems = refs
        swap = Exchange(away, near, *sems, True)
        now = pl.program_id(0) * pl.num_programs(1) + pl.program_id(1)

        @pl.when(now == 0)
        def _():
            swap.meet()
            swap.start(0)

        @pl.when(now == pl.num_programs(0) * pl.num_programs(1) - 1)
        def _():
            swap.wait(0)
    else:
        mix_ref, stat_ref = refs
    row_len = k_ref.shape[0]
    blocks = row_len // BLK
    keys, vals, features_q, features_k = k_ref[...], v_ref[...], fq_ref[0], fk_ref[0]
    q_pair = q_ref[...].T
    lane = lax.broadcasted_iota(jnp.int32, (row_len, BLK), 1)
    ones = jnp.ones_like(vals)
    queries = [stack_q(q_pair, features_q, h) for h in range(2)]
    keys_all = [jnp.concatenate([keys, halves(keys, None, features_k, h)], axis=1) for h in range(2)]
    values = [halves(vals, None, ones, h) for h in range(2)]
    mixed, stats = [], []
    for h in range(2):
        raw = dot(keys_all[h], queries[h], 1, 0)
        scores = [
            raw[b * BLK : (b + 1) * BLK] + bias_tile(bias_ref, h, b, 0, blocks, blocks)
            for b in range(blocks)
        ]
        top = functools.reduce(jnp.maximum, scores)
        top = jnp.max(top, axis=0, keepdims=True)
        probs = jnp.concatenate([jnp.exp2(s - top).astype(BF) for s in scores], axis=0)
        summed = dot(probs, values[h], 0, 0)
        at = HALF if h == 0 else 0
        total = summed[:, at : at + 1]
        mixed.append(summed * (1.0 / total))
        stats.append(top)
        stats.append(total)
    mix_ref[...] = jnp.where(lane < HALF, mixed[0], mixed[1]).astype(BF)
    totals = jnp.where(lane == 0, stats[1], stats[3]).T
    for h in range(2):
        stat_ref[0, 0, h : h + 1] = stats[2 * h] + jnp.log2(totals[h : h + 1])


def three(row):
    one = row.astype(BF)
    rest = row - one.astype(F32)
    two = rest.astype(BF)
    return one, two, (rest - two.astype(F32)).astype(BF)


def feature_rows(base, row):
    parts = three(row)
    at = lax.broadcasted_iota(jnp.int32, base.shape, 0)
    out = base.astype(F32)
    for i, part in enumerate(parts):
        out = jnp.where(at == ONES_AT + i, part.astype(F32), out)
    return out.astype(BF)


def block_buckets(at, blocks):
    ahead = (at - blocks + 1) * BLK
    low, high = ahead - BLK + 1, ahead + BLK - 1
    if low >= THRESHOLDS[-1] or high <= -THRESHOLDS[-1]:
        return BUCKETS - 1 if low > 0 else BUCKETS // 2 - 1, None, ()
    row = lax.broadcasted_iota(jnp.int32, (BLK, BLK), 0)
    lane = lax.broadcasted_iota(jnp.int32, (BLK, BLK), 1)
    first = BUCKETS // 2 if low > 0 else 0
    last = BUCKETS // 2 if high <= 0 else BUCKETS
    return None, bucket_of(ahead + row - lane, BUCKETS), range(first, last)


def bias_blocks(table_ref, bias_ref):
    heads, number = bias_ref.shape[:2]
    for at in range(number):
        one, bucket, some = block_buckets(at, (number + 1) // 2)

        def head_blocks(h, _):
            if one is not None:
                bias_ref[h, at] = jnp.full((BLK, BLK), table_ref[one, h] * LOG2E, F32)
                return 0
            value = jnp.zeros((BLK, BLK), F32)
            for b in some:
                value = jnp.where(bucket == b, table_ref[b, h] * LOG2E, value)
            bias_ref[h, at] = value
            return 0

        lax.fori_loop(0, heads, head_blocks, 0)


def bucket_sums(acc_ref, head, blocks):
    sums = BUCKETS * [jnp.zeros((1, BLK), F32)]
    for at in range(2 * blocks - 1):
        value = acc_ref[head, at]
        one, bucket, some = block_buckets(at, blocks)
        if one is not None:
            sums[one] = sums[one] + jnp.sum(value, axis=0, keepdims=True)
        for b in some:
            picked = jnp.sum(jnp.where(bucket == b, value, 0.0), axis=0, keepdims=True)
            sums[b] = sums[b] + picked
    return jnp.concatenate(sums, axis=0)


def attend_back_kernel(
    depth, q_ref, k_ref, v_ref, wp_ref, gb_ref, mix_ref, stat_ref, fq_ref, fk_ref, bias_ref, *refs
):
    if depth:
        share, done, dq_ref, dk_ref, dv_ref, table_ref, gi_ref, go_ref, out_ref = refs[:9]
        acc_ref, dk_sum, dv_sum, *sems = refs[9:15]
        swap = Exchange(done, out_ref, *sems, False, SWAPS)
        giving = Summing(
            depth, share, give_refs=refs[15:], targets=(gi_ref, go_ref), turned=True,
            given=(share.shape[0] // 2 - gi_ref.shape[1] // CH_COLS, share.shape[0] // 2),
        )
        now = pl.program_id(0) * pl.num_programs(1) + pl.program_id(1)

        @pl.when(now == 0)
        def _():
            giving.meet()

        @pl.when(now < SWAPS)
        def _():
            swap.start(now)

        giving.tick(now + giving.given[0] + GIVE_LAG, GIVE_STEPS, GIVE_LAG)
    else:
        dq_ref, dk_ref, dv_ref, table_ref, acc_ref, dk_sum, dv_sum = refs
    row_len = k_ref.shape[0]
    blocks = row_len // BLK
    keys, vals, features_k = k_ref[...], v_ref[...], fk_ref[0]
    k_flat = keys.T
    do_pair = dot(wp_ref[...], gb_ref[...], 1, 1).astype(BF)
    q_rows, do_rows = q_ref[...], do_pair.T
    q_pair, mix_pair = q_rows.T, mix_ref[...].T
    zero_rows = jnp.zeros((row_len, BLK), BF)

    @pl.when(pl.program_id(1) == 0)
    def _():
        acc_ref[...] = jnp.zeros_like(acc_ref)

    for head in range(2):
        span = slice(head * HALF, (head + 1) * HALF)
        do_head = do_pair[span]
        delta = jnp.sum(do_head.astype(F32) * mix_pair[span].astype(F32), axis=0, keepdims=True)
        zeros = jnp.zeros((HALF, row_len), BF)
        q_all = stack_q(q_pair, feature_rows(fq_ref[0], -stat_ref[0, 0, head : head + 1]), head)
        k_all = jnp.concatenate([keys, halves(keys, None, features_k, head)], axis=1)
        v_all = halves(vals, None, features_k, head)
        back = feature_rows(zeros, -delta)
        do_all = jnp.concatenate([do_head, back] if head == 0 else [back, do_head], axis=0)
        q_own = halves(q_rows, None, zero_rows, head)
        do_own = halves(do_rows, None, zero_rows, head)
        for tile in range(row_len // QT):
            cut = slice(tile * QT, (tile + 1) * QT)
            raw = dot(k_all, q_all[:, cut], 1, 0)
            grad_probs = dot(v_all, do_all[:, cut], 1, 0)
            probs_list, grads_list = [], []
            sums = {}
            for b in range(blocks):
                part = slice(b * BLK, (b + 1) * BLK)
                probs = jnp.exp2(raw[part] + bias_tile(bias_ref, head, b, tile * (QT // BLK), QT // BLK, blocks))
                grads = probs * grad_probs[part]
                probs_list.append(probs.astype(BF))
                grads_list.append(grads.astype(BF))
                for i in range(QT // BLK):
                    at = b - tile * (QT // BLK) - i + blocks - 1
                    piece = grads[:, i * BLK : (i + 1) * BLK]
                    sums[at] = sums[at] + piece if at in sums else piece
            for at, piece in sums.items():
                acc_ref[head, at] += piece
            probs_low = jnp.concatenate(probs_list, axis=0)
            grads_low = jnp.concatenate(grads_list, axis=0)
            dv_new = dot(probs_low, do_own[cut], 1, 0)
            dk_new = dot(grads_low, q_own[cut], 1, 0)
            if head == 0 and tile == 0:
                dv_sum[...] = dv_new
                dk_sum[...] = dk_new
            else:
                dv_sum[...] += dv_new
                dk_sum[...] += dk_new
            dq_ref[span, cut] = dot(k_flat[span], grads_low, 1, 0).astype(BF)
    dk_ref[...] = dk_sum[...].astype(BF)
    dv_ref[...] = dv_sum[...].astype(BF)

    @pl.when(pl.program_id(1) == pl.num_programs(1) - 1)
    def _():
        for head in range(2):
            table_ref[head] = bucket_sums(acc_ref, head, blocks)

    if depth:
        steps = pl.num_programs(0) * pl.num_programs(1)

        @pl.when(now == steps - 1)
        def _():
            giving.drain(steps + giving.given[0] + GIVE_LAG, GIVE_STEPS, GIVE_LAG)
            giving.finish()
            swap.finish()


def specs(row_len):
    flat = pl.BlockSpec((BLK, row_len), lambda g, r: (g, r))
    rows = pl.BlockSpec((row_len, BLK), lambda g, r: (r, g))
    stat = pl.BlockSpec((1, 1, 2, row_len), lambda g, r: (r, g, 0, 0))
    fq = pl.BlockSpec((1, HALF, row_len), lambda g, r: (r, 0, 0))
    fk = pl.BlockSpec((1, row_len, BLK), lambda g, r: (r, 0, 0))
    blocks = 2 * (row_len // BLK) - 1
    bias = pl.BlockSpec((2, blocks, BLK, BLK), lambda g, r: (g, 0, 0, 0))
    return flat, rows, stat, fq, fk, bias


def attend(q_rows, k_rows, v_rows, fq, fk, bias, row_len, away=None):
    count, width = q_rows.shape
    flat, rows, stat, fqs, fks, biass = specs(row_len)
    pairs, row_count = width // BLK, count // row_len
    anywhere = pl.BlockSpec(memory_space=pl.ANY)
    extra, near, scratch, params = (), [], [], {}
    if away is not None:
        extra, near = (away,), [jax.ShapeDtypeStruct((row_count, row_len, width), BF)]
        scratch, params = Exchange.scratch(), dict(collective_id=5, has_side_effects=True)
    return pl.pallas_call(
        attend_kernel,
        grid=(pairs, row_count),
        in_specs=[rows, rows, rows, fqs, fks, biass] + [anywhere] * len(extra),
        out_specs=[rows, stat] + [anywhere] * len(near),
        out_shape=[
            jax.ShapeDtypeStruct((count, width), BF),
            jax.ShapeDtypeStruct((row_count, pairs, 2, row_len), F32),
        ] + near,
        scratch_shapes=scratch,
        compiler_params=pltpu.CompilerParams(vmem_limit_bytes=48 << 20, **params),
        cost_estimate=pl.CostEstimate(
            flops=4 * 4 * width * count * row_len,
            bytes_accessed=8 * width * count,
            transcendentals=0,
        ),
    )(q_rows, k_rows, v_rows, fq, fk, bias, *extra)


def attend_back(q_rows, k_rows, v_rows, wp, gb, mix, stat_in, fq, fk, bias, row_len, gives):
    count, width = q_rows.shape
    flat, rows, stat, fqs, fks, biass = specs(row_len)
    pairs, row_count = width // BLK, count // row_len
    anywhere = pl.BlockSpec(memory_space=pl.ANY)
    depth, extra, extra_in, extra_out, scratch, params = 0, (), [], [], [], {}
    if gives is not None:
        share, depth, early, done = gives
        shapes = [(width, share.shape[0] // 2 * CH_COLS - early), (share.shape[0] // 2 * CH_COLS - early, width)]
        done = done.reshape(row_count, row_len, width)
        extra, extra_in = (share, done), [pl.BlockSpec(share.shape, lambda g, r: (0, 0, 0)), anywhere]
        extra_out = [jax.ShapeDtypeStruct(shape, BF) for shape in shapes]
        extra_out += [jax.ShapeDtypeStruct((row_count * SEQ, row_len // SEQ, width), BF)]
        scratch = Exchange.scratch(SWAPS) + Summing.give_scratch(share.shape[0], depth, True)
        params = dict(collective_id=3, has_side_effects=True)
    return pl.pallas_call(
        functools.partial(attend_back_kernel, depth),
        grid=(pairs, row_count),
        in_specs=[
            rows, rows, rows, pl.BlockSpec((BLK, width), lambda g, r: (g, 0)),
            pl.BlockSpec((row_len, width), lambda g, r: (r, 0)), rows, stat, fqs, fks, biass,
        ] + extra_in,
        out_specs=[flat, rows, rows, pl.BlockSpec((2, BUCKETS, BLK), lambda g, r: (g, 0, 0))]
        + [anywhere] * len(extra_out),
        out_shape=[
            jax.ShapeDtypeStruct((width, count), BF),
            jax.ShapeDtypeStruct((count, width), BF),
            jax.ShapeDtypeStruct((count, width), BF),
            jax.ShapeDtypeStruct((2 * pairs, BUCKETS, BLK), F32),
        ] + extra_out,
        scratch_shapes=[pltpu.VMEM((2,) + bias.shape[1:], F32)]
        + [pltpu.VMEM((row_len, BLK), F32)] * 2
        + scratch,
        compiler_params=pltpu.CompilerParams(vmem_limit_bytes=48 << 20, **params),
        cost_estimate=pl.CostEstimate(
            flops=10 * 4 * width * count * row_len,
            bytes_accessed=16 * width * count,
            transcendentals=0,
        ),
    )(q_rows, k_rows, v_rows, wp, gb, mix, stat_in, fq, fk, bias, *extra)


class Place:
    def __init__(self):
        self.r, self.s = lax.axis_index("rows"), lax.axis_index("seq")
        self.x, self.z = lax.rem(self.r, 2), self.r // 2
        self.core, self.y = lax.rem(self.s, 2), self.s // 2

    def at(self, x=None, y=None, core=None, z=None):
        x = self.x if x is None else x
        y = self.y if y is None else y
        core = self.core if core is None else core
        z = self.z if z is None else z
        return (z * 2 + x, y * 2 + core)


def spans(base, size, step=16):
    return pl.ds(pl.multiple_of(base, step), size)


class Exchange:
    def __init__(self, src, dst, send, recv, keep, to_rows, parts=1):
        self.src, self.dst, self.send, self.recv, self.keep, self.to_rows = src, dst, send, recv, keep, to_rows
        pieces, rows = (src, dst) if to_rows else (dst, src)
        self.mine, self.piece, self.parts = rows.shape[0], pieces.shape[1], parts
        self.r, self.s = lax.axis_index("rows"), lax.axis_index("seq")

    @staticmethod
    def scratch(parts=1):
        dma = pltpu.SemaphoreType.DMA
        return [dma((parts, SEQ - 1)), dma((parts, SEQ - 1)), dma((parts,))]

    def meet(self):
        barrier = pltpu.get_barrier_semaphore()
        for k in range(1, SEQ):
            place = (self.r, lax.rem(self.s + k, SEQ))
            pl.semaphore_signal(barrier, inc=1, device_id=place, device_id_type=MESH)
        pl.semaphore_wait(barrier, SEQ - 1)

    def ends(self, part, peer):
        if self.parts <= self.mine:
            size, long = self.mine // self.parts, self.piece
            row, at = part * size, 0
        else:
            cuts = self.parts // self.mine
            size, long = 1, self.piece // cuts
            row, at = part // cuts, lax.rem(part, cuts) * long
        if self.to_rows:
            return (self.src.at[pl.ds(peer * self.mine + row, size), spans(at, long)],
                    self.dst.at[pl.ds(row, size), spans(self.s * self.piece + at, long)])
        return (self.src.at[pl.ds(row, size), spans(peer * self.piece + at, long)],
                self.dst.at[pl.ds(self.s * self.mine + row, size), spans(at, long)])

    def copies(self, part):
        out = []
        for k in range(1, SEQ):
            peer = lax.rem(self.s + k, SEQ)
            src, dst = self.ends(part, peer)
            out.append(pltpu.make_async_remote_copy(
                src_ref=src, dst_ref=dst, send_sem=self.send.at[part, k - 1],
                recv_sem=self.recv.at[part, SEQ - 1 - k], device_id=(self.r, peer), device_id_type=MESH))
        src, dst = self.ends(part, self.s)
        return out, pltpu.make_async_copy(src, dst, self.keep.at[part])

    def start(self, part):
        away, here = self.copies(part)
        for d in away:
            d.start()
        here.start()

    def wait(self, part):
        away, here = self.copies(part)
        for d in away:
            d.wait()
        here.wait()

    def finish(self):
        def one(part, _):
            self.wait(part)
            return 0

        lax.fori_loop(0, self.parts, one, 0)


class Summing:
    def __init__(self, depth, share, sum_refs=None, give_refs=None, scale=1.0, targets=None, turned=False, mixed=True, given=None):
        if sum_refs is not None:
            (self.snd, self.got, self.own, self.got_one, self.got_two, self.got_z,
             self.send_sum, self.recv_sum, self.send_sum_z, self.recv_sum_z) = sum_refs
        if give_refs is not None:
            (self.gath, self.flip, self.sems,
             self.send_give, self.recv_give, self.send_give_z, self.recv_give_z) = give_refs
        self.summed = (0, share.shape[0] // 2)
        self.given = self.summed if given is None else given
        self.share, self.chunks, self.targets, self.turned = share, share.shape[0], targets, turned
        self.depth, self.scale, self.mixed = depth, scale, mixed
        self.me = Place()
        self.w = CH_COLS // 2
        self.half, self.quarter = CH_ROWS // 2, CH_ROWS // 4
        self.piece = CH_ROWS // (4 * depth)

    @staticmethod
    def sum_scratch(chunks, depth):
        w, piece = CH_COLS // 2, CH_ROWS // (4 * depth)
        dma = pltpu.SemaphoreType.DMA
        return [
            pltpu.VMEM((SEND_SLOTS, CH_ROWS, w), BF),
            pltpu.VMEM((chunks, CH_ROWS, w), BF),
            pltpu.VMEM((chunks, CH_ROWS, w), BF),
            pltpu.VMEM((chunks, CH_ROWS // 2, w), BF),
            pltpu.VMEM((chunks, CH_ROWS // 4, w), BF),
            pltpu.VMEM((chunks, depth - 1, piece, w), BF),
            dma((3, chunks)), dma((3, chunks)),
            dma((chunks, depth - 1)), dma((chunks, depth - 1)),
        ]

    @staticmethod
    def give_scratch(chunks, depth, turned):
        dma = pltpu.SemaphoreType.DMA
        return [
            pltpu.VMEM((chunks, 2, CH_ROWS, CH_COLS // 2), BF),
            pltpu.VMEM((2, CH_COLS, CH_ROWS) if turned else (1, 16, 128), BF),
            dma((2, chunks)),
            dma((3, chunks)), dma((3, chunks)),
            dma((chunks, depth - 1)), dma((chunks, depth - 1)),
        ]

    @staticmethod
    def share_shape(chunks, depth):
        return (chunks, CH_ROWS // (4 * depth), CH_COLS // 2)

    def meet(self):
        me = self.me
        barrier = pltpu.get_barrier_semaphore()
        others = [me.at(x=1 - me.x)] + [(me.r, lax.rem(me.s + k, SEQ)) for k in range(1, SEQ)]
        others += [me.at(z=lax.rem(me.z + k, self.depth)) for k in range(1, self.depth)]
        for place in others:
            pl.semaphore_signal(barrier, inc=1, device_id=place, device_id_type=MESH)
        pl.semaphore_wait(barrier, len(others))

    def copy(self, src, dst, stage, c, place):
        if stage < 3:
            send, recv = self.send_sum.at[stage, c], self.recv_sum.at[stage, c]
        else:
            send, recv = self.send_give.at[stage - 3, c], self.recv_give.at[stage - 3, c]
        return pltpu.make_async_remote_copy(
            src_ref=src, dst_ref=dst, send_sem=send, recv_sem=recv, device_id=place, device_id_type=MESH)

    def part(self, c, start, size):
        return self.gath.at[c, self.me.core, spans(start, size)]

    def order(self, c):
        me, odd = self.me, lax.rem(c, 2) if self.mixed else 0
        one = me.x + odd * (me.y - me.x)
        two = me.y + odd * (me.x - me.y)
        x_there, y_there = 1 - 2 * me.x, 2 - 4 * me.y
        first = (me.r + (1 - odd) * x_there, me.s + odd * y_there)
        second = (me.r + odd * x_there, me.s + (1 - odd) * y_there)
        return one, two, first, second

    def put(self, c, value):
        left, right = value[:, : self.w].astype(BF), value[:, self.w :].astype(BF)
        first = self.me.core == 0
        self.own[c] = jnp.where(first, left, right)
        self.snd[lax.rem(c, SEND_SLOTS)] = jnp.where(first, right, left)
        self.step_core(c).start()

    def step_core(self, c):
        return self.copy(self.snd.at[lax.rem(c, SEND_SLOTS)], self.got.at[c], 0, c, self.me.at(core=1 - self.me.core))

    def step_one(self, c):
        one, _, place, _ = self.order(c)
        return self.copy(self.own.at[c, spans((1 - one) * self.half, self.half)], self.got_one.at[c], 1, c, place)

    def step_two(self, c):
        one, two, _, place = self.order(c)
        part = spans(one * self.half + (1 - two) * self.quarter, self.quarter)
        return self.copy(self.own.at[c, part], self.got_two.at[c], 2, c, place)

    def base(self, c):
        one, two, _, _ = self.order(c)
        return one * self.half + two * self.quarter

    def step_z(self, c, k):
        to = lax.rem(self.me.z + k, self.depth)
        return pltpu.make_async_remote_copy(
            src_ref=self.own.at[c, spans(self.base(c) + to * self.piece, self.piece)],
            dst_ref=self.got_z.at[c, self.depth - 1 - k],
            send_sem=self.send_sum_z.at[c, k - 1], recv_sem=self.recv_sum_z.at[c, self.depth - 1 - k],
            device_id=self.me.at(z=to), device_id_type=MESH)

    def mine(self, c):
        return self.part(c, self.base(c) + self.me.z * self.piece, self.piece)

    def give_z(self, c, k):
        return pltpu.make_async_remote_copy(
            src_ref=self.mine(c), dst_ref=self.mine(c),
            send_sem=self.send_give_z.at[c, k - 1], recv_sem=self.recv_give_z.at[c, self.depth - 1 - k],
            device_id=self.me.at(z=lax.rem(self.me.z + k, self.depth)), device_id_type=MESH)

    def give_two(self, c):
        part = self.part(c, self.base(c), self.quarter)
        return self.copy(part, part, 3, c, self.order(c)[3])

    def give_one(self, c):
        one, _, place, _ = self.order(c)
        part = self.part(c, one * self.half, self.half)
        return self.copy(part, part, 4, c, place)

    def give_core(self, c):
        part = self.part(c, 0, CH_ROWS)
        return self.copy(part, part, 5, c, self.me.at(core=1 - self.me.core))

    def leave(self, c, kind):
        if len(self.targets) == 1:
            array, at = self.targets[0], c * CH_COLS
        else:
            array, at = self.targets[kind], (c // 2 - self.given[0]) * CH_COLS
        if self.turned and kind == 1:
            flip = self.flip.at[lax.rem(c // 2, 2)]
            return [pltpu.make_async_copy(flip, array.at[spans(at, CH_COLS, CH_COLS)], self.sems.at[0, c])]
        return [
            pltpu.make_async_copy(
                self.gath.at[c, i], array.at[:, spans(at + i * self.w, self.w, 128)], self.sems.at[i, c])
            for i in range(2)
        ]

    def add(self, c, start, size, from_ref):
        part = spans(start, size)
        self.own[c, part] = (self.own[c, part].astype(F32) + from_ref[c].astype(F32)).astype(BF)

    def run(self, stage, c, kind):
        depth = self.depth
        if stage == 1:
            self.step_core(c).wait()
            self.add(c, 0, CH_ROWS, self.got)
            self.step_one(c).start()
        if stage == 2:
            self.step_one(c).wait_recv()
            self.add(c, self.order(c)[0] * self.half, self.half, self.got_one)
            self.step_two(c).start()
        if stage == 3:
            self.step_two(c).wait_recv()
            self.add(c, self.base(c), self.quarter, self.got_two)
            for k in range(1, depth):
                self.step_z(c, k).start()
        if stage == 4:
            for k in range(1, depth):
                self.step_z(c, k).wait_recv()
            total = self.own[c, spans(self.base(c) + self.me.z * self.piece, self.piece)].astype(F32)
            for k in range(depth - 1):
                total = total + self.got_z[c, k].astype(F32)
            self.share[c] = (total * self.scale).astype(BF)
            for d in (self.step_one(c), self.step_two(c)):
                d.wait_send()
            for k in range(1, depth):
                self.step_z(c, k).wait_send()
        if stage == 5:
            self.gath[c, self.me.core, spans(self.base(c) + self.me.z * self.piece, self.piece)] = self.share[c]
            for k in range(1, depth):
                self.give_z(c, k).start()
        if stage == 6:
            for k in range(1, depth):
                self.give_z(c, k).wait_recv()
            self.give_two(c).start()
        if stage == 7:
            self.give_two(c).wait_recv()
            self.give_one(c).start()
        if stage == 8:
            self.give_one(c).wait_recv()
            self.give_core(c).start()
        if stage == 9:
            self.give_core(c).wait_recv()
            if self.turned and kind == 1:

                @pl.when(c // 2 >= self.given[0] + 2)
                def _():
                    for d in self.leave(c - 4, kind):
                        d.wait()

                slot = lax.rem(c // 2, 2)
                for i in range(2):
                    self.flip[slot, i * self.w : (i + 1) * self.w] = self.gath[c, i].T
            for d in self.leave(c, kind):
                d.start()
            for d in (self.give_two, self.give_one, self.give_core):
                d(c).wait_send()
            for k in range(1, depth):
                self.give_z(c, k).wait_send()

    def tick(self, t, steps, lag):
        for at in range(len(steps), 0, -1):
            p = t - at * lag
            for stage in steps[at - 1]:
                low, high = self.summed if stage < 5 else self.given

                @pl.when((p >= low) & (p < high))
                def _():
                    for kind in range(2):
                        self.run(stage, 2 * p + kind, kind)

    def drain(self, start, steps, lag):
        def one(t, _):
            self.tick(t, steps, lag)
            return 0

        last = 0
        for at in range(len(steps), 0, -1):
            for stage in steps[at - 1]:
                last = max(last, (self.summed if stage < 5 else self.given)[1] + at * lag)
        lax.fori_loop(start, last, one, 0)

    def finish(self):
        def one(c, kind):
            for d in self.leave(c, kind):
                d.wait()

        def pair(p, _):
            one(2 * p, 0)
            if not self.turned:
                one(2 * p + 1, 1)
            return 0

        low, high = self.given
        lax.fori_loop(low, high, pair, 0)
        if self.turned:
            for p in range(max(low, high - 2), high):
                one(2 * p + 1, 1)


def before_kernel(
    fused, tok, gain, wq, wk, wv, table, normed_ref, flat_ref, q_ref, k_ref, v_ref, bias_ref, *refs
):
    if fused:
        tok_ref, rows, *sems = refs
        swap = Exchange(tok, rows, *sems, True, rows.shape[0])
        m = pl.program_id(0)

        @pl.when(m == 0)
        def _():
            swap.meet()
            for part in range(rows.shape[0]):
                swap.start(part)

    @pl.when(pl.program_id(0) == 0)
    def _():
        bias_blocks(table, bias_ref)

    if fused:
        swap.wait(m)
        own = rows[m]
        tok_ref[...] = own
        wide = own.astype(F32)
    else:
        wide = tok[...].astype(F32)
    normed = apply_rms_scaling(wide, gain[...])[0].astype(BF)
    normed_ref[...] = normed
    flat_ref[...] = normed.T
    q_ref[...] = dot(normed, wq[...], 1, 0).astype(BF)
    k_ref[...] = dot(normed, wk[...], 1, 0).astype(BF)
    v_ref[...] = dot(normed, wv[...], 1, 0).astype(BF)


def tall(width):
    return pl.BlockSpec((TOK, width), lambda m: (m, 0))


def broad(width):
    return pl.BlockSpec((width, TOK), lambda m: (0, m))


def whole(array):
    return pl.BlockSpec(array.shape, lambda m: (0,) * array.ndim)


def plain_call(kernel, count, ins, in_specs, outs, out_specs, flops, scratch=(), collective_id=None):
    params = {} if collective_id is None else dict(collective_id=collective_id, has_side_effects=True)
    return pl.pallas_call(
        kernel,
        grid=(count // TOK,),
        in_specs=in_specs,
        out_specs=out_specs,
        out_shape=[jax.ShapeDtypeStruct(shape, kind) for shape, kind in outs],
        scratch_shapes=list(scratch),
        compiler_params=pltpu.CompilerParams(vmem_limit_bytes=48 << 20, **params),
        cost_estimate=pl.CostEstimate(flops=flops, bytes_accessed=16 << 20, transcendentals=0),
    )(*ins)


def before(tok, gain, wq, wk, wv, table, mine, fused):
    width = tok.shape[-1]
    count = tok.size // width
    t, f = tall(width), broad(width)
    spec, more, scratch = t, [], []
    bias = (table.shape[1], 2 * (count // mine // BLK) - 1, BLK, BLK)
    if fused:
        spec = pl.BlockSpec(memory_space=pl.ANY)
        more = [((count, width), BF)]
        scratch = [pltpu.VMEM((mine, count // mine, width), BF)] + Exchange.scratch(mine)
    return plain_call(
        functools.partial(before_kernel, fused), count, (tok, gain, wq, wk, wv, table),
        [spec] + [whole(a) for a in (gain, wq, wk, wv)] + [pl.BlockSpec(memory_space=pltpu.SMEM)],
        [((count, width), BF), ((width, count), BF)] + [((count, width), BF)] * 3
        + [(bias, F32)] + more,
        [t, f, t, t, t] + [pl.BlockSpec(bias, lambda m: (0, 0, 0, 0))] + [t] * len(more), 6 * count * width * width, scratch, 4 if fused else None,
    )


def between_kernel(tok, mix, wo, gain, dy, hidden_ref, nt_ref, nt_flat_ref, dy_flat_ref, mix_flat_ref):
    hidden = tok[...].astype(F32) + dot(mix[...], wo[...], 1, 0)
    hidden_ref[...] = hidden
    normed = apply_rms_scaling(hidden, gain[...])[0].astype(BF)
    nt_ref[...] = normed
    nt_flat_ref[...] = normed.T
    dy_flat_ref[...] = dy[...].T
    mix_flat_ref[...] = mix[...].T


def between(tok, mix, wo, gain, dy):
    count, width = tok.shape
    t, f = tall(width), broad(width)
    return plain_call(
        between_kernel, count, (tok, mix, wo, gain, dy), [t, t, whole(wo), whole(gain), t],
        [((count, width), F32), ((count, width), BF)] + [((width, count), BF)] * 3,
        [t, t, f, f, f], 2 * count * width * width,
    )


def after_kernel(tok, gain, gh, dq, dk, dv, wq, wk, wv, grad_ref, gain_ref):
    wide = tok[...].astype(F32)
    _, inverse = apply_rms_scaling(wide, gain[...])
    grad_normed = (
        dot(dq[...].T, wq[...], 1, 1) + dot(dk[...], wk[...], 1, 1) + dot(dv[...], wv[...], 1, 1)
    )
    part, grad_gain = norm_back(wide, inverse, gain[...], grad_normed)
    grad_ref[...] = (gh[...] + part).astype(BF)

    @pl.when(pl.program_id(0) == 0)
    def _():
        gain_ref[...] = jnp.zeros_like(gain_ref)

    gain_ref[...] += grad_gain[None]


def after(tok, gain, gh, dq, dk, dv, wq, wk, wv):
    count, width = tok.shape
    t, f = tall(width), broad(width)
    return plain_call(
        after_kernel, count, (tok, gain, gh, dq, dk, dv, wq, wk, wv),
        [t, whole(gain), t, f, t, t, whole(wq), whole(wk), whole(wv)],
        [((count, width), BF), ((1, width), F32)], [t, whole(gain)], 6 * count * width * width,
    )


def ffn_kernel(depth, scale, nt, nt_flat, dy, dy_flat, gain, wi_hbm, wo_hbm, hidden_hbm,
               res_hbm, gh_hbm, gb_hbm, gain_ref, share, gi_ref, go_ref,
               out_acc, gnt_acc, wi_buf, wo_buf, act, gp, hid, res_buf, gb_buf, w_sem, h_sem, *refs):
    count, width = nt.shape
    tile = 2 * CH_COLS
    tiles = wi_hbm.shape[1] // tile
    parts = count // TOK
    given = gi_ref.shape[1] // CH_COLS
    summing = Summing(
        depth, share, refs[:10], refs[10:], scale, targets=(gi_ref, go_ref), turned=True, given=(0, given)
    )

    def weights(j):
        cut, slot = spans(j * tile, tile, tile), lax.rem(j, 2)
        return (
            pltpu.make_async_copy(wi_hbm.at[:, cut], wi_buf.at[slot], w_sem.at[0, slot]),
            pltpu.make_async_copy(wo_hbm.at[cut], wo_buf.at[slot], w_sem.at[1, slot]),
        )

    def hidden(m):
        return pltpu.make_async_copy(hidden_hbm.at[pl.ds(m * TOK, TOK)], hid, h_sem.at[0])

    for w in weights(0):
        w.start()
    hidden(0).start()
    out_acc[...] = jnp.zeros_like(out_acc)
    gnt_acc[...] = jnp.zeros_like(gnt_acc)
    summing.meet()

    def step(j, _):
        for w in weights(j):
            w.wait()

        @pl.when(j + 1 < tiles)
        def _():
            for w in weights(j + 1):
                w.start()

        slot = lax.rem(j, 2)
        wi, wo = wi_buf.at[slot], wo_buf.at[slot]
        for m in range(count // TILE_TOK):
            part = slice(m * TILE_TOK, (m + 1) * TILE_TOK)
            pre = dot(nt[part], wi[...], 1, 0)
            grad_active = dot(dy[part], wo[...], 1, 1)
            value, slope = gelu_both(pre)
            act[part] = value.astype(BF)
            gp[part] = (grad_active * slope).astype(BF)
        for h in range(2):
            cut = slice(h * CH_COLS, (h + 1) * CH_COLS)
            summing.put(4 * j + 2 * h, dot(nt_flat[...], gp[:, cut], 1, 0))
            summing.put(4 * j + 2 * h + 1, dot(dy_flat[...], act[:, cut], 1, 0))
            if h == 0:
                summing.tick(2 * j, BOTH_STEPS, 1)
        for m in range(count // TILE_TOK):
            part = slice(m * TILE_TOK, (m + 1) * TILE_TOK)
            out_acc[part] += dot(act[part], wo[...], 1, 0)
            gnt_acc[part] += dot(gp[part], wi[...], 1, 1)
        summing.tick(2 * j + 1, BOTH_STEPS, 1)
        return 0

    lax.fori_loop(0, tiles, step, 0)

    def outputs(m):
        rows = pl.ds(m * TOK, TOK)
        return (
            pltpu.make_async_copy(res_buf.at[m % 2], res_hbm.at[rows], h_sem.at[1 + m % 2]),
            pltpu.make_async_copy(gb_buf.at[m % 2], gb_hbm.at[rows], h_sem.at[3 + m % 2]),
            pltpu.make_async_copy(gnt_acc.at[rows], gh_hbm.at[rows], h_sem.at[5 + m % 2]),
        )

    total_gain = jnp.zeros((1, width), F32)
    gain_row = gain[...]
    for m in range(parts):
        summing.tick(2 * tiles + m, BOTH_STEPS, 1)
        rows = slice(m * TOK, (m + 1) * TOK)
        hidden(m).wait()
        if m >= 2:
            for d in outputs(m - 2):
                d.wait()
        value = hid[...]
        res_buf[m % 2] = (value + out_acc[rows]).astype(BF)
        _, inverse = apply_rms_scaling(value, gain_row)
        part, grad_gain = norm_back(value, inverse, gain_row, gnt_acc[rows])
        total_gain = total_gain + grad_gain[None]
        grad_hidden = dy[rows].astype(F32) + part
        gnt_acc[rows] = grad_hidden
        gb_buf[m % 2] = grad_hidden.astype(BF)
        if m + 1 < parts:
            hidden(m + 1).start()
        for d in outputs(m):
            d.start()
    gain_ref[...] = total_gain
    summing.drain(2 * tiles + parts, BOTH_STEPS, 1)
    summing.finish()
    for m in range(max(0, parts - 2), parts):
        for d in outputs(m):
            d.wait()


def ffn_summed(nt, nt_flat, dy, dy_flat, gain, w_inner, w_outer, hidden, scale, depth):
    count, width = nt.shape
    ff = w_inner.shape[1]
    chunks = 2 * ff // CH_COLS
    tile = 2 * CH_COLS
    vm = pl.BlockSpec(memory_space=pltpu.VMEM)
    anywhere = pl.BlockSpec(memory_space=pl.ANY)
    return pl.pallas_call(
        functools.partial(ffn_kernel, depth, scale),
        in_specs=[vm] * 5 + [anywhere] * 3,
        out_specs=[anywhere] * 3 + [vm] * 2 + [anywhere] * 2,
        out_shape=[
            jax.ShapeDtypeStruct((count, width), BF),
            jax.ShapeDtypeStruct((count, width), F32),
            jax.ShapeDtypeStruct((count, width), BF),
            jax.ShapeDtypeStruct((1, width), F32),
            jax.ShapeDtypeStruct(Summing.share_shape(chunks, depth), BF),
            jax.ShapeDtypeStruct((width, EARLY * CH_COLS), BF),
            jax.ShapeDtypeStruct((EARLY * CH_COLS, width), BF),
        ],
        scratch_shapes=[
            pltpu.VMEM((count, width), F32),
            pltpu.VMEM((count, width), F32),
            pltpu.VMEM((2, width, tile), BF),
            pltpu.VMEM((2, tile, width), BF),
            pltpu.VMEM((count, tile), BF),
            pltpu.VMEM((count, tile), BF),
            pltpu.VMEM((TOK, width), F32),
            pltpu.VMEM((2, TOK, width), BF),
            pltpu.VMEM((2, TOK, width), BF),
            pltpu.SemaphoreType.DMA((2, 2)),
            pltpu.SemaphoreType.DMA((7,)),
        ] + Summing.sum_scratch(chunks, depth) + Summing.give_scratch(2 * EARLY, depth, True),
        compiler_params=pltpu.CompilerParams(
            collective_id=1, has_side_effects=True, vmem_limit_bytes=62 << 20),
        cost_estimate=pl.CostEstimate(
            flops=12 * count * width * ff, bytes_accessed=40 << 20, transcendentals=0),
    )(nt, nt_flat, dy, dy_flat, gain, w_inner, w_outer, hidden)


def rest_kernel(depth, scale, *refs):
    sources, (small, gain, out, out_ref) = refs[:11], refs[11:15]
    mix, gb, normed_flat, dq, dk, dv, tok, gh, wq, wk, wv = held = refs[15:26]
    done, gain_sum, load_sem, share, *refs = refs[26:]
    width = normed_flat.shape[0]
    each = width // CH_COLS
    chunks = share.shape[0]
    loads = [pltpu.make_async_copy(a, b, load_sem.at[i]) for i, (a, b) in enumerate(zip(sources, held))]
    gain_sum[...] = jnp.zeros_like(gain_sum)
    for d in loads:
        d.start()
    swap = Exchange(done, out_ref, *refs[:3], False, SWAPS)
    summing = Summing(depth, share, refs[3:13], refs[13:], scale, targets=(out,), mixed=False)
    summing.meet()

    def terms(which, cut):
        if which == 0:
            return dot(mix[...], gb[:, cut], 1, 0)
        if which == 1:
            return dot(normed_flat[...], dq[cut], 1, 1)
        return dot(normed_flat[...], (dk if which == 2 else dv)[:, cut], 1, 0)

    def tokens_back(m):
        rows = spans(m * TOK, TOK, TOK)
        wide = tok[rows].astype(F32)
        _, inverse = apply_rms_scaling(wide, gain[...])
        grad_normed = (
            dot(dq[:, rows].T, wq[...], 1, 1) + dot(dk[rows], wk[...], 1, 1) + dot(dv[rows], wv[...], 1, 1)
        )
        part, grad_gain = norm_back(wide, inverse, gain[...], grad_normed)
        done[m] = (gh[rows] + part).astype(BF)
        gain_sum[...] += grad_gain[None]
        each_row = SWAPS // done.shape[0]
        for i in range(each_row):
            swap.start(m * each_row + i)

    def step(p, _):
        @pl.when(p == 0)
        def _():
            for d in loads[:2]:
                d.wait()

        @pl.when(p == 1)
        def _():
            for d in loads[2:]:
                d.wait()

        for kind in range(2):
            c = 2 * p + kind
            for which in range(4):

                @pl.when(c // each == which)
                def _():
                    cut = spans((c - which * each) * CH_COLS, CH_COLS, CH_COLS)
                    summing.put(c, terms(which, cut))

            @pl.when(c >= 4 * each)
            def _():
                value = small[:, spans((c - 4 * each) * CH_COLS, CH_COLS, CH_COLS)]
                lines = width // BLK
                first = [gain_sum[:, i * BLK : (i + 1) * BLK] for i in range(lines)]
                first.append(jnp.zeros((CH_ROWS - lines, BLK), F32))
                first = jnp.concatenate([jnp.concatenate(first, axis=0), jnp.zeros((CH_ROWS, BLK), F32)], axis=1)
                summing.put(c, value.astype(F32) + jnp.where(c == 4 * each, first, 0.0))

        summing.tick(p, BOTH_STEPS, REST_LAG)

        @pl.when((p >= 1) & (p <= done.shape[0]))
        def _():
            tokens_back(p - 1)

        return 0

    lax.fori_loop(0, chunks // 2, step, 0)
    summing.drain(chunks // 2, BOTH_STEPS, REST_LAG)
    summing.finish()
    swap.finish()


def rest_summed(normed_flat, dq, dk, dv, mix, gb, tok, gh, wq, wk, wv, gain, small, mine, scale, depth):
    width, count = normed_flat.shape
    chunks = (4 * width + small.shape[1]) // CH_COLS
    vm = pl.BlockSpec(memory_space=pltpu.VMEM)
    anywhere = pl.BlockSpec(memory_space=pl.ANY)
    row_len = count // mine
    sources = (mix, gb, normed_flat, dq, dk, dv, tok, gh, wq, wk, wv)
    return pl.pallas_call(
        functools.partial(rest_kernel, depth, scale),
        in_specs=[anywhere] * len(sources) + [vm, vm],
        out_specs=[anywhere] * 2,
        out_shape=[
            jax.ShapeDtypeStruct((CH_ROWS, chunks * CH_COLS), BF),
            jax.ShapeDtypeStruct((mine * SEQ, row_len // SEQ, width), BF),
        ],
        scratch_shapes=[pltpu.VMEM(a.shape, a.dtype) for a in sources]
        + [pltpu.VMEM((mine, row_len, width), BF), pltpu.VMEM((1, width), F32)]
        + [pltpu.SemaphoreType.DMA((len(sources),)), pltpu.VMEM(Summing.share_shape(chunks, depth), BF)]
        + Exchange.scratch(SWAPS)
        + Summing.sum_scratch(chunks, depth)
        + Summing.give_scratch(chunks, depth, False),
        compiler_params=pltpu.CompilerParams(
            collective_id=2, has_side_effects=True, vmem_limit_bytes=60 << 20),
    )(*sources, small, gain)


def reduce_plain(flat, scale):
    share = lax.psum_scatter(flat, ("rows", "seq"), scatter_dimension=0, tiled=True)
    share = (share.astype(F32) * scale).astype(BF)
    return lax.all_gather(share, ("rows", "seq"), axis=0, tiled=True)


def prepare(seg_lengths, mine, row_len):
    seg_count = seg_lengths.shape[1]
    lengths = lax.dynamic_slice_in_dim(seg_lengths, lax.axis_index("seq") * mine, mine, 0)
    seg = segment_ids(lengths, row_len)
    slots = jnp.arange(HALF, dtype=jnp.int32)
    fq = (seg[:, None, :] == slots[None, :, None]).astype(BF)
    fk_half = jnp.where(
        slots < seg_count,
        jnp.where(seg[:, :, None] != slots, NEGATIVE, 0.0),
        jnp.where((slots >= ONES_AT) & (slots < ONES_AT + 3), 1.0, 0.0),
    ).astype(BF)
    fk = jnp.concatenate([fk_half, fk_half], axis=2)
    return fq, fk


def per_device(
    tokens, seg_lengths, w_query, w_key, w_value, w_output, w_inner, w_outer,
    gain_attn, gain_ffn, bucket_bias_table, cotangent,
):
    rows_dev, piece_len, width = tokens.shape
    seq_parts = lax.axis_size("seq")
    row_len = piece_len * seq_parts
    mine = rows_dev // seq_parts
    count = mine * row_len
    gain_one = gain_attn.astype(F32)[None]
    gain_two = gain_ffn.astype(F32)[None]
    depth = lax.axis_size("rows") // 2
    scale = float(rows_dev * lax.axis_size("rows") * row_len) ** (-0.5)
    fused = seq_parts == 4 and CH_ROWS % (4 * depth * 16) == 0 and width == CH_ROWS

    def to_rows(array_in):
        out = lax.all_to_all(array_in, "seq", split_axis=0, concat_axis=1, tiled=True)
        return lax.optimization_barrier(out.reshape(count, width))

    def from_rows(array_in):
        return lax.all_to_all(
            array_in.reshape(mine, row_len, width), "seq", split_axis=1, concat_axis=0, tiled=True
        )

    fq, fk = prepare(seg_lengths, mine, row_len)
    tok = tokens if fused else to_rows(tokens)
    normed, normed_flat, q_rows, k_rows, v_rows, bias, *rows = before(
        tok, gain_one, w_query, w_key, w_value, bucket_bias_table.astype(F32), mine, fused
    )
    if fused:
        tok = rows[0]
    mix, stat, *near = attend(
        q_rows, k_rows, v_rows, fq, fk, bias, row_len, cotangent if fused else None
    )
    dy = near[0].reshape(count, width) if fused else to_rows(cotangent)
    hidden, nt, nt_flat, dy_flat, mix_flat = between(tok, mix, w_output, gain_two, dy)
    if fused:
        result, grad_hidden, branch, sum_two, share, *early = ffn_summed(
            nt, nt_flat, dy, dy_flat, gain_two, w_inner, w_outer, hidden, scale, depth
        )
        gives = (share, depth, early[0].shape[1], result)
    else:
        value, slope = gelu_both(dot(nt, w_inner, 1, 0))
        active = value.astype(BF)
        grad_pre = (dot(dy, w_outer, 1, 1) * slope).astype(BF)
        result = (hidden + dot(active, w_outer, 1, 0)).astype(BF)
        sum_outer, sum_inner = dot(active, dy, 0, 0), dot(grad_pre, nt, 0, 0)
        _, inverse = apply_rms_scaling(hidden, gain_two)
        part, sum_two = norm_back(hidden, inverse, gain_two, dot(grad_pre, w_inner, 1, 1))
        grad_hidden = dy.astype(F32) + part
        branch = grad_hidden.astype(BF)
        gives = None
    dq_flat, dk_rows, dv_rows, table, *given = attend_back(
        q_rows, k_rows, v_rows, w_output, branch, mix, stat, fq, fk, bias, row_len, gives
    )
    if fused:
        sum_one = jnp.zeros((1, width), F32)
    else:
        grad_input, sum_one = after(
            tok, gain_one, grad_hidden, dq_flat, dk_rows, dv_rows, w_query, w_key, w_value
        )
    sum_table = jnp.sum(table, axis=2).T
    small = jnp.concatenate([sum_one.reshape(-1), sum_two.reshape(-1), sum_table.reshape(-1)])
    if fused:
        small = jnp.pad(small, (0, -small.size % (CH_ROWS * BLK))).reshape(CH_ROWS, BLK)
        small = jnp.pad(small.astype(BF), ((0, 0), (0, 2 * CH_COLS - BLK)))
        total, grad_back = rest_summed(
            normed_flat, dq_flat, dk_rows, dv_rows, mix_flat, branch, tok, grad_hidden,
            w_query, w_key, w_value, gain_one, small, mine, scale, depth,
        )
        out_back = given[2]
        grad_inner = jnp.concatenate([early[0], given[0]], axis=1).astype(F32)
        grad_outer = jnp.concatenate([early[1], given[1]], axis=0).astype(F32)
        squares = [total[:, i * width : (i + 1) * width].astype(F32) for i in range(4)]
        rest = total[:, 4 * width : 4 * width + BLK].astype(F32).reshape(-1)
    else:
        devices = lax.axis_size("rows") * seq_parts
        small = jnp.pad(small, (0, -small.size % (16 * devices * width))).reshape(-1, width)
        parts = (
            dot(mix_flat, branch, 1, 0), dot(normed, dq_flat, 0, 1), dot(normed, dk_rows, 0, 0),
            dot(normed, dv_rows, 0, 0), small, sum_outer, sum_inner,
        )
        total = reduce_plain(jnp.concatenate([g.astype(BF) for g in parts]), scale).astype(F32)
        outs, at = [], 0
        for g in parts:
            outs.append(total[at : at + g.shape[0]])
            at += g.shape[0]
        squares, grad_outer, grad_inner = outs[:4], outs[5], outs[6].T
        rest = outs[4].reshape(-1)
        out_back, grad_back = from_rows(result), from_rows(grad_input)
    return (
        out_back,
        grad_back,
        squares[1],
        squares[2],
        squares[3],
        squares[0],
        grad_inner,
        grad_outer,
        rest[:width],
        rest[width : 2 * width],
        rest[2 * width : 2 * width + sum_table.size].reshape(sum_table.shape),
    )


def solution(mesh):
    tok = P("rows", "seq", None)
    in_specs = (tok, P("rows", None)) + (P(),) * 9 + (tok,)
    out_specs = (tok, tok) + (P(),) * 9
    return jax.shard_map(
        per_device, mesh=mesh, in_specs=in_specs, out_specs=out_specs, check_vma=False
    )
```

```python
import functools
import math

import jax
import jax.numpy as jnp
from jax import lax
from jax.experimental import pallas as pl
from jax.experimental.pallas import tpu as pltpu
from jax.sharding import PartitionSpec as P

EPSILON = 1e-06
THRESHOLDS = (12, 16, 23, 32, 46, 64, 91)
NEGATIVE = -1e30
BUCKETS = 32
GELU_SCALE = math.sqrt(2.0 / math.pi)
GELU_CUBIC = 0.044715
LOG2E = math.log2(math.e)
BLK = 128
QT = 256
HALF = 64
ONES_AT = 8
BF = jnp.bfloat16
F32 = jnp.float32
TOK = 512
TILE_TOK = 256
MESH = pl.DeviceIdType.MESH
CH_ROWS, CH_COLS = 768, 256
SUM_STEPS = ((1,), (2,), (3,), (4,))
GIVE_STEPS = ((5,), (6,), (7,), (8,), (9,))
GIVE_LAG = 4
EARLY = 6
SWAPS = 12
SEQ = 4
SEND_SLOTS = 8
BOTH_STEPS = ((1,), (2,), (3,), (4, 5), (6,), (7,), (8,), (9,))
REST_LAG = 2


def bucket_of(offsets, bucket_count):
    distance = jnp.abs(offsets)
    levels = 8 + sum(((distance >= threshold).astype(jnp.int32) for threshold in THRESHOLDS))
    return jnp.where(offsets > 0, bucket_count // 2, 0) + jnp.where(distance < 8, distance, levels)


def segment_ids(seg_lengths, row_len):
    order = jnp.arange(seg_lengths.shape[1])
    ends = jnp.sum(
        jnp.where(order[None, :, None] <= order[None, None, :], seg_lengths[:, :, None], 0), axis=1
    )
    positions = jnp.arange(row_len, dtype=jnp.int32)
    return jnp.sum((positions[None, :, None] >= ends[:, None, :]).astype(jnp.int32), axis=2)


def gelu_both(x):
    square = x * x
    tangent = jnp.tanh(x * (GELU_SCALE + GELU_SCALE * GELU_CUBIC * square))
    upper = 0.5 * tangent + 0.5
    slope = upper + (0.5 * x) * (1.0 - tangent * tangent) * (
        GELU_SCALE + 3.0 * GELU_SCALE * GELU_CUBIC * square
    )
    return x * upper, slope


def apply_rms_scaling(values_in, gain_row):
    inverse = lax.rsqrt(jnp.mean(values_in * values_in, axis=-1, keepdims=True) + EPSILON)
    return (values_in * inverse * gain_row, inverse)


def norm_back(values_in, inverse, gain_row, grad_normed):
    weighted = grad_normed * gain_row
    inner_mean = jnp.mean(weighted * values_in, axis=-1, keepdims=True)
    grad_values = inverse * weighted - values_in * (inverse * inverse * inverse) * inner_mean
    grad_gain = jnp.sum(grad_normed * values_in * inverse, axis=0)
    return (grad_values, grad_gain)


def dot(a, b, ca, cb):
    return lax.dot_general(a, b, (((ca,), (cb,)), ((), ())), preferred_element_type=F32)


def halves(value, own, other, head):
    lane = lax.broadcasted_iota(jnp.int32, value.shape, 1)
    mine = (lane < HALF) if head == 0 else (lane >= HALF)
    return jnp.where(mine, value, other)


def stack_q(q_pair, features, head):
    scaled = q_pair[head * HALF : (head + 1) * HALF].astype(F32) * LOG2E
    high = scaled.astype(BF)
    low = (scaled - high.astype(F32)).astype(BF)
    zero = jnp.zeros_like(high)
    if head == 0:
        return jnp.concatenate([high, zero, low, features], axis=0)
    return jnp.concatenate([zero, high, features, low], axis=0)


def bias_tile(bias_ref, head, key_block, query_block, number, blocks):
    at = key_block - query_block + blocks - 1
    return jnp.concatenate([bias_ref[head, at - i] for i in range(number)], axis=1)


def attend_kernel(q_ref, k_ref, v_ref, fq_ref, fk_ref, bias_ref, *refs):
    if len(refs) > 2:
        away, mix_ref, stat_ref, near, *sems = refs
        swap = Exchange(away, near, *sems, True)
        now = pl.program_id(0) * pl.num_programs(1) + pl.program_id(1)

        @pl.when(now == 0)
        def _():
            swap.meet()
            swap.start(0)

        @pl.when(now == pl.num_programs(0) * pl.num_programs(1) - 1)
        def _():
            swap.wait(0)
    else:
        mix_ref, stat_ref = refs
    row_len = k_ref.shape[0]
    blocks = row_len // BLK
    keys, vals, features_q, features_k = k_ref[...], v_ref[...], fq_ref[0], fk_ref[0]
    q_pair = q_ref[...].T
    lane = lax.broadcasted_iota(jnp.int32, (row_len, BLK), 1)
    ones = jnp.ones_like(vals)
    queries = [stack_q(q_pair, features_q, h) for h in range(2)]
    keys_all = [jnp.concatenate([keys, halves(keys, None, features_k, h)], axis=1) for h in range(2)]
    values = [halves(vals, None, ones, h) for h in range(2)]
    mixed, stats = [], []
    for h in range(2):
        raw = dot(keys_all[h], queries[h], 1, 0)
        scores = [
            raw[b * BLK : (b + 1) * BLK] + bias_tile(bias_ref, h, b, 0, blocks, blocks)
            for b in range(blocks)
        ]
        top = functools.reduce(jnp.maximum, scores)
        top = jnp.max(top, axis=0, keepdims=True)
        probs = jnp.concatenate([jnp.exp2(s - top).astype(BF) for s in scores], axis=0)
        summed = dot(probs, values[h], 0, 0)
        at = HALF if h == 0 else 0
        total = summed[:, at : at + 1]
        mixed.append(summed * (1.0 / total))
        stats.append(top)
        stats.append(total)
    mix_ref[...] = jnp.where(lane < HALF, mixed[0], mixed[1]).astype(BF)
    totals = jnp.where(lane == 0, stats[1], stats[3]).T
    for h in range(2):
        stat_ref[0, 0, h : h + 1] = stats[2 * h] + jnp.log2(totals[h : h + 1])


def three(row):
    one = row.astype(BF)
    rest = row - one.astype(F32)
    two = rest.astype(BF)
    return one, two, (rest - two.astype(F32)).astype(BF)


def feature_rows(base, row):
    parts = three(row)
    at = lax.broadcasted_iota(jnp.int32, base.shape, 0)
    out = base.astype(F32)
    for i, part in enumerate(parts):
        out = jnp.where(at == ONES_AT + i, part.astype(F32), out)
    return out.astype(BF)


def block_buckets(at, blocks):
    ahead = (at - blocks + 1) * BLK
    low, high = ahead - BLK + 1, ahead + BLK - 1
    if low >= THRESHOLDS[-1] or high <= -THRESHOLDS[-1]:
        return BUCKETS - 1 if low > 0 else BUCKETS // 2 - 1, None, ()
    row = lax.broadcasted_iota(jnp.int32, (BLK, BLK), 0)
    lane = lax.broadcasted_iota(jnp.int32, (BLK, BLK), 1)
    first = BUCKETS // 2 if low > 0 else 0
    last = BUCKETS // 2 if high <= 0 else BUCKETS
    return None, bucket_of(ahead + row - lane, BUCKETS), range(first, last)


def bias_blocks(table_ref, bias_ref):
    heads, number = bias_ref.shape[:2]
    for at in range(number):
        one, bucket, some = block_buckets(at, (number + 1) // 2)

        def head_blocks(h, _):
            if one is not None:
                bias_ref[h, at] = jnp.full((BLK, BLK), table_ref[one, h] * LOG2E, F32)
                return 0
            value = jnp.zeros((BLK, BLK), F32)
            for b in some:
                value = jnp.where(bucket == b, table_ref[b, h] * LOG2E, value)
            bias_ref[h, at] = value
            return 0

        lax.fori_loop(0, heads, head_blocks, 0)


def bucket_sums(acc_ref, head, blocks):
    sums = BUCKETS * [jnp.zeros((1, BLK), F32)]
    for at in range(2 * blocks - 1):
        value = acc_ref[head, at]
        one, bucket, some = block_buckets(at, blocks)
        if one is not None:
            sums[one] = sums[one] + jnp.sum(value, axis=0, keepdims=True)
        for b in some:
            picked = jnp.sum(jnp.where(bucket == b, value, 0.0), axis=0, keepdims=True)
            sums[b] = sums[b] + picked
    return jnp.concatenate(sums, axis=0)


def attend_back_kernel(
    depth, q_ref, k_ref, v_ref, wp_ref, gb_ref, mix_ref, stat_ref, fq_ref, fk_ref, bias_ref, *refs
):
    if depth:
        share, done, dq_ref, dk_ref, dv_ref, table_ref, gi_ref, go_ref, out_ref = refs[:9]
        acc_ref, dk_sum, dv_sum, *sems = refs[9:15]
        swap = Exchange(done, out_ref, *sems, False, SWAPS)
        giving = Summing(
            depth, share, give_refs=refs[15:], targets=(gi_ref, go_ref), turned=True,
            given=(share.shape[0] // 2 - gi_ref.shape[1] // CH_COLS, share.shape[0] // 2),
        )
        now = pl.program_id(0) * pl.num_programs(1) + pl.program_id(1)

        @pl.when(now == 0)
        def _():
            giving.meet()

        @pl.when(now < SWAPS)
        def _():
            swap.start(now)

        giving.tick(now + giving.given[0] + GIVE_LAG, GIVE_STEPS, GIVE_LAG)
    else:
        dq_ref, dk_ref, dv_ref, table_ref, acc_ref, dk_sum, dv_sum = refs
    row_len = k_ref.shape[0]
    blocks = row_len // BLK
    keys, vals, features_k = k_ref[...], v_ref[...], fk_ref[0]
    k_flat = keys.T
    do_pair = dot(wp_ref[...], gb_ref[...], 1, 1).astype(BF)
    q_rows, do_rows = q_ref[...], do_pair.T
    q_pair, mix_pair = q_rows.T, mix_ref[...].T
    zero_rows = jnp.zeros((row_len, BLK), BF)

    @pl.when(pl.program_id(1) == 0)
    def _():
        acc_ref[...] = jnp.zeros_like(acc_ref)

    for head in range(2):
        span = slice(head * HALF, (head + 1) * HALF)
        do_head = do_pair[span]
        delta = jnp.sum(do_head.astype(F32) * mix_pair[span].astype(F32), axis=0, keepdims=True)
        zeros = jnp.zeros((HALF, row_len), BF)
        q_all = stack_q(q_pair, feature_rows(fq_ref[0], -stat_ref[0, 0, head : head + 1]), head)
        k_all = jnp.concatenate([keys, halves(keys, None, features_k, head)], axis=1)
        v_all = halves(vals, None, features_k, head)
        back = feature_rows(zeros, -delta)
        do_all = jnp.concatenate([do_head, back] if head == 0 else [back, do_head], axis=0)
        q_own = halves(q_rows, None, zero_rows, head)
        do_own = halves(do_rows, None, zero_rows, head)
        for tile in range(row_len // QT):
            cut = slice(tile * QT, (tile + 1) * QT)
            raw = dot(k_all, q_all[:, cut], 1, 0)
            grad_probs = dot(v_all, do_all[:, cut], 1, 0)
            probs_list, grads_list = [], []
            sums = {}
            for b in range(blocks):
                part = slice(b * BLK, (b + 1) * BLK)
                probs = jnp.exp2(raw[part] + bias_tile(bias_ref, head, b, tile * (QT // BLK), QT // BLK, blocks))
                grads = probs * grad_probs[part]
                probs_list.append(probs.astype(BF))
                grads_list.append(grads.astype(BF))
                for i in range(QT // BLK):
                    at = b - tile * (QT // BLK) - i + blocks - 1
                    piece = grads[:, i * BLK : (i + 1) * BLK]
                    sums[at] = sums[at] + piece if at in sums else piece
            for at, piece in sums.items():
                acc_ref[head, at] += piece
            probs_low = jnp.concatenate(probs_list, axis=0)
            grads_low = jnp.concatenate(grads_list, axis=0)
            dv_new = dot(probs_low, do_own[cut], 1, 0)
            dk_new = dot(grads_low, q_own[cut], 1, 0)
            if head == 0 and tile == 0:
                dv_sum[...] = dv_new
                dk_sum[...] = dk_new
            else:
                dv_sum[...] += dv_new
                dk_sum[...] += dk_new
            dq_ref[span, cut] = dot(k_flat[span], grads_low, 1, 0).astype(BF)
    dk_ref[...] = dk_sum[...].astype(BF)
    dv_ref[...] = dv_sum[...].astype(BF)

    @pl.when(pl.program_id(1) == pl.num_programs(1) - 1)
    def _():
        for head in range(2):
            table_ref[head] = bucket_sums(acc_ref, head, blocks)

    if depth:
        steps = pl.num_programs(0) * pl.num_programs(1)

        @pl.when(now == steps - 1)
        def _():
            giving.drain(steps + giving.given[0] + GIVE_LAG, GIVE_STEPS, GIVE_LAG)
            giving.finish()
            swap.finish()


def specs(row_len):
    flat = pl.BlockSpec((BLK, row_len), lambda g, r: (g, r))
    rows = pl.BlockSpec((row_len, BLK), lambda g, r: (r, g))
    stat = pl.BlockSpec((1, 1, 2, row_len), lambda g, r: (r, g, 0, 0))
    fq = pl.BlockSpec((1, HALF, row_len), lambda g, r: (r, 0, 0))
    fk = pl.BlockSpec((1, row_len, BLK), lambda g, r: (r, 0, 0))
    blocks = 2 * (row_len // BLK) - 1
    bias = pl.BlockSpec((2, blocks, BLK, BLK), lambda g, r: (g, 0, 0, 0))
    return flat, rows, stat, fq, fk, bias


def attend(q_rows, k_rows, v_rows, fq, fk, bias, row_len, away=None):
    count, width = q_rows.shape
    flat, rows, stat, fqs, fks, biass = specs(row_len)
    pairs, row_count = width // BLK, count // row_len
    anywhere = pl.BlockSpec(memory_space=pl.ANY)
    extra, near, scratch, params = (), [], [], {}
    if away is not None:
        extra, near = (away,), [jax.ShapeDtypeStruct((row_count, row_len, width), BF)]
        scratch, params = Exchange.scratch(), dict(collective_id=5, has_side_effects=True)
    return pl.pallas_call(
        attend_kernel,
        grid=(pairs, row_count),
        in_specs=[rows, rows, rows, fqs, fks, biass] + [anywhere] * len(extra),
        out_specs=[rows, stat] + [anywhere] * len(near),
        out_shape=[
            jax.ShapeDtypeStruct((count, width), BF),
            jax.ShapeDtypeStruct((row_count, pairs, 2, row_len), F32),
        ] + near,
        scratch_shapes=scratch,
        compiler_params=pltpu.CompilerParams(vmem_limit_bytes=48 << 20, **params),
        cost_estimate=pl.CostEstimate(
            flops=4 * 4 * width * count * row_len,
            bytes_accessed=8 * width * count,
            transcendentals=0,
        ),
    )(q_rows, k_rows, v_rows, fq, fk, bias, *extra)


def attend_back(q_rows, k_rows, v_rows, wp, gb, mix, stat_in, fq, fk, bias, row_len, gives):
    count, width = q_rows.shape
    flat, rows, stat, fqs, fks, biass = specs(row_len)
    pairs, row_count = width // BLK, count // row_len
    anywhere = pl.BlockSpec(memory_space=pl.ANY)
    depth, extra, extra_in, extra_out, scratch, params = 0, (), [], [], [], {}
    if gives is not None:
        share, depth, early, done = gives
        shapes = [(width, share.shape[0] // 2 * CH_COLS - early), (share.shape[0] // 2 * CH_COLS - early, width)]
        done = done.reshape(row_count, row_len, width)
        extra, extra_in = (share, done), [pl.BlockSpec(share.shape, lambda g, r: (0, 0, 0)), anywhere]
        extra_out = [jax.ShapeDtypeStruct(shape, BF) for shape in shapes]
        extra_out += [jax.ShapeDtypeStruct((row_count * SEQ, row_len // SEQ, width), BF)]
        scratch = Exchange.scratch(SWAPS) + Summing.give_scratch(share.shape[0], depth, True)
        params = dict(collective_id=3, has_side_effects=True)
    return pl.pallas_call(
        functools.partial(attend_back_kernel, depth),
        grid=(pairs, row_count),
        in_specs=[
            rows, rows, rows, pl.BlockSpec((BLK, width), lambda g, r: (g, 0)),
            pl.BlockSpec((row_len, width), lambda g, r: (r, 0)), rows, stat, fqs, fks, biass,
        ] + extra_in,
        out_specs=[flat, rows, rows, pl.BlockSpec((2, BUCKETS, BLK), lambda g, r: (g, 0, 0))]
        + [anywhere] * len(extra_out),
        out_shape=[
            jax.ShapeDtypeStruct((width, count), BF),
            jax.ShapeDtypeStruct((count, width), BF),
            jax.ShapeDtypeStruct((count, width), BF),
            jax.ShapeDtypeStruct((2 * pairs, BUCKETS, BLK), F32),
        ] + extra_out,
        scratch_shapes=[pltpu.VMEM((2,) + bias.shape[1:], F32)]
        + [pltpu.VMEM((row_len, BLK), F32)] * 2
        + scratch,
        compiler_params=pltpu.CompilerParams(vmem_limit_bytes=48 << 20, **params),
        cost_estimate=pl.CostEstimate(
            flops=10 * 4 * width * count * row_len,
            bytes_accessed=16 * width * count,
            transcendentals=0,
        ),
    )(q_rows, k_rows, v_rows, wp, gb, mix, stat_in, fq, fk, bias, *extra)


class Place:
    def __init__(self):
        self.r, self.s = lax.axis_index("rows"), lax.axis_index("seq")
        self.x, self.z = lax.rem(self.r, 2), self.r // 2
        self.core, self.y = lax.rem(self.s, 2), self.s // 2

    def at(self, x=None, y=None, core=None, z=None):
        x = self.x if x is None else x
        y = self.y if y is None else y
        core = self.core if core is None else core
        z = self.z if z is None else z
        return (z * 2 + x, y * 2 + core)


def spans(base, size, step=16):
    return pl.ds(pl.multiple_of(base, step), size)


class Exchange:
    def __init__(self, src, dst, send, recv, keep, to_rows, parts=1):
        self.src, self.dst, self.send, self.recv, self.keep, self.to_rows = src, dst, send, recv, keep, to_rows
        pieces, rows = (src, dst) if to_rows else (dst, src)
        self.mine, self.piece, self.parts = rows.shape[0], pieces.shape[1], parts
        self.r, self.s = lax.axis_index("rows"), lax.axis_index("seq")

    @staticmethod
    def scratch(parts=1):
        dma = pltpu.SemaphoreType.DMA
        return [dma((parts, SEQ - 1)), dma((parts, SEQ - 1)), dma((parts,))]

    def meet(self):
        barrier = pltpu.get_barrier_semaphore()
        for k in range(1, SEQ):
            place = (self.r, lax.rem(self.s + k, SEQ))
            pl.semaphore_signal(barrier, inc=1, device_id=place, device_id_type=MESH)
        pl.semaphore_wait(barrier, SEQ - 1)

    def ends(self, part, peer):
        if self.parts <= self.mine:
            size, long = self.mine // self.parts, self.piece
            row, at = part * size, 0
        else:
            cuts = self.parts // self.mine
            size, long = 1, self.piece // cuts
            row, at = part // cuts, lax.rem(part, cuts) * long
        if self.to_rows:
            return (self.src.at[pl.ds(peer * self.mine + row, size), spans(at, long)],
                    self.dst.at[pl.ds(row, size), spans(self.s * self.piece + at, long)])
        return (self.src.at[pl.ds(row, size), spans(peer * self.piece + at, long)],
                self.dst.at[pl.ds(self.s * self.mine + row, size), spans(at, long)])

    def copies(self, part):
        out = []
        for k in range(1, SEQ):
            peer = lax.rem(self.s + k, SEQ)
            src, dst = self.ends(part, peer)
            out.append(pltpu.make_async_remote_copy(
                src_ref=src, dst_ref=dst, send_sem=self.send.at[part, k - 1],
                recv_sem=self.recv.at[part, SEQ - 1 - k], device_id=(self.r, peer), device_id_type=MESH))
        src, dst = self.ends(part, self.s)
        return out, pltpu.make_async_copy(src, dst, self.keep.at[part])

    def start(self, part):
        away, here = self.copies(part)
        for d in away:
            d.start()
        here.start()

    def wait(self, part):
        away, here = self.copies(part)
        for d in away:
            d.wait()
        here.wait()

    def finish(self):
        def one(part, _):
            self.wait(part)
            return 0

        lax.fori_loop(0, self.parts, one, 0)


class Summing:
    def __init__(self, depth, share, sum_refs=None, give_refs=None, scale=1.0, targets=None, turned=False, mixed=True, given=None):
        if sum_refs is not None:
            (self.snd, self.got, self.own, self.got_one, self.got_two, self.got_z,
             self.send_sum, self.recv_sum, self.send_sum_z, self.recv_sum_z) = sum_refs
        if give_refs is not None:
            (self.gath, self.flip, self.sems,
             self.send_give, self.recv_give, self.send_give_z, self.recv_give_z) = give_refs
        self.summed = (0, share.shape[0] // 2)
        self.given = self.summed if given is None else given
        self.share, self.chunks, self.targets, self.turned = share, share.shape[0], targets, turned
        self.depth, self.scale, self.mixed = depth, scale, mixed
        self.me = Place()
        self.w = CH_COLS // 2
        self.half, self.quarter = CH_ROWS // 2, CH_ROWS // 4
        self.piece = CH_ROWS // (4 * depth)

    @staticmethod
    def sum_scratch(chunks, depth):
        w, piece = CH_COLS // 2, CH_ROWS // (4 * depth)
        dma = pltpu.SemaphoreType.DMA
        return [
            pltpu.VMEM((SEND_SLOTS, CH_ROWS, w), BF),
            pltpu.VMEM((chunks, CH_ROWS, w), BF),
            pltpu.VMEM((chunks, CH_ROWS, w), BF),
            pltpu.VMEM((chunks, CH_ROWS // 2, w), BF),
            pltpu.VMEM((chunks, CH_ROWS // 4, w), BF),
            pltpu.VMEM((chunks, depth - 1, piece, w), BF),
            dma((3, chunks)), dma((3, chunks)),
            dma((chunks, depth - 1)), dma((chunks, depth - 1)),
        ]

    @staticmethod
    def give_scratch(chunks, depth, turned):
        dma = pltpu.SemaphoreType.DMA
        return [
            pltpu.VMEM((chunks, 2, CH_ROWS, CH_COLS // 2), BF),
            pltpu.VMEM((2, CH_COLS, CH_ROWS) if turned else (1, 16, 128), BF),
            dma((2, chunks)),
            dma((3, chunks)), dma((3, chunks)),
            dma((chunks, depth - 1)), dma((chunks, depth - 1)),
        ]

    @staticmethod
    def share_shape(chunks, depth):
        return (chunks, CH_ROWS // (4 * depth), CH_COLS // 2)

    def meet(self):
        me = self.me
        barrier = pltpu.get_barrier_semaphore()
        others = [me.at(x=1 - me.x)] + [(me.r, lax.rem(me.s + k, SEQ)) for k in range(1, SEQ)]
        others += [me.at(z=lax.rem(me.z + k, self.depth)) for k in range(1, self.depth)]
        for place in others:
            pl.semaphore_signal(barrier, inc=1, device_id=place, device_id_type=MESH)
        pl.semaphore_wait(barrier, len(others))

    def copy(self, src, dst, stage, c, place):
        if stage < 3:
            send, recv = self.send_sum.at[stage, c], self.recv_sum.at[stage, c]
        else:
            send, recv = self.send_give.at[stage - 3, c], self.recv_give.at[stage - 3, c]
        return pltpu.make_async_remote_copy(
            src_ref=src, dst_ref=dst, send_sem=send, recv_sem=recv, device_id=place, device_id_type=MESH)

    def part(self, c, start, size):
        return self.gath.at[c, self.me.core, spans(start, size)]

    def order(self, c):
        me, odd = self.me, lax.rem(c, 2) if self.mixed else 0
        one = me.x + odd * (me.y - me.x)
        two = me.y + odd * (me.x - me.y)
        x_there, y_there = 1 - 2 * me.x, 2 - 4 * me.y
        first = (me.r + (1 - odd) * x_there, me.s + odd * y_there)
        second = (me.r + odd * x_there, me.s + (1 - odd) * y_there)
        return one, two, first, second

    def put(self, c, value):
        left, right = value[:, : self.w].astype(BF), value[:, self.w :].astype(BF)
        first = self.me.core == 0
        self.own[c] = jnp.where(first, left, right)
        self.snd[lax.rem(c, SEND_SLOTS)] = jnp.where(first, right, left)
        self.step_core(c).start()

    def step_core(self, c):
        return self.copy(self.snd.at[lax.rem(c, SEND_SLOTS)], self.got.at[c], 0, c, self.me.at(core=1 - self.me.core))

    def step_one(self, c):
        one, _, place, _ = self.order(c)
        return self.copy(self.own.at[c, spans((1 - one) * self.half, self.half)], self.got_one.at[c], 1, c, place)

    def step_two(self, c):
        one, two, _, place = self.order(c)
        part = spans(one * self.half + (1 - two) * self.quarter, self.quarter)
        return self.copy(self.own.at[c, part], self.got_two.at[c], 2, c, place)

    def base(self, c):
        one, two, _, _ = self.order(c)
        return one * self.half + two * self.quarter

    def step_z(self, c, k):
        to = lax.rem(self.me.z + k, self.depth)
        return pltpu.make_async_remote_copy(
            src_ref=self.own.at[c, spans(self.base(c) + to * self.piece, self.piece)],
            dst_ref=self.got_z.at[c, self.depth - 1 - k],
            send_sem=self.send_sum_z.at[c, k - 1], recv_sem=self.recv_sum_z.at[c, self.depth - 1 - k],
            device_id=self.me.at(z=to), device_id_type=MESH)

    def mine(self, c):
        return self.part(c, self.base(c) + self.me.z * self.piece, self.piece)

    def give_z(self, c, k):
        return pltpu.make_async_remote_copy(
            src_ref=self.mine(c), dst_ref=self.mine(c),
            send_sem=self.send_give_z.at[c, k - 1], recv_sem=self.recv_give_z.at[c, self.depth - 1 - k],
            device_id=self.me.at(z=lax.rem(self.me.z + k, self.depth)), device_id_type=MESH)

    def give_two(self, c):
        part = self.part(c, self.base(c), self.quarter)
        return self.copy(part, part, 3, c, self.order(c)[3])

    def give_one(self, c):
        one, _, place, _ = self.order(c)
        part = self.part(c, one * self.half, self.half)
        return self.copy(part, part, 4, c, place)

    def give_core(self, c):
        part = self.part(c, 0, CH_ROWS)
        return self.copy(part, part, 5, c, self.me.at(core=1 - self.me.core))

    def leave(self, c, kind):
        if len(self.targets) == 1:
            array, at = self.targets[0], c * CH_COLS
        else:
            array, at = self.targets[kind], (c // 2 - self.given[0]) * CH_COLS
        if self.turned and kind == 1:
            flip = self.flip.at[lax.rem(c // 2, 2)]
            return [pltpu.make_async_copy(flip, array.at[spans(at, CH_COLS, CH_COLS)], self.sems.at[0, c])]
        return [
            pltpu.make_async_copy(
                self.gath.at[c, i], array.at[:, spans(at + i * self.w, self.w, 128)], self.sems.at[i, c])
            for i in range(2)
        ]

    def add(self, c, start, size, from_ref):
        part = spans(start, size)
        self.own[c, part] = (self.own[c, part].astype(F32) + from_ref[c].astype(F32)).astype(BF)

    def run(self, stage, c, kind):
        depth = self.depth
        if stage == 1:
            self.step_core(c).wait()
            self.add(c, 0, CH_ROWS, self.got)
            self.step_one(c).start()
        if stage == 2:
            self.step_one(c).wait_recv()
            self.add(c, self.order(c)[0] * self.half, self.half, self.got_one)
            self.step_two(c).start()
        if stage == 3:
            self.step_two(c).wait_recv()
            self.add(c, self.base(c), self.quarter, self.got_two)
            for k in range(1, depth):
                self.step_z(c, k).start()
        if stage == 4:
            for k in range(1, depth):
                self.step_z(c, k).wait_recv()
            total = self.own[c, spans(self.base(c) + self.me.z * self.piece, self.piece)].astype(F32)
            for k in range(depth - 1):
                total = total + self.got_z[c, k].astype(F32)
            self.share[c] = (total * self.scale).astype(BF)
            for d in (self.step_one(c), self.step_two(c)):
                d.wait_send()
            for k in range(1, depth):
                self.step_z(c, k).wait_send()
        if stage == 5:
            self.gath[c, self.me.core, spans(self.base(c) + self.me.z * self.piece, self.piece)] = self.share[c]
            for k in range(1, depth):
                self.give_z(c, k).start()
        if stage == 6:
            for k in range(1, depth):
                self.give_z(c, k).wait_recv()
            self.give_two(c).start()
        if stage == 7:
            self.give_two(c).wait_recv()
            self.give_one(c).start()
        if stage == 8:
            self.give_one(c).wait_recv()
            self.give_core(c).start()
        if stage == 9:
            self.give_core(c).wait_recv()
            if self.turned and kind == 1:

                @pl.when(c // 2 >= self.given[0] + 2)
                def _():
                    for d in self.leave(c - 4, kind):
                        d.wait()

                slot = lax.rem(c // 2, 2)
                for i in range(2):
                    self.flip[slot, i * self.w : (i + 1) * self.w] = self.gath[c, i].T
            for d in self.leave(c, kind):
                d.start()
            for d in (self.give_two, self.give_one, self.give_core):
                d(c).wait_send()
            for k in range(1, depth):
                self.give_z(c, k).wait_send()

    def tick(self, t, steps, lag):
        for at in range(len(steps), 0, -1):
            p = t - at * lag
            for stage in steps[at - 1]:
                low, high = self.summed if stage < 5 else self.given

                @pl.when((p >= low) & (p < high))
                def _():
                    for kind in range(2):
                        self.run(stage, 2 * p + kind, kind)

    def drain(self, start, steps, lag):
        def one(t, _):
            self.tick(t, steps, lag)
            return 0

        last = 0
        for at in range(len(steps), 0, -1):
            for stage in steps[at - 1]:
                last = max(last, (self.summed if stage < 5 else self.given)[1] + at * lag)
        lax.fori_loop(start, last, one, 0)

    def finish(self):
        def one(c, kind):
            for d in self.leave(c, kind):
                d.wait()

        def pair(p, _):
            one(2 * p, 0)
            if not self.turned:
                one(2 * p + 1, 1)
            return 0

        low, high = self.given
        lax.fori_loop(low, high, pair, 0)
        if self.turned:
            for p in range(max(low, high - 2), high):
                one(2 * p + 1, 1)


def before_kernel(
    fused, tok, gain, wq, wk, wv, table, normed_ref, flat_ref, q_ref, k_ref, v_ref, bias_ref, *refs
):
    if fused:
        tok_ref, rows, *sems = refs
        swap = Exchange(tok, rows, *sems, True, rows.shape[0])
        m = pl.program_id(0)

        @pl.when(m == 0)
        def _():
            swap.meet()
            for part in range(rows.shape[0]):
                swap.start(part)

    @pl.when(pl.program_id(0) == 0)
    def _():
        bias_blocks(table, bias_ref)

    if fused:
        swap.wait(m)
        own = rows[m]
        tok_ref[...] = own
        wide = own.astype(F32)
    else:
        wide = tok[...].astype(F32)
    normed = apply_rms_scaling(wide, gain[...])[0].astype(BF)
    normed_ref[...] = normed
    flat_ref[...] = normed.T
    q_ref[...] = dot(normed, wq[...], 1, 0).astype(BF)
    k_ref[...] = dot(normed, wk[...], 1, 0).astype(BF)
    v_ref[...] = dot(normed, wv[...], 1, 0).astype(BF)


def tall(width):
    return pl.BlockSpec((TOK, width), lambda m: (m, 0))


def broad(width):
    return pl.BlockSpec((width, TOK), lambda m: (0, m))


def whole(array):
    return pl.BlockSpec(array.shape, lambda m: (0,) * array.ndim)


def plain_call(kernel, count, ins, in_specs, outs, out_specs, flops, scratch=(), collective_id=None):
    params = {} if collective_id is None else dict(collective_id=collective_id, has_side_effects=True)
    return pl.pallas_call(
        kernel,
        grid=(count // TOK,),
        in_specs=in_specs,
        out_specs=out_specs,
        out_shape=[jax.ShapeDtypeStruct(shape, kind) for shape, kind in outs],
        scratch_shapes=list(scratch),
        compiler_params=pltpu.CompilerParams(vmem_limit_bytes=48 << 20, **params),
        cost_estimate=pl.CostEstimate(flops=flops, bytes_accessed=16 << 20, transcendentals=0),
    )(*ins)


def before(tok, gain, wq, wk, wv, table, mine, fused):
    width = tok.shape[-1]
    count = tok.size // width
    t, f = tall(width), broad(width)
    spec, more, scratch = t, [], []
    bias = (table.shape[1], 2 * (count // mine // BLK) - 1, BLK, BLK)
    if fused:
        spec = pl.BlockSpec(memory_space=pl.ANY)
        more = [((count, width), BF)]
        scratch = [pltpu.VMEM((mine, count // mine, width), BF)] + Exchange.scratch(mine)
    return plain_call(
        functools.partial(before_kernel, fused), count, (tok, gain, wq, wk, wv, table),
        [spec] + [whole(a) for a in (gain, wq, wk, wv)] + [pl.BlockSpec(memory_space=pltpu.SMEM)],
        [((count, width), BF), ((width, count), BF)] + [((count, width), BF)] * 3
        + [(bias, F32)] + more,
        [t, f, t, t, t] + [pl.BlockSpec(bias, lambda m: (0, 0, 0, 0))] + [t] * len(more), 6 * count * width * width, scratch, 4 if fused else None,
    )


def between_kernel(tok, mix, wo, gain, dy, hidden_ref, nt_ref, nt_flat_ref, dy_flat_ref, mix_flat_ref):
    hidden = tok[...].astype(F32) + dot(mix[...], wo[...], 1, 0)
    hidden_ref[...] = hidden
    normed = apply_rms_scaling(hidden, gain[...])[0].astype(BF)
    nt_ref[...] = normed
    nt_flat_ref[...] = normed.T
    dy_flat_ref[...] = dy[...].T
    mix_flat_ref[...] = mix[...].T


def between(tok, mix, wo, gain, dy):
    count, width = tok.shape
    t, f = tall(width), broad(width)
    return plain_call(
        between_kernel, count, (tok, mix, wo, gain, dy), [t, t, whole(wo), whole(gain), t],
        [((count, width), F32), ((count, width), BF)] + [((width, count), BF)] * 3,
        [t, t, f, f, f], 2 * count * width * width,
    )


def after_kernel(tok, gain, gh, dq, dk, dv, wq, wk, wv, grad_ref, gain_ref):
    wide = tok[...].astype(F32)
    _, inverse = apply_rms_scaling(wide, gain[...])
    grad_normed = (
        dot(dq[...].T, wq[...], 1, 1) + dot(dk[...], wk[...], 1, 1) + dot(dv[...], wv[...], 1, 1)
    )
    part, grad_gain = norm_back(wide, inverse, gain[...], grad_normed)
    grad_ref[...] = (gh[...] + part).astype(BF)

    @pl.when(pl.program_id(0) == 0)
    def _():
        gain_ref[...] = jnp.zeros_like(gain_ref)

    gain_ref[...] += grad_gain[None]


def after(tok, gain, gh, dq, dk, dv, wq, wk, wv):
    count, width = tok.shape
    t, f = tall(width), broad(width)
    return plain_call(
        after_kernel, count, (tok, gain, gh, dq, dk, dv, wq, wk, wv),
        [t, whole(gain), t, f, t, t, whole(wq), whole(wk), whole(wv)],
        [((count, width), BF), ((1, width), F32)], [t, whole(gain)], 6 * count * width * width,
    )


def ffn_kernel(depth, scale, nt, nt_flat, dy, dy_flat, gain, wi_hbm, wo_hbm, hidden_hbm,
               res_hbm, gh_hbm, gb_hbm, gain_ref, share, gi_ref, go_ref,
               out_acc, gnt_acc, wi_buf, wo_buf, act, gp, hid, res_buf, gb_buf, w_sem, h_sem, *refs):
    count, width = nt.shape
    tile = 2 * CH_COLS
    tiles = wi_hbm.shape[1] // tile
    parts = count // TOK
    given = gi_ref.shape[1] // CH_COLS
    summing = Summing(
        depth, share, refs[:10], refs[10:], scale, targets=(gi_ref, go_ref), turned=True, given=(0, given)
    )

    def weights(j):
        cut, slot = spans(j * tile, tile, tile), lax.rem(j, 2)
        return (
            pltpu.make_async_copy(wi_hbm.at[:, cut], wi_buf.at[slot], w_sem.at[0, slot]),
            pltpu.make_async_copy(wo_hbm.at[cut], wo_buf.at[slot], w_sem.at[1, slot]),
        )

    def hidden(m):
        return pltpu.make_async_copy(hidden_hbm.at[pl.ds(m * TOK, TOK)], hid, h_sem.at[0])

    for w in weights(0):
        w.start()
    hidden(0).start()
    out_acc[...] = jnp.zeros_like(out_acc)
    gnt_acc[...] = jnp.zeros_like(gnt_acc)
    summing.meet()

    def step(j, _):
        for w in weights(j):
            w.wait()

        @pl.when(j + 1 < tiles)
        def _():
            for w in weights(j + 1):
                w.start()

        slot = lax.rem(j, 2)
        wi, wo = wi_buf.at[slot], wo_buf.at[slot]
        for m in range(count // TILE_TOK):
            part = slice(m * TILE_TOK, (m + 1) * TILE_TOK)
            pre = dot(nt[part], wi[...], 1, 0)
            grad_active = dot(dy[part], wo[...], 1, 1)
            value, slope = gelu_both(pre)
            act[part] = value.astype(BF)
            gp[part] = (grad_active * slope).astype(BF)
        for h in range(2):
            cut = slice(h * CH_COLS, (h + 1) * CH_COLS)
            summing.put(4 * j + 2 * h, dot(nt_flat[...], gp[:, cut], 1, 0))
            summing.put(4 * j + 2 * h + 1, dot(dy_flat[...], act[:, cut], 1, 0))
            if h == 0:
                summing.tick(2 * j, BOTH_STEPS, 1)
        for m in range(count // TILE_TOK):
            part = slice(m * TILE_TOK, (m + 1) * TILE_TOK)
            out_acc[part] += dot(act[part], wo[...], 1, 0)
            gnt_acc[part] += dot(gp[part], wi[...], 1, 1)
        summing.tick(2 * j + 1, BOTH_STEPS, 1)
        return 0

    lax.fori_loop(0, tiles, step, 0)

    def outputs(m):
        rows = pl.ds(m * TOK, TOK)
        return (
            pltpu.make_async_copy(res_buf.at[m % 2], res_hbm.at[rows], h_sem.at[1 + m % 2]),
            pltpu.make_async_copy(gb_buf.at[m % 2], gb_hbm.at[rows], h_sem.at[3 + m % 2]),
            pltpu.make_async_copy(gnt_acc.at[rows], gh_hbm.at[rows], h_sem.at[5 + m % 2]),
        )

    total_gain = jnp.zeros((1, width), F32)
    gain_row = gain[...]
    for m in range(parts):
        summing.tick(2 * tiles + m, BOTH_STEPS, 1)
        rows = slice(m * TOK, (m + 1) * TOK)
        hidden(m).wait()
        if m >= 2:
            for d in outputs(m - 2):
                d.wait()
        value = hid[...]
        res_buf[m % 2] = (value + out_acc[rows]).astype(BF)
        _, inverse = apply_rms_scaling(value, gain_row)
        part, grad_gain = norm_back(value, inverse, gain_row, gnt_acc[rows])
        total_gain = total_gain + grad_gain[None]
        grad_hidden = dy[rows].astype(F32) + part
        gnt_acc[rows] = grad_hidden
        gb_buf[m % 2] = grad_hidden.astype(BF)
        if m + 1 < parts:
            hidden(m + 1).start()
        for d in outputs(m):
            d.start()
    gain_ref[...] = total_gain
    summing.drain(2 * tiles + parts, BOTH_STEPS, 1)
    summing.finish()
    for m in range(max(0, parts - 2), parts):
        for d in outputs(m):
            d.wait()


def ffn_summed(nt, nt_flat, dy, dy_flat, gain, w_inner, w_outer, hidden, scale, depth):
    count, width = nt.shape
    ff = w_inner.shape[1]
    chunks = 2 * ff // CH_COLS
    tile = 2 * CH_COLS
    vm = pl.BlockSpec(memory_space=pltpu.VMEM)
    anywhere = pl.BlockSpec(memory_space=pl.ANY)
    return pl.pallas_call(
        functools.partial(ffn_kernel, depth, scale),
        in_specs=[vm] * 5 + [anywhere] * 3,
        out_specs=[anywhere] * 3 + [vm] * 2 + [anywhere] * 2,
        out_shape=[
            jax.ShapeDtypeStruct((count, width), BF),
            jax.ShapeDtypeStruct((count, width), F32),
            jax.ShapeDtypeStruct((count, width), BF),
            jax.ShapeDtypeStruct((1, width), F32),
            jax.ShapeDtypeStruct(Summing.share_shape(chunks, depth), BF),
            jax.ShapeDtypeStruct((width, EARLY * CH_COLS), BF),
            jax.ShapeDtypeStruct((EARLY * CH_COLS, width), BF),
        ],
        scratch_shapes=[
            pltpu.VMEM((count, width), F32),
            pltpu.VMEM((count, width), F32),
            pltpu.VMEM((2, width, tile), BF),
            pltpu.VMEM((2, tile, width), BF),
            pltpu.VMEM((count, tile), BF),
            pltpu.VMEM((count, tile), BF),
            pltpu.VMEM((TOK, width), F32),
            pltpu.VMEM((2, TOK, width), BF),
            pltpu.VMEM((2, TOK, width), BF),
            pltpu.SemaphoreType.DMA((2, 2)),
            pltpu.SemaphoreType.DMA((7,)),
        ] + Summing.sum_scratch(chunks, depth) + Summing.give_scratch(2 * EARLY, depth, True),
        compiler_params=pltpu.CompilerParams(
            collective_id=1, has_side_effects=True, vmem_limit_bytes=62 << 20),
        cost_estimate=pl.CostEstimate(
            flops=12 * count * width * ff, bytes_accessed=40 << 20, transcendentals=0),
    )(nt, nt_flat, dy, dy_flat, gain, w_inner, w_outer, hidden)


def rest_kernel(depth, scale, *refs):
    sources, (small, gain, out, out_ref) = refs[:11], refs[11:15]
    mix, gb, normed_flat, dq, dk, dv, tok, gh, wq, wk, wv = held = refs[15:26]
    done, gain_sum, load_sem, share, *refs = refs[26:]
    width = normed_flat.shape[0]
    each = width // CH_COLS
    chunks = share.shape[0]
    loads = [pltpu.make_async_copy(a, b, load_sem.at[i]) for i, (a, b) in enumerate(zip(sources, held))]
    gain_sum[...] = jnp.zeros_like(gain_sum)
    for d in loads:
        d.start()
    swap = Exchange(done, out_ref, *refs[:3], False, SWAPS)
    summing = Summing(depth, share, refs[3:13], refs[13:], scale, targets=(out,), mixed=False)
    summing.meet()

    def terms(which, cut):
        if which == 0:
            return dot(mix[...], gb[:, cut], 1, 0)
        if which == 1:
            return dot(normed_flat[...], dq[cut], 1, 1)
        return dot(normed_flat[...], (dk if which == 2 else dv)[:, cut], 1, 0)

    def tokens_back(m):
        rows = spans(m * TOK, TOK, TOK)
        wide = tok[rows].astype(F32)
        _, inverse = apply_rms_scaling(wide, gain[...])
        grad_normed = (
            dot(dq[:, rows].T, wq[...], 1, 1) + dot(dk[rows], wk[...], 1, 1) + dot(dv[rows], wv[...], 1, 1)
        )
        part, grad_gain = norm_back(wide, inverse, gain[...], grad_normed)
        done[m] = (gh[rows] + part).astype(BF)
        gain_sum[...] += grad_gain[None]
        each_row = SWAPS // done.shape[0]
        for i in range(each_row):
            swap.start(m * each_row + i)

    def step(p, _):
        @pl.when(p == 0)
        def _():
            for d in loads[:2]:
                d.wait()

        @pl.when(p == 1)
        def _():
            for d in loads[2:]:
                d.wait()

        for kind in range(2):
            c = 2 * p + kind
            for which in range(4):

                @pl.when(c // each == which)
                def _():
                    cut = spans((c - which * each) * CH_COLS, CH_COLS, CH_COLS)
                    summing.put(c, terms(which, cut))

            @pl.when(c >= 4 * each)
            def _():
                value = small[:, spans((c - 4 * each) * CH_COLS, CH_COLS, CH_COLS)]
                lines = width // BLK
                first = [gain_sum[:, i * BLK : (i + 1) * BLK] for i in range(lines)]
                first.append(jnp.zeros((CH_ROWS - lines, BLK), F32))
                first = jnp.concatenate([jnp.concatenate(first, axis=0), jnp.zeros((CH_ROWS, BLK), F32)], axis=1)
                summing.put(c, value.astype(F32) + jnp.where(c == 4 * each, first, 0.0))

        summing.tick(p, BOTH_STEPS, REST_LAG)

        @pl.when((p >= 1) & (p <= done.shape[0]))
        def _():
            tokens_back(p - 1)

        return 0

    lax.fori_loop(0, chunks // 2, step, 0)
    summing.drain(chunks // 2, BOTH_STEPS, REST_LAG)
    summing.finish()
    swap.finish()


def rest_summed(normed_flat, dq, dk, dv, mix, gb, tok, gh, wq, wk, wv, gain, small, mine, scale, depth):
    width, count = normed_flat.shape
    chunks = (4 * width + small.shape[1]) // CH_COLS
    vm = pl.BlockSpec(memory_space=pltpu.VMEM)
    anywhere = pl.BlockSpec(memory_space=pl.ANY)
    row_len = count // mine
    sources = (mix, gb, normed_flat, dq, dk, dv, tok, gh, wq, wk, wv)
    return pl.pallas_call(
        functools.partial(rest_kernel, depth, scale),
        in_specs=[anywhere] * len(sources) + [vm, vm],
        out_specs=[anywhere] * 2,
        out_shape=[
            jax.ShapeDtypeStruct((CH_ROWS, chunks * CH_COLS), BF),
            jax.ShapeDtypeStruct((mine * SEQ, row_len // SEQ, width), BF),
        ],
        scratch_shapes=[pltpu.VMEM(a.shape, a.dtype) for a in sources]
        + [pltpu.VMEM((mine, row_len, width), BF), pltpu.VMEM((1, width), F32)]
        + [pltpu.SemaphoreType.DMA((len(sources),)), pltpu.VMEM(Summing.share_shape(chunks, depth), BF)]
        + Exchange.scratch(SWAPS)
        + Summing.sum_scratch(chunks, depth)
        + Summing.give_scratch(chunks, depth, False),
        compiler_params=pltpu.CompilerParams(
            collective_id=2, has_side_effects=True, vmem_limit_bytes=60 << 20),
    )(*sources, small, gain)


def reduce_plain(flat, scale):
    share = lax.psum_scatter(flat, ("rows", "seq"), scatter_dimension=0, tiled=True)
    share = (share.astype(F32) * scale).astype(BF)
    return lax.all_gather(share, ("rows", "seq"), axis=0, tiled=True)


def prepare(seg_lengths, mine, row_len):
    seg_count = seg_lengths.shape[1]
    lengths = lax.dynamic_slice_in_dim(seg_lengths, lax.axis_index("seq") * mine, mine, 0)
    seg = segment_ids(lengths, row_len)
    slots = jnp.arange(HALF, dtype=jnp.int32)
    fq = (seg[:, None, :] == slots[None, :, None]).astype(BF)
    fk_half = jnp.where(
        slots < seg_count,
        jnp.where(seg[:, :, None] != slots, NEGATIVE, 0.0),
        jnp.where((slots >= ONES_AT) & (slots < ONES_AT + 3), 1.0, 0.0),
    ).astype(BF)
    fk = jnp.concatenate([fk_half, fk_half], axis=2)
    return fq, fk


def per_device(
    tokens, seg_lengths, w_query, w_key, w_value, w_output, w_inner, w_outer,
    gain_attn, gain_ffn, bucket_bias_table, cotangent,
):
    rows_dev, piece_len, width = tokens.shape
    seq_parts = lax.axis_size("seq")
    row_len = piece_len * seq_parts
    mine = rows_dev // seq_parts
    count = mine * row_len
    gain_one = gain_attn.astype(F32)[None]
    gain_two = gain_ffn.astype(F32)[None]
    depth = lax.axis_size("rows") // 2
    scale = float(rows_dev * lax.axis_size("rows") * row_len) ** (-0.5)
    fused = seq_parts == 4 and CH_ROWS % (4 * depth * 16) == 0 and width == CH_ROWS

    def to_rows(array_in):
        out = lax.all_to_all(array_in, "seq", split_axis=0, concat_axis=1, tiled=True)
        return lax.optimization_barrier(out.reshape(count, width))

    def from_rows(array_in):
        return lax.all_to_all(
            array_in.reshape(mine, row_len, width), "seq", split_axis=1, concat_axis=0, tiled=True
        )

    fq, fk = prepare(seg_lengths, mine, row_len)
    tok = tokens if fused else to_rows(tokens)
    normed, normed_flat, q_rows, k_rows, v_rows, bias, *rows = before(
        tok, gain_one, w_query, w_key, w_value, bucket_bias_table.astype(F32), mine, fused
    )
    if fused:
        tok = rows[0]
    mix, stat, *near = attend(
        q_rows, k_rows, v_rows, fq, fk, bias, row_len, cotangent if fused else None
    )
    dy = near[0].reshape(count, width) if fused else to_rows(cotangent)
    hidden, nt, nt_flat, dy_flat, mix_flat = between(tok, mix, w_output, gain_two, dy)
    if fused:
        result, grad_hidden, branch, sum_two, share, *early = ffn_summed(
            nt, nt_flat, dy, dy_flat, gain_two, w_inner, w_outer, hidden, scale, depth
        )
        gives = (share, depth, early[0].shape[1], result)
    else:
        value, slope = gelu_both(dot(nt, w_inner, 1, 0))
        active = value.astype(BF)
        grad_pre = (dot(dy, w_outer, 1, 1) * slope).astype(BF)
        result = (hidden + dot(active, w_outer, 1, 0)).astype(BF)
        sum_outer, sum_inner = dot(active, dy, 0, 0), dot(grad_pre, nt, 0, 0)
        _, inverse = apply_rms_scaling(hidden, gain_two)
        part, sum_two = norm_back(hidden, inverse, gain_two, dot(grad_pre, w_inner, 1, 1))
        grad_hidden = dy.astype(F32) + part
        branch = grad_hidden.astype(BF)
        gives = None
    dq_flat, dk_rows, dv_rows, table, *given = attend_back(
        q_rows, k_rows, v_rows, w_output, branch, mix, stat, fq, fk, bias, row_len, gives
    )
    if fused:
        sum_one = jnp.zeros((1, width), F32)
    else:
        grad_input, sum_one = after(
            tok, gain_one, grad_hidden, dq_flat, dk_rows, dv_rows, w_query, w_key, w_value
        )
    sum_table = jnp.sum(table, axis=2).T
    small = jnp.concatenate([sum_one.reshape(-1), sum_two.reshape(-1), sum_table.reshape(-1)])
    if fused:
        small = jnp.pad(small, (0, -small.size % (CH_ROWS * BLK))).reshape(CH_ROWS, BLK)
        small = jnp.pad(small.astype(BF), ((0, 0), (0, 2 * CH_COLS - BLK)))
        total, grad_back = rest_summed(
            normed_flat, dq_flat, dk_rows, dv_rows, mix_flat, branch, tok, grad_hidden,
            w_query, w_key, w_value, gain_one, small, mine, scale, depth,
        )
        out_back = given[2]
        grad_inner = jnp.concatenate([early[0], given[0]], axis=1).astype(F32)
        grad_outer = jnp.concatenate([early[1], given[1]], axis=0).astype(F32)
        squares = [total[:, i * width : (i + 1) * width].astype(F32) for i in range(4)]
        rest = total[:, 4 * width : 4 * width + BLK].astype(F32).reshape(-1)
    else:
        devices = lax.axis_size("rows") * seq_parts
        small = jnp.pad(small, (0, -small.size % (16 * devices * width))).reshape(-1, width)
        parts = (
            dot(mix_flat, branch, 1, 0), dot(normed, dq_flat, 0, 1), dot(normed, dk_rows, 0, 0),
            dot(normed, dv_rows, 0, 0), small, sum_outer, sum_inner,
        )
        total = reduce_plain(jnp.concatenate([g.astype(BF) for g in parts]), scale).astype(F32)
        outs, at = [], 0
        for g in parts:
            outs.append(total[at : at + g.shape[0]])
            at += g.shape[0]
        squares, grad_outer, grad_inner = outs[:4], outs[5], outs[6].T
        rest = outs[4].reshape(-1)
        out_back, grad_back = from_rows(result), from_rows(grad_input)
    return (
        out_back,
        grad_back,
        squares[1],
        squares[2],
        squares[3],
        squares[0],
        grad_inner,
        grad_outer,
        rest[:width],
        rest[width : 2 * width],
        rest[2 * width : 2 * width + sum_table.size].reshape(sum_table.shape),
    )


def solution(mesh):
    tok = P("rows", "seq", None)
    in_specs = (tok, P("rows", None)) + (P(),) * 9 + (tok,)
    out_specs = (tok, tok) + (P(),) * 9
    return jax.shard_map(
        per_device, mesh=mesh, in_specs=in_specs, out_specs=out_specs, check_vma=False
    )
```
